512 devices in a mesh: ray: 16 (over z_lo, x), mp: 32 (over y, z_hi, core).
Axes of the slice: x: 4, y: 8, z: 8 (z_hi: 2, z_lo: 4; z = z_hi * 4 + z_lo), core: 2. Of those that a mesh axis runs over, the one named last changes fastest.
Arguments:
- slowness: float32 [128, 128, 128], P('mp', 'ray'), may hold values from 0.5 to 1.5
- accumulated: float32 [128, 128, 128], P('mp', 'ray'), may hold values from -3 to 3
- extrapolated: float32 [128, 128, 128], P('mp', 'ray'), may hold values from -3 to 3
- tv_dual: float32 [3, 128, 128, 128], P(None, 'mp', 'ray'), may hold values from -1.2 to 1.2
- ray_dual: float32 [256, 128], P('ray'), may hold values from -3 to 3
- traveltimes: float32 [256, 128], P('ray'), may hold values from -6 to 6
- tiles: bfloat16 [256, 256, 128, 128], P('ray', 'mp'), may hold values from -0.03125 to 0.03125
- pattern: int32 [256, 256], P('ray', 'mp'), may hold values from 0 to 511, as said below
- selected: int32 [2, 256], P(None, 'ray'), may hold values from 0 to 1, as said below
Outputs:
- slowness_out: float32 [128, 128, 128], P('mp', 'ray')
- ray_dual_out: float32 [256, 128], P('ray')
- tv_dual_out: float32 [3, 128, 128, 128], P(None, 'mp', 'ray')
- accumulated_out: float32 [128, 128, 128], P('mp', 'ray')
- extrapolated_out: float32 [128, 128, 128], P('mp', 'ray')
The draws below stay inside these ranges and needn't reach their ends.
Inputs may be any that keep to these rules, and one draw needn't show every extreme that they name: In each iteration every aligned block of 16 ray blocks (those of one index of ray) has 1 to 8 selected ray blocks, and some block has exactly 8. Among the 128 tiles of one index of ray's ray blocks on one index of mp, at most 16 have model blocks whose grid rows lie on one index of ray (pattern % 128 // 8), and one index of ray has exactly 16.
All inputs are finite; a program needn't handle non-finite values.
Results may differ from the reference program's by a relative error of at most 0.0022.
Values may be sent and summed in bfloat16 or wider, within the bound.
No kernel may reach another device: no remote copies, remote signals or barrier semaphores. Data moves between devices by JAX's collectives and lax.ppermute only.
A program may use at most 64 MiB of HBM per device.

```python
import jax
import jax.numpy as jnp
from jax import lax

TILE = 128
GX = 4
GY = 8
RB_DEV = 16
CAP = 8
ITERS = 2
MAXSEL = 8
ROUTE = 16
NX = 128
NY = 128
NZ = 128
RB = 256
SLOTS = 256
N_RAY = 16
N_MP = 32


def draw_selected(key, part):
    key = jax.random.fold_in(key, 5)
    first, second, third = jax.random.split(key, 3)
    counts = jax.random.randint(first, (ITERS, N_RAY), 1, MAXSEL + 1)
    fullest = jax.random.randint(second, (ITERS,), 0, N_RAY)
    counts = jnp.where(jnp.arange(N_RAY)[None, :] == fullest[:, None], MAXSEL, counts)
    keys = jax.random.split(third, ITERS * N_RAY)
    orders = jax.vmap(lambda single: jax.random.permutation(single, RB_DEV))(keys)
    orders = orders.reshape(ITERS, N_RAY, RB_DEV)
    chosen = (orders < counts[:, :, None]).astype(jnp.int32)
    return chosen.reshape(ITERS, N_RAY * RB_DEV)


def owners_of_group(single):
    keys = jax.random.split(single, 5)
    count = RB_DEV * CAP
    pool = jnp.tile(jnp.arange(N_RAY, dtype=jnp.int32), ROUTE)
    favored = jax.random.randint(keys[0], (), 0, N_RAY)
    scores = jax.random.permutation(keys[1], N_RAY * ROUTE) + (pool == favored).astype(jnp.int32) * (N_RAY * ROUTE)
    rest = pool[jnp.argsort(scores, stable=True)][:count - ROUTE]
    listed = jnp.concatenate([jnp.full((ROUTE,), favored, jnp.int32), rest])
    listed = listed[jax.random.permutation(keys[2], count)]
    plane = jax.random.randint(keys[3], (count,), 0, GX)
    within = jax.random.randint(keys[4], (count,), 0, GY)
    blocks = plane * (GY * N_RAY) + listed * GY + within
    return blocks.reshape(RB_DEV, CAP)


def draw_pattern(key, part):
    key = jax.random.fold_in(key, 9)
    keys = jax.random.split(key, N_RAY * N_MP)
    groups = jax.vmap(owners_of_group)(keys)
    groups = groups.reshape(N_RAY, N_MP, RB_DEV, CAP)
    return jnp.transpose(groups, (0, 2, 1, 3)).reshape(N_RAY * RB_DEV, N_MP * CAP).astype(jnp.int32)


def block_levels(own_key, dims, pieces, least, top_value):
    def one(axis_at, blocks):
        steps = jax.random.uniform(jax.random.fold_in(jax.random.fold_in(own_key, 6), axis_at), (blocks,), jnp.float32, least / len(pieces), top_value / len(pieces))
        return jnp.repeat(jnp.exp(steps), dims[axis_at] // blocks).reshape((-1,) + (1,) * (len(dims) - axis_at - 1))

    gain = one(*pieces[0])
    for cut in pieces[1:]:
        gain = gain * one(*cut)
    return gain


def noise(own_key, extent, width, most, cuts=(), held_as=jnp.bfloat16):
    array = width * jax.random.normal(own_key, extent, jnp.float32)
    if cuts:
        array = array * block_levels(own_key, extent, cuts, -0.22, 0.18)
    return jnp.clip(array, -most, most).astype(held_as)


def setup_inputs(seed: int = 0) -> dict:
    key_of = jax.random.split(jax.random.key(seed), 10)
    slowness = jnp.clip(0.5 + 1.0 * jax.random.uniform(key_of[0], (NX, NY, NZ), jnp.float32) ** block_levels(key_of[0], (NX, NY, NZ), ((0, 32), (1, 16)), -0.2, 0.2), 0.5, 1.5)
    accumulated = noise(key_of[1], (NX, NY, NZ), 0.5, 3.0, ((0, 32), (1, 16)), jnp.float32)
    extrapolated = noise(key_of[2], (NX, NY, NZ), 0.5, 3.0, ((0, 32), (1, 16)), jnp.float32)
    tv_dual = noise(key_of[3], (3, NX, NY, NZ), 0.2, 1.2, ((1, 32), (2, 16)), jnp.float32)
    ray_dual = noise(key_of[4], (RB, TILE), 0.5, 3.0, ((0, 16),), jnp.float32)
    traveltimes = noise(key_of[5], (RB, TILE), 1.0, 6.0, ((0, 16),), jnp.float32)
    tiles = noise(key_of[6], (RB, SLOTS, TILE, TILE), (SLOTS * TILE) ** -0.5, 0.03125, ((0, 16), (1, 32)))
    pattern = draw_pattern(jax.random.fold_in(key_of[9], 71), 0)
    selected = draw_selected(jax.random.fold_in(key_of[9], 71), 0)
    return dict(slowness=slowness, accumulated=accumulated, extrapolated=extrapolated, tv_dual=tv_dual, ray_dual=ray_dual, traveltimes=traveltimes, tiles=tiles, pattern=pattern, selected=selected)


primal_step = 0.5
dual_step = 0.5
tv_step = 0.25
tv_weight = 0.3

def forward_diff(field, axis):
    count = field.shape[axis]
    ahead = lax.slice_in_dim(field, 1, count, axis=axis)
    here = lax.slice_in_dim(field, 0, count - 1, axis=axis)
    widths = [(0, 0)] * field.ndim
    widths[axis] = (0, 1)
    return jnp.pad(ahead - here, widths)

def adjoint_diff(component, axis):
    count = component.shape[axis]
    kept = lax.slice_in_dim(component, 0, count - 1, axis=axis)
    after = [(0, 0)] * component.ndim
    after[axis] = (0, 1)
    before = [(0, 0)] * component.ndim
    before[axis] = (1, 0)
    return jnp.pad(kept, before) - jnp.pad(kept, after)

def total_variation(field, dual):
    grad = jnp.stack([forward_diff(field, 0), forward_diff(field, 1), forward_diff(field, 2)])
    moved = dual + tv_step * grad
    length = jnp.sqrt(lax.optimization_barrier(jnp.sum(moved * moved, axis=0)))
    fresh = moved / jnp.maximum(1.0, length / tv_weight)
    delta = fresh - dual
    back = adjoint_diff(delta[0], 0) + adjoint_diff(delta[1], 1) + adjoint_diff(delta[2], 2)
    return (fresh, back)

def reference(slowness, accumulated, extrapolated, tv_dual, ray_dual, traveltimes, tiles, pattern, selected):
    extrapolation = 2.0 * RB_DEV / (MAXSEL + 1)
    owner = jnp.arange(SLOTS, dtype=jnp.int32) // CAP
    columns = (pattern + owner[None, :] * (GX * NY)).astype(jnp.int32)
    field, image, image_bar, dual, rays = (slowness, accumulated, extrapolated, tv_dual, ray_dual)
    for step in range(ITERS):
        field = field - primal_step * image_bar
        blocks = field.astype(jnp.bfloat16).reshape(NX * NY, NZ)
        taken = selected[step].astype(jnp.float32)

        def one_row(back, inputs):
            tile_row, cols, y_row, t_row, flag = inputs
            tiles_f = tile_row.astype(jnp.float32)
            cells = blocks[cols].astype(jnp.float32)
            predicted = jnp.einsum('sij,sj->i', tiles_f, cells, precision=lax.Precision.HIGHEST)
            fresh = (y_row + dual_step * (predicted - t_row)) / (1.0 + dual_step)
            change = flag * (fresh - y_row)
            change_b = change.astype(jnp.bfloat16).astype(jnp.float32)
            contrib = jnp.einsum('sij,i->sj', tiles_f, change_b, precision=lax.Precision.HIGHEST)
            return (back.at[cols].add(contrib), change)
        back, change = lax.scan(one_row, jnp.zeros((NX * NY, NZ), jnp.float32), (tiles, columns, rays, traveltimes, taken))
        rays = rays + change
        back = back.reshape(NX, NY, NZ)
        dual, tv_back = total_variation(field, dual)
        image = image + back + tv_back
        image_bar = image + extrapolation * back + tv_back
    return (field, rays, dual, image, image_bar)
```

```python
import jax
import jax.numpy as jnp
from jax import lax
from jax.sharding import PartitionSpec as P

RB_DEV = 16
ITERS = 2
MAXSEL = 8


primal_step = 0.5
dual_step = 0.5
tv_step = 0.25
tv_weight = 0.3


def shifted(block, axis, distance):
    devices = range(lax.axis_size(axis))
    route = [(i - distance, i) for i in devices if i - distance in devices]
    return lax.ppermute(block, axis, route)


def to_all(block, axis):
    count = lax.axis_size(axis)
    copies = jnp.broadcast_to(block[None], (count,) + block.shape)
    return lax.all_to_all(copies, axis, 0, 0, tiled=True)


def ray_work(blocks, rays, traveltimes, tiles, cols, flags):
    taken = flags.astype(jnp.float32)[:, None]
    cells = blocks[cols]
    partial_value = jnp.einsum("rsij,rsj->ri", tiles, cells, preferred_element_type=jnp.float32)
    predicted = jnp.sum(to_all(partial_value, "mp"), axis=0)
    fresh = (rays + dual_step * (predicted - traveltimes)) / (1.0 + dual_step)
    change = taken * (fresh - rays)
    contrib = jnp.einsum(
        "rsij,ri->rsj", tiles, change.astype(jnp.bfloat16), preferred_element_type=jnp.float32
    )
    return (rays + change, contrib)


def total_variation(field, dual):
    plane_len, row_len, depth = field.shape
    full_x = plane_len * lax.axis_size("mp")
    xpos = lax.axis_index("mp") * plane_len + jnp.arange(plane_len)
    last_x = (xpos == full_x - 1)[:, None, None]
    full_y = row_len * lax.axis_size("ray")
    ypos = lax.axis_index("ray") * row_len + jnp.arange(row_len)
    last_y = (ypos == full_y - 1)[None, :, None]
    last_z = (jnp.arange(depth) == depth - 1)[None, None, :]
    after_x = shifted(field[0:1], "mp", -1)
    after_y = shifted(field[:, 0:1], "ray", -1)
    step_x = jnp.where(last_x, 0.0, jnp.concatenate([field[1:], after_x], 0) - field)
    step_y = jnp.where(last_y, 0.0, jnp.concatenate([field[:, 1:], after_y], 1) - field)
    step_z = jnp.where(
        last_z,
        0.0,
        jnp.concatenate([field[:, :, 1:], jnp.zeros((plane_len, row_len, 1), jnp.float32)], 2)
        - field,
    )
    moved = dual + tv_step * jnp.stack([step_x, step_y, step_z])
    length = jnp.sqrt(jnp.sum(moved * moved, axis=0))
    fresh = moved / jnp.maximum(1.0, length / tv_weight)
    delta = fresh - dual
    comp_x = jnp.where(last_x, 0.0, delta[0])
    before_x = shifted(comp_x[-1:], "mp", 1)
    back_x = jnp.concatenate([before_x, comp_x[:-1]], 0) - comp_x
    comp_y = jnp.where(last_y, 0.0, delta[1])
    before_y = shifted(comp_y[:, -1:], "ray", 1)
    back_y = jnp.concatenate([before_y, comp_y[:, :-1]], 1) - comp_y
    comp_z = jnp.where(last_z, 0.0, delta[2])
    back_z = (
        jnp.concatenate([jnp.zeros((plane_len, row_len, 1), jnp.float32), comp_z[:, :, :-1]], 2)
        - comp_z
    )
    return (fresh, back_x + back_y + back_z)


def on_device(
    slowness, accumulated, extrapolated, tv_dual, ray_dual, traveltimes, tiles, pattern, selected
):
    extrapolation = 2.0 * RB_DEV / (MAXSEL + 1)
    field, image, image_bar, dual = (slowness, accumulated, extrapolated, tv_dual)
    rays = ray_dual
    planes, rows, depth = field.shape
    peers = lax.axis_size("ray")
    row = pattern % (rows * peers)
    cols = (row // rows) * (planes * rows) + (pattern // (rows * peers)) * rows + row % rows
    for step in range(ITERS):
        field = field - primal_step * image_bar
        rounded = field.astype(jnp.bfloat16).reshape(planes * rows, depth)
        blocks = to_all(rounded, "ray").reshape(-1, depth)
        rays, contrib = ray_work(blocks, rays, traveltimes, tiles, cols, selected[step])
        summed = jax.ops.segment_sum(
            contrib.reshape(-1, depth), cols.reshape(-1), num_segments=blocks.shape[0]
        )
        parts = lax.all_to_all(
            summed.reshape(peers, planes * rows, depth), "ray", 0, 0, tiled=True
        )
        back = jnp.sum(parts, axis=0).reshape(field.shape)
        dual, tv_back = total_variation(field, dual)
        image = image + back + tv_back
        image_bar = image + extrapolation * back + tv_back
    return (field, rays, dual, image, image_bar)


def solution(mesh):
    in_specs = (
        P("mp", "ray", None),
        P("mp", "ray", None),
        P("mp", "ray", None),
        P(None, "mp", "ray", None),
        P("ray", None),
        P("ray", None),
        P("ray", "mp", None, None),
        P("ray", "mp"),
        P(None, "ray"),
    )
    out_specs = (
        P("mp", "ray", None),
        P("ray", None),
        P(None, "mp", "ray", None),
        P("mp", "ray", None),
        P("mp", "ray", None),
    )
    return jax.shard_map(
        on_device, mesh=mesh, in_specs=in_specs, out_specs=out_specs, check_vma=False
    )
```

```python
import functools

import jax
import jax.numpy as jnp
from jax import lax
from jax.experimental import pallas as pl
from jax.experimental.pallas import tpu as pltpu
from jax.sharding import PartitionSpec as P

TILE = 128
GX = 4
GY = 8
RB_DEV = 16
CAP = 8
MAXSEL = 8
N_RAY = 16
N_MP = 32
OWN = GX * GY
ALL = N_RAY * OWN
PRODUCTS = MAXSEL * CAP
SENT = OWN + 16

primal_step = 0.5
dual_step = 0.5
tv_step = 0.25
tv_weight = 0.3
extrapolation = 2.0 * RB_DEV / (MAXSEL + 1)

F32 = jnp.float32
BF16 = jnp.bfloat16


def shifted(block, axis, distance):
    devices = range(lax.axis_size(axis))
    route = [(i - distance, i) for i in devices if i - distance in devices]
    return lax.ppermute(block, axis, route)


def exchange(copies, axis):
    return lax.all_to_all(copies, axis, 0, 0, tiled=True)


def block_number(pattern):
    row = pattern & (GY * N_RAY - 1)
    plane = pattern // (GY * N_RAY)
    return (row // GY) * OWN + plane * GY + (row & (GY - 1))


def list_selected(selected_ref, step, list_ref):
    for n in range(MAXSEL):
        list_ref[n] = 0
    count = jnp.int32(0)
    for r in range(RB_DEV):
        list_ref[count] = jnp.int32(r)
        count = count + selected_ref[step, r]
    return count


def forward(table_ref, pattern_ref, tiles_ref, list_ref):
    sub = lax.broadcasted_iota(jnp.int32, (MAXSEL, TILE), 0)
    total = jnp.zeros((MAXSEL, TILE), F32)
    for n in range(MAXSEL):
        r = list_ref[n]
        cells = []
        for s in range(CAP):
            b = block_number(pattern_ref[r, s])
            row = table_ref[pl.ds(b, 1), :]
            cells.append(jnp.where(sub == n, row, 0.0).astype(BF16))
        for s in range(CAP):
            total = total + lax.dot_general(
                cells[s], tiles_ref[r, s], (((1,), (1,)), ((), ())), preferred_element_type=F32
            )
    return total


def first_kernel(slowness_ref, bar_ref, pattern_ref, selected_ref, field_ref, sent_ref, list_ref):
    field = slowness_ref[...] - primal_step * bar_ref[...]
    field_ref[...] = field
    rounded = field.reshape(OWN, TILE).astype(BF16)
    list_selected(selected_ref, 0, list_ref)
    lane = lax.broadcasted_iota(jnp.int32, (16, TILE), 1)
    sub = lax.broadcasted_iota(jnp.int32, (16, TILE), 0)
    numbers = jnp.zeros((16, TILE), jnp.int32)
    for n in range(MAXSEL):
        r = list_ref[n]
        for s in range(CAP):
            b = block_number(pattern_ref[r, s])
            numbers = jnp.where((lane & (PRODUCTS - 1)) == n * CAP + s, b, numbers)
    numbers = jnp.where(sub == 0, numbers // OWN, numbers & (OWN - 1))
    numbers = numbers.astype(F32).astype(BF16)
    for p in range(N_RAY):
        sent_ref[p, 0:OWN, :] = rounded
        sent_ref[p, OWN:SENT, :] = numbers


def predict_kernel(gathered_ref, tiles_ref, pattern_ref, selected_ref, out_ref, table_ref, list_ref):
    list_selected(selected_ref, 0, list_ref)
    for p in range(N_RAY):
        table_ref[p * OWN : (p + 1) * OWN, :] = gathered_ref[p, 0:OWN, :].astype(F32)
    total = forward(table_ref, pattern_ref, tiles_ref, list_ref)
    for m in range(N_MP):
        out_ref[m] = total


def dual_update(parts_ref, rays_ref, times_ref, new_rays_ref, list_ref, count):
    predicted = parts_ref[0]
    for m in range(1, N_MP):
        predicted = predicted + parts_ref[m]
    rays = jnp.concatenate([rays_ref[pl.ds(list_ref[n], 1), :] for n in range(MAXSEL)], axis=0)
    times = jnp.concatenate([times_ref[pl.ds(list_ref[n], 1), :] for n in range(MAXSEL)], axis=0)
    fresh = (rays + dual_step * (predicted - times)) / (1.0 + dual_step)
    sub = lax.broadcasted_iota(jnp.int32, (MAXSEL, TILE), 0)
    change = jnp.where(sub < count, fresh - rays, 0.0)
    new_rays_ref[...] = rays_ref[...]
    for n in range(MAXSEL):
        r = list_ref[n]
        new_rays_ref[pl.ds(r, 1), :] = new_rays_ref[pl.ds(r, 1), :] + change[n : n + 1]
    return change


def products(change, tiles_ref, list_ref, n):
    sub = lax.broadcasted_iota(jnp.int32, (CAP, TILE), 0)
    row = change[n : n + 1]
    r = list_ref[n]
    total = jnp.zeros((CAP, TILE), F32)
    for s in range(CAP):
        lhs = jnp.where(sub == s, row, 0.0).astype(BF16)
        total = total + lax.dot_general(
            lhs, tiles_ref[r, s], (((1,), (0,)), ((), ())), preferred_element_type=F32
        )
    return total


def back_share_kernel(
    parts_ref, rays_ref, times_ref, tiles_ref, selected_ref, rest_ref, new_rays_ref, out_ref, list_ref
):
    count = list_selected(selected_ref, 0, list_ref)
    change = dual_update(parts_ref, rays_ref, times_ref, new_rays_ref, list_ref, count)
    for n in range(0, MAXSEL, 2):
        pair = jnp.concatenate(
            [products(change, tiles_ref, list_ref, n), products(change, tiles_ref, list_ref, n + 1)]
        ).astype(BF16)
        for p in range(N_RAY):
            out_ref[p, n * CAP : (n + 2) * CAP, :] = pair
    rest = rest_ref[...]
    for p in range(N_RAY):
        out_ref[p, PRODUCTS : PRODUCTS + OWN, :] = rest


def image_kernel(
    shared_ref, gathered_ref, tiles_ref, pattern_ref, selected_ref, me_ref, back_ref, out_ref, table_ref, list_ref
):
    list_selected(selected_ref, 1, list_ref)
    lane = lax.broadcasted_iota(jnp.int32, (1, TILE), 1)
    pairs = []
    for p in range(N_RAY):
        rows = gathered_ref[p, OWN:SENT, :].astype(F32)
        pairs.append(rows[0:1] * OWN + rows[1:2])
    pairs = [jnp.where(lane < PRODUCTS, pairs[p], pairs[p + 1]) for p in range(0, N_RAY, 2)]
    group = 4
    numbers = []
    terms = []
    for g in range(0, N_RAY, group):
        numbers.append(jnp.concatenate([pairs[g // 2], pairs[g // 2 + 1]], axis=1).astype(jnp.int32))
        terms.append(jnp.concatenate([shared_ref[p, 0:PRODUCTS, :] for p in range(g, g + group)], axis=0))
    chunk = group * OWN
    me = me_ref[0]
    place = lax.broadcasted_iota(jnp.int32, (chunk, group * PRODUCTS), 0)
    for g in range(0, N_RAY, group):
        back = jnp.zeros((chunk, TILE), F32)
        for k in range(N_RAY // group):
            hot = jnp.where(place + g * OWN == numbers[k], 1.0, 0.0).astype(BF16)
            back = back + lax.dot_general(
                hot, terms[k], (((1,), (0,)), ((), ())), preferred_element_type=F32
            )
        table_ref[g * OWN : g * OWN + chunk, :] = back
    back_ref[...] = table_ref[pl.ds(pl.multiple_of(me * OWN, OWN), OWN), :]
    for p in range(N_RAY):
        rows = slice(p * OWN, (p + 1) * OWN)
        before = gathered_ref[p, 0:OWN, :].astype(F32)
        rest = shared_ref[p, PRODUCTS : PRODUCTS + OWN, :].astype(F32)
        field = before + (rest - (primal_step * (1.0 + extrapolation)) * table_ref[rows, :])
        table_ref[rows, :] = field.astype(BF16).astype(F32)
    total = forward(table_ref, pattern_ref, tiles_ref, list_ref)
    for m in range(N_MP):
        out_ref[m] = total


def back_kernel(
    parts_ref, rays_ref, times_ref, tiles_ref, pattern_ref, selected_ref, new_rays_ref, out_ref, table_ref, list_ref
):
    count = list_selected(selected_ref, 1, list_ref)
    change = dual_update(parts_ref, rays_ref, times_ref, new_rays_ref, list_ref, count)
    table_ref[...] = jnp.zeros_like(table_ref)
    for n in range(MAXSEL):
        r = list_ref[n]
        total = products(change, tiles_ref, list_ref, n)
        for s in range(CAP):
            b = block_number(pattern_ref[r, s])
            table_ref[pl.ds(b, 1), :] = table_ref[pl.ds(b, 1), :] + total[s : s + 1]
    for p in range(N_RAY):
        out_ref[p] = table_ref[p * OWN : (p + 1) * OWN, :].astype(BF16)


def call(kernel, outs, places, *args):
    spaces = {"v": pltpu.VMEM, "s": pltpu.SMEM}
    scratch = [pltpu.SMEM((RB_DEV,), jnp.int32)]
    if kernel in (predict_kernel, image_kernel, back_kernel):
        scratch = [pltpu.VMEM((ALL, TILE), F32)] + scratch
    return pl.pallas_call(
        kernel,
        out_shape=[jax.ShapeDtypeStruct(shape, dtype) for shape, dtype in outs],
        in_specs=[pl.BlockSpec(memory_space=spaces[c]) for c in places],
        out_specs=[pl.BlockSpec(memory_space=pltpu.VMEM) for _ in outs],
        scratch_shapes=scratch,
        compiler_params=pltpu.CompilerParams(vmem_limit_bytes=24 * 1024 * 1024),
    )(*args)


def total_variation(field, dual):
    plane_len, row_len, depth = field.shape
    full_x = plane_len * lax.axis_size("mp")
    xpos = lax.axis_index("mp") * plane_len + jnp.arange(plane_len)
    last_x = (xpos == full_x - 1)[:, None, None]
    full_y = row_len * lax.axis_size("ray")
    ypos = lax.axis_index("ray") * row_len + jnp.arange(row_len)
    last_y = (ypos == full_y - 1)[None, :, None]
    last_z = (jnp.arange(depth) == depth - 1)[None, None, :]
    after_x = shifted(field[0:1], "mp", -1)
    after_y = shifted(field[:, 0:1], "ray", -1)
    step_x = jnp.where(last_x, 0.0, jnp.concatenate([field[1:], after_x], 0) - field)
    step_y = jnp.where(last_y, 0.0, jnp.concatenate([field[:, 1:], after_y], 1) - field)
    step_z = jnp.where(
        last_z,
        0.0,
        jnp.concatenate([field[:, :, 1:], jnp.zeros((plane_len, row_len, 1), jnp.float32)], 2)
        - field,
    )
    moved = dual + tv_step * jnp.stack([step_x, step_y, step_z])
    length = jnp.sqrt(jnp.sum(moved * moved, axis=0))
    fresh = moved / jnp.maximum(1.0, length / tv_weight)
    delta = fresh - dual
    comp_x = jnp.where(last_x, 0.0, delta[0])
    before_x = shifted(comp_x[-1:], "mp", 1)
    back_x = jnp.concatenate([before_x, comp_x[:-1]], 0) - comp_x
    comp_y = jnp.where(last_y, 0.0, delta[1])
    before_y = shifted(comp_y[:, -1:], "ray", 1)
    back_y = jnp.concatenate([before_y, comp_y[:, :-1]], 1) - comp_y
    comp_z = jnp.where(last_z, 0.0, delta[2])
    back_z = (
        jnp.concatenate([jnp.zeros((plane_len, row_len, 1), jnp.float32), comp_z[:, :, :-1]], 2)
        - comp_z
    )
    return (fresh, back_x + back_y + back_z)


def on_device(
    slowness, accumulated, extrapolated, tv_dual, ray_dual, traveltimes, tiles, pattern, selected
):
    grid = slowness.shape
    me = lax.axis_index("ray").astype(jnp.int32).reshape(1)
    sums = ((N_MP, MAXSEL, TILE), F32)
    rays_out = (ray_dual.shape, F32)

    field, sent = call(
        first_kernel, [(grid, F32), ((N_RAY, SENT, TILE), BF16)], "vvss",
        slowness, extrapolated, pattern, selected,
    )
    gathered = exchange(sent, "ray")
    (partial_value,) = call(predict_kernel, [sums], "vvss", gathered, tiles, pattern, selected)
    parts = exchange(partial_value, "mp")

    dual, tv_back = total_variation(field, tv_dual)
    base = field - primal_step * (accumulated + 2.0 * tv_back)
    rest = (base - field.astype(BF16).astype(F32)).astype(BF16).reshape(OWN, TILE)

    rays, share = call(
        back_share_kernel, [rays_out, ((N_RAY, PRODUCTS + OWN, TILE), BF16)], "vvvvsv",
        parts, ray_dual, traveltimes, tiles, selected, rest,
    )
    shared = exchange(share, "ray")
    back, partial_value = call(
        image_kernel, [((OWN, TILE), F32), sums], "vvvsss",
        shared, gathered, tiles, pattern, selected, me,
    )
    parts = exchange(partial_value, "mp")

    back = back.reshape(grid)
    field = base - (primal_step * (1.0 + extrapolation)) * back
    image = accumulated + back + tv_back
    dual, tv_back = total_variation(field, dual)
    image = image + tv_back

    rays, share = call(
        back_kernel, [rays_out, ((N_RAY, OWN, TILE), BF16)], "vvvvss",
        parts, rays, traveltimes, tiles, pattern, selected,
    )
    back = jnp.sum(exchange(share, "ray").astype(F32), axis=0).reshape(grid)
    image = image + back
    image_bar = image + extrapolation * back + tv_back
    return (field, rays, dual, image, image_bar)


def solution(mesh):
    in_specs = (
        P("mp", "ray", None),
        P("mp", "ray", None),
        P("mp", "ray", None),
        P(None, "mp", "ray", None),
        P("ray", None),
        P("ray", None),
        P("ray", "mp", None, None),
        P("ray", "mp"),
        P(None, "ray"),
    )
    out_specs = (
        P("mp", "ray", None),
        P("ray", None),
        P(None, "mp", "ray", None),
        P("mp", "ray", None),
        P("mp", "ray", None),
    )
    return jax.shard_map(
        on_device, mesh=mesh, in_specs=in_specs, out_specs=out_specs, check_vma=False
    )
```

```python
import jax
import jax.numpy as jnp
from jax import lax
from jax.experimental import pallas as pl
from jax.experimental.pallas import tpu as pltpu
from jax.sharding import PartitionSpec as P

TILE = 128
GX = 4
GY = 8
RB_DEV = 16
CAP = 8
MAXSEL = 8
N_RAY = 16
N_MP = 32
OWN = GX * GY
ALL = N_RAY * OWN
PRODUCTS = MAXSEL * CAP
SENT = OWN + 16

primal_step = 0.5
dual_step = 0.5
tv_step = 0.25
tv_weight = 0.3
extrapolation = 2.0 * RB_DEV / (MAXSEL + 1)
gain = primal_step * (1.0 + extrapolation)

F32 = jnp.float32
BF16 = jnp.bfloat16
GRID = (GX, GY, TILE)
SUMS = ((N_MP, MAXSEL, TILE), F32)
RAYS = ((RB_DEV, TILE), F32)


def exchange(copies, axis):
    return lax.all_to_all(copies, axis, 0, 0, tiled=True)


def call(kernel, outs, places, args, scratch=(), busy=0):
    spaces = {"v": pltpu.VMEM, "h": pltpu.HBM}
    cost = pl.CostEstimate(flops=0, bytes_accessed=busy, transcendentals=0) if busy else None
    return pl.pallas_call(
        kernel,
        out_shape=[jax.ShapeDtypeStruct(shape, dtype) for shape, dtype in outs],
        in_specs=[pl.BlockSpec(memory_space=spaces[c]) for c in places],
        out_specs=[pl.BlockSpec(memory_space=pltpu.VMEM) for _ in outs],
        scratch_shapes=list(scratch),
        cost_estimate=cost,
        compiler_params=pltpu.CompilerParams(vmem_limit_bytes=20 * 1024 * 1024),
    )(*args)


SCALARS = (
    pltpu.SMEM((CAP, RB_DEV), jnp.int32),
    pltpu.SMEM((2, RB_DEV), jnp.int32),
    pltpu.SMEM((RB_DEV,), jnp.int32),
    pltpu.SemaphoreType.DMA((2,)),
)


def scalar_copies(pattern_hbm, selected_hbm, pattern_ref, selected_ref, sems):
    return [
        pltpu.make_async_copy(pattern_hbm, pattern_ref, sems.at[0]),
        pltpu.make_async_copy(selected_hbm, selected_ref, sems.at[1]),
    ]


def block_number(pattern):
    row = pattern & (GY * N_RAY - 1)
    plane = lax.shift_right_logical(pattern, 7)
    return lax.shift_right_logical(row, 3) * OWN + plane * GY + (row & (GY - 1))


def list_selected(selected_ref, step, list_ref):
    for n in range(MAXSEL):
        list_ref[n] = jnp.int32(0)
    count = jnp.int32(0)
    for r in range(RB_DEV):
        list_ref[count] = jnp.int32(r)
        count = count + selected_ref[step, r]
    return count


def start_kernel(
    slowness_hbm, bar_hbm, pattern_hbm, selected_hbm, field_ref, sent_ref,
    slowness_ref, bar_ref, sems, pattern_ref, selected_ref, list_ref, scalar_sems,
):
    copies = scalar_copies(pattern_hbm, selected_hbm, pattern_ref, selected_ref, scalar_sems)
    copies.append(pltpu.make_async_copy(slowness_hbm, slowness_ref, sems.at[0]))
    copies.append(pltpu.make_async_copy(bar_hbm, bar_ref, sems.at[1]))
    for copy in copies:
        copy.start()
    copies[0].wait()
    copies[1].wait()
    list_selected(selected_ref, 0, list_ref)
    lane = lax.broadcasted_iota(jnp.int32, (16, TILE), 1) & (PRODUCTS - 1)
    sub = lax.broadcasted_iota(jnp.int32, (16, TILE), 0)
    numbers = jnp.zeros((16, TILE), jnp.int32)
    for n in range(MAXSEL):
        r = list_ref[n]
        for s in range(CAP):
            numbers = jnp.where(lane == n * CAP + s, block_number(pattern_ref[s, r]), numbers)
    numbers = jnp.where(sub == 0, lax.shift_right_logical(numbers, 5), numbers & (OWN - 1))
    numbers = numbers.astype(F32).astype(BF16)
    copies[2].wait()
    copies[3].wait()
    field = slowness_ref[...] - primal_step * bar_ref[...]
    field_ref[...] = field
    rounded = field.reshape(OWN, TILE).astype(BF16)
    for p in range(N_RAY):
        sent_ref[p, 0:OWN, :] = rounded
        sent_ref[p, OWN:SENT, :] = numbers


def fetch_kernel(step):
    def kernel(
        tiles_hbm, pattern_hbm, selected_hbm, after_ref, picked_ref, hot_ref, pick_ref,
        pattern_ref, selected_ref, list_ref, scalar_sems, sems,
    ):
        for copy in scalar_copies(pattern_hbm, selected_hbm, pattern_ref, selected_ref, scalar_sems):
            copy.start()
            copy.wait()
        count = list_selected(selected_ref, step, list_ref)
        copies = [
            pltpu.make_async_copy(tiles_hbm.at[list_ref[n]], picked_ref.at[n], sems.at[n])
            for n in range(MAXSEL)
        ]
        for copy in copies:
            copy.start()
        sub = lax.broadcasted_iota(jnp.int32, (MAXSEL, TILE), 0)
        lane = lax.broadcasted_iota(jnp.int32, (2 * CAP, TILE), 1)
        for n in range(0, MAXSEL, 2):
            halves = []
            for m in (n, n + 1):
                r = list_ref[m]
                numbers = jnp.zeros((CAP, TILE), jnp.int32)
                for s in range(CAP):
                    numbers = jnp.where(sub == s, block_number(pattern_ref[s, r]), numbers)
                halves.append(numbers)
            numbers = jnp.concatenate(halves, axis=0)
            for c in range(ALL // TILE):
                hot = jnp.where(numbers == lane + c * TILE, 1.0, 0.0).astype(BF16)
                hot_ref[n * CAP : (n + 2) * CAP, c * TILE : (c + 1) * TILE] = hot
        listed = jnp.full((MAXSEL, TILE), RB_DEV, jnp.int32)
        for n in range(MAXSEL):
            listed = jnp.where((sub == n) & (sub < count), list_ref[n], listed)
        for r in range(RB_DEV):
            pick_ref[r] = jnp.where(listed == r, 1.0, 0.0)
        for copy in copies:
            copy.wait()

    return kernel


def fetch(step, tiles, pattern, selected, after):
    outs = [
        ((MAXSEL, CAP, TILE, TILE), BF16),
        ((PRODUCTS, ALL), BF16),
        ((RB_DEV, MAXSEL, TILE), F32),
    ]
    scratch = SCALARS + (pltpu.SemaphoreType.DMA((MAXSEL,)),)
    return call(
        fetch_kernel(step), outs, "hhhh", (tiles, pattern, selected, after), scratch, 8 * 2**20
    )


def forward(hot_ref, blocks, picked_ref, out_ref):
    cells = jnp.dot(hot_ref[...], blocks, preferred_element_type=F32)
    sub = lax.broadcasted_iota(jnp.int32, (MAXSEL, TILE), 0)
    total = jnp.zeros((MAXSEL, TILE), F32)
    for n in range(MAXSEL):
        for s in range(CAP):
            row = cells[n * CAP + s : n * CAP + s + 1]
            lhs = jnp.where(sub == n, row, 0.0).astype(BF16)
            total = total + lax.dot_general(
                lhs, picked_ref[n, s], (((1,), (1,)), ((), ())), preferred_element_type=F32
            )
    for m in range(N_MP):
        out_ref[m] = total


def predict_kernel(gathered_ref, picked_ref, hot_ref, out_ref):
    blocks = jnp.concatenate([gathered_ref[p, 0:OWN, :] for p in range(N_RAY)], axis=0)
    forward(hot_ref, blocks, picked_ref, out_ref)


def dual_update(parts_ref, rays_ref, times_ref, pick_ref, new_rays_ref):
    predicted = parts_ref[0]
    for m in range(1, N_MP):
        predicted = predicted + parts_ref[m]
    rays = jnp.zeros((MAXSEL, TILE), F32)
    times = jnp.zeros((MAXSEL, TILE), F32)
    taken = jnp.zeros((MAXSEL, TILE), F32)
    for r in range(RB_DEV):
        pick = pick_ref[r]
        rays = rays + pick * rays_ref[r : r + 1, :]
        times = times + pick * times_ref[r : r + 1, :]
        taken = taken + pick
    fresh = (rays + dual_step * (predicted - times)) / (1.0 + dual_step)
    change = taken * (fresh - rays)
    for r in range(RB_DEV):
        new_rays_ref[r : r + 1, :] = rays_ref[r : r + 1, :] + jnp.sum(
            pick_ref[r] * change, axis=0, keepdims=True
        )
    return change


def products(change, picked_ref, n):
    sub = lax.broadcasted_iota(jnp.int32, (CAP, TILE), 0)
    row = change[n : n + 1]
    total = jnp.zeros((CAP, TILE), F32)
    for s in range(CAP):
        lhs = jnp.where(sub == s, row, 0.0).astype(BF16)
        total = total + jnp.dot(lhs, picked_ref[n, s], preferred_element_type=F32)
    return total


def share_kernel(
    parts_ref, rays_ref, times_ref, pick_ref, picked_ref, rest_ref, new_rays_ref, out_ref
):
    change = dual_update(parts_ref, rays_ref, times_ref, pick_ref, new_rays_ref)
    for n in range(0, MAXSEL, 2):
        pair = jnp.concatenate(
            [products(change, picked_ref, n), products(change, picked_ref, n + 1)], axis=0
        ).astype(BF16)
        for p in range(N_RAY):
            out_ref[p, n * CAP : (n + 2) * CAP, :] = pair
    rest = rest_ref[...]
    for p in range(N_RAY):
        out_ref[p, PRODUCTS : PRODUCTS + OWN, :] = rest


def image_kernel(
    shared_ref, gathered_ref, picked_ref, hot_ref, back_ref, edge_ref, out_ref, table_ref
):
    lane = lax.broadcasted_iota(jnp.int32, (1, TILE), 1)
    singles = []
    for p in range(N_RAY):
        rows = gathered_ref[p, OWN:SENT, :].astype(F32)
        singles.append(rows[0:1] * OWN + rows[1:2])
    pairs = [jnp.where(lane < PRODUCTS, singles[p], singles[p + 1]) for p in range(0, N_RAY, 2)]
    group = 4
    chunk = group * OWN
    numbers = []
    terms = []
    for g in range(0, N_RAY, group):
        numbers.append(jnp.concatenate(pairs[g // 2 : g // 2 + 2], axis=1).astype(jnp.int32))
        terms.append(
            jnp.concatenate([shared_ref[p, 0:PRODUCTS, :] for p in range(g, g + group)], axis=0)
        )
    place = lax.broadcasted_iota(jnp.int32, (chunk, group * PRODUCTS), 0)
    blocks = []
    for g in range(0, N_RAY, group):
        back = jnp.zeros((chunk, TILE), F32)
        for k in range(N_RAY // group):
            hot = jnp.where(place + g * OWN == numbers[k], 1.0, 0.0).astype(BF16)
            back = back + jnp.dot(hot, terms[k], preferred_element_type=F32)
        table_ref[g * OWN : g * OWN + chunk, :] = back
        before = jnp.concatenate([gathered_ref[p, 0:OWN, :] for p in range(g, g + group)], axis=0)
        rest = jnp.concatenate(
            [shared_ref[p, PRODUCTS : PRODUCTS + OWN, :] for p in range(g, g + group)], axis=0
        )
        blocks.append((before.astype(F32) + (rest.astype(F32) - gain * back)).astype(BF16))
    forward(hot_ref, jnp.concatenate(blocks, axis=0), picked_ref, out_ref)
    me = lax.axis_index("ray")
    back_ref[...] = table_ref[pl.ds(pl.multiple_of(me * OWN, OWN), OWN), :]
    for at, peer, row in ((0, jnp.maximum(me - 1, 0), GY - 1), (1, jnp.minimum(me + 1, N_RAY - 1), 0)):
        before = gathered_ref[peer, 0:OWN, :].astype(F32)
        rest = shared_ref[peer, PRODUCTS : PRODUCTS + OWN, :].astype(F32)
        back = table_ref[pl.ds(pl.multiple_of(peer * OWN, OWN), OWN), :]
        field = before + (rest - gain * back)
        for x in range(GX):
            edge_ref[at * GX + x : at * GX + x + 1, :] = field[x * GY + row : x * GY + row + 1]


def back_kernel(
    parts_ref, rays_ref, times_ref, pick_ref, picked_ref, hot_ref, new_rays_ref, out_ref
):
    change = dual_update(parts_ref, rays_ref, times_ref, pick_ref, new_rays_ref)
    terms = jnp.concatenate([products(change, picked_ref, n) for n in range(MAXSEL)], axis=0)
    high = terms.astype(BF16)
    low = (terms - high.astype(F32)).astype(BF16)
    turned = (((0,), (0,)), ((), ()))
    image = lax.dot_general(hot_ref[...], high, turned, preferred_element_type=F32)
    image = image + lax.dot_general(hot_ref[...], low, turned, preferred_element_type=F32)
    for p in range(N_RAY):
        out_ref[p] = image[p * OWN : (p + 1) * OWN].astype(BF16)


def x_swaps(far, near):
    far_route = [(m, m + 1) for m in range(1, N_MP - 1, 2)]
    near_route = [(m, m + 1) for m in range(0, N_MP - 1, 2)]
    far = lax.ppermute(far, "mp", far_route + [(b, a) for a, b in far_route])
    near = lax.ppermute(near, "mp", near_route + [(b, a) for a, b in near_route])
    return far, near


def first_edges_kernel(field_ref, dual_ref, far_ref, near_ref):
    odd = (lax.axis_index("mp") & 1) == 1
    first = field_ref[0]
    last = field_ref[GX - 1]
    far_ref[0:GY] = jnp.where(odd, last, first)
    near_ref[0:GY] = jnp.where(odd, first, last)
    for c in range(3):
        rows = slice((c + 1) * GY, (c + 2) * GY)
        far_ref[rows] = dual_ref[c, GX - 1]
        near_ref[rows] = dual_ref[c, GX - 1]


def x_halos(far_ref, near_ref):
    odd = (lax.axis_index("mp") & 1) == 1
    far, near = far_ref[...], near_ref[...]
    return jnp.where(odd, near, far), jnp.where(odd, far, near)


def row_edges_kernel(field_ref, dual_ref, far_ref, near_ref, after_ref, up_ref, down_ref):
    before, behind = x_halos(far_ref, near_ref)
    up_ref[...] = jnp.zeros_like(up_ref)
    down_ref[...] = jnp.zeros_like(down_ref)
    up_ref[GX : GX + 1] = before[0:1]
    down_ref[GX : GX + 1] = behind[GY - 1 : GY]
    for x in range(GX):
        up_ref[x : x + 1] = field_ref[x, 0:1]
        down_ref[x : x + 1] = field_ref[x, GY - 1 : GY]
        for c in range(3):
            at = 8 + c * GX + x
            down_ref[at : at + 1] = dual_ref[c, x, GY - 1 : GY]


def tv_cells(here, ahead_x, ahead_y, dual, no_x, no_y):
    lane = lax.broadcasted_iota(jnp.int32, here.shape, len(here.shape) - 1)
    ahead_z = pltpu.roll(here, TILE - 1, len(here.shape) - 1)
    steps = (
        jnp.where(no_x, 0.0, ahead_x - here),
        jnp.where(no_y, 0.0, ahead_y - here),
        jnp.where(lane == TILE - 1, 0.0, ahead_z - here),
    )
    moved = [d + tv_step * g for d, g in zip(dual, steps)]
    length = jnp.sqrt(moved[0] * moved[0] + moved[1] * moved[1] + moved[2] * moved[2])
    scale = jnp.maximum(1.0, length / tv_weight)
    fresh = [m / scale for m in moved]
    return fresh, [a - b for a, b in zip(fresh, dual)]


def up_one(plane, row):
    sub = lax.broadcasted_iota(jnp.int32, plane.shape, 0)
    return jnp.where(sub == GY - 1, row, pltpu.roll(plane, GY - 1, 0))


def tv_step_all(field, dual, before, before_next, dual_before, behind, corner, rows, dual_rows, next_rows):
    mp, ray = lax.axis_index("mp"), lax.axis_index("ray")
    sub = lax.broadcasted_iota(jnp.int32, (GY, TILE), 0)
    end_x = mp == N_MP - 1
    last_y = (sub == GY - 1) & (ray == N_RAY - 1)
    never = sub < 0
    lane = lax.broadcasted_iota(jnp.int32, (GY, TILE), 1)

    halo, halo_change = tv_cells(
        before, field[0], up_one(before, before_next), dual_before, never, last_y
    )
    from_x = jnp.where(mp == 0, 0.0, halo_change[0])
    fresh, backs, halo_rows = [], [], []
    for x in range(GX):
        ahead = field[x + 1] if x + 1 < GX else behind
        no_x = (end_x & (sub >= 0)) if x + 1 == GX else never
        new, change = tv_cells(
            field[x], ahead, up_one(field[x], next_rows[x]), [d[x] for d in dual], no_x, last_y
        )
        ahead_row = rows[x + 1] if x + 1 < GX else corner
        no_row = (end_x & (sub[0:1] >= 0)) if x + 1 == GX else never[0:1]
        new_row, row_change = tv_cells(
            rows[x], ahead_row, field[x][0:1], [d[x] for d in dual_rows], no_row, never[0:1]
        )
        from_y = jnp.where(ray == 0, 0.0, row_change[1])
        comp_x = jnp.where(no_x, 0.0, change[0])
        comp_y = jnp.where(last_y, 0.0, change[1])
        comp_z = jnp.where(lane == TILE - 1, 0.0, change[2])
        back = from_x - comp_x
        back = back + (jnp.where(sub == 0, from_y, pltpu.roll(comp_y, 1, 0)) - comp_y)
        back = back + (jnp.where(lane == 0, 0.0, pltpu.roll(comp_z, 1, 1)) - comp_z)
        from_x = comp_x
        fresh.append(new)
        backs.append(back)
        halo_rows.append(new_row)
    return fresh, backs, halo, halo_rows


def first_tv_kernel(
    field_ref, dual_ref, far_ref, near_ref, up_ref, down_ref, image_ref,
    new_dual_ref, plane_ref, row_ref, back_ref, base_ref, rest_ref,
):
    before, behind = x_halos(far_ref, near_ref)
    field = [field_ref[x] for x in range(GX)]
    dual = [[dual_ref[c, x] for x in range(GX)] for c in range(3)]
    up, down = up_ref[...], down_ref[...]
    rows = [down[x : x + 1] for x in range(GX)]
    dual_rows = [[down[8 + c * GX + x : 9 + c * GX + x] for x in range(GX)] for c in range(3)]
    fresh, backs, halo, halo_rows = tv_step_all(
        field, dual, before[0:GY], up[GX : GX + 1],
        [before[(c + 1) * GY : (c + 2) * GY] for c in range(3)],
        behind[0:GY], down[GX : GX + 1], rows, dual_rows, [up[x : x + 1] for x in range(GX)],
    )
    for x in range(GX):
        base = field[x] - primal_step * (image_ref[x] + 2.0 * backs[x])
        back_ref[x] = backs[x]
        base_ref[x] = base
        rest_ref[x] = base - field[x].astype(BF16).astype(F32)
        for c in range(3):
            new_dual_ref[c, x] = fresh[x][c]
            row_ref[c * GX + x : c * GX + x + 1] = halo_rows[x][c]
    for c in range(3):
        plane_ref[c] = halo[c]


def second_edges_kernel(base_ref, back_ref, edge_ref, image_ref, tv_ref, field_ref, new_image_ref, far_ref, near_ref):
    odd = (lax.axis_index("mp") & 1) == 1
    field = []
    for x in range(GX):
        back = back_ref[x * GY : (x + 1) * GY]
        field.append(base_ref[x] - gain * back)
        field_ref[x] = field[x]
        new_image_ref[x] = image_ref[x] + back + tv_ref[x]
    first = jnp.concatenate([field[0], edge_ref[...]], axis=0)
    last = jnp.concatenate([field[GX - 1], edge_ref[...]], axis=0)
    far_ref[...] = jnp.where(odd, last, first)
    near_ref[...] = jnp.where(odd, first, last)


def second_tv_kernel(
    field_ref, dual_ref, plane_ref, row_ref, far_ref, near_ref, edge_ref, new_dual_ref, back_ref
):
    before, behind = x_halos(far_ref, near_ref)
    edge = edge_ref[...]
    fresh, backs, _, _ = tv_step_all(
        [field_ref[x] for x in range(GX)],
        [[dual_ref[c, x] for x in range(GX)] for c in range(3)],
        before[0:GY], before[GY + 2 * GX - 1 : GY + 2 * GX],
        [plane_ref[c] for c in range(3)],
        behind[0:GY], behind[GY : GY + 1],
        [edge[x : x + 1] for x in range(GX)],
        [[row_ref[c * GX + x : c * GX + x + 1] for x in range(GX)] for c in range(3)],
        [edge[GX + x : GX + x + 1] for x in range(GX)],
    )
    for x in range(GX):
        back_ref[x] = backs[x]
        for c in range(3):
            new_dual_ref[c, x] = fresh[x][c]


def on_device(
    slowness, accumulated, extrapolated, tv_dual, ray_dual, traveltimes, tiles, pattern, selected
):
    pattern = pattern.T
    busy = 8 * 2**20
    grid = (GRID, F32)
    duals = ((3,) + GRID, F32)

    field, sent = call(
        start_kernel, [grid, ((N_RAY, SENT, TILE), BF16)], "hhhh",
        (slowness, extrapolated, pattern, selected),
        (pltpu.VMEM(GRID, F32), pltpu.VMEM(GRID, F32), pltpu.SemaphoreType.DMA((2,))) + SCALARS,
    )
    gathered = exchange(sent, "ray")
    far, near = call(
        first_edges_kernel, [((4 * GY, TILE), F32)] * 2, "vv", (field, tv_dual), busy=busy
    )
    far, near = x_swaps(far, near)
    picked, hot, pick = fetch(0, tiles, pattern, selected, field)
    (partial_value,) = call(predict_kernel, [SUMS], "vvv", (gathered, picked, hot))
    parts = exchange(partial_value, "mp")

    up, down = call(
        row_edges_kernel, [((8, TILE), F32), ((24, TILE), F32)], "vvvvh",
        (field, tv_dual, far, near, partial_value), busy=busy,
    )
    up = lax.ppermute(up, "ray", [(i + 1, i) for i in range(N_RAY - 1)])
    down = lax.ppermute(down, "ray", [(i, i + 1) for i in range(N_RAY - 1)])
    dual, dual_plane, dual_row, tv_back, base, rest = call(
        first_tv_kernel,
        [duals, ((3, GY, TILE), F32), ((3 * GX, TILE), F32), grid, grid, grid],
        "vvvvvvv", (field, tv_dual, far, near, up, down, accumulated), busy=busy,
    )
    picked_2, hot_2, pick_2 = fetch(1, tiles, pattern, selected, partial_value)

    rays, share = call(
        share_kernel, [RAYS, ((N_RAY, PRODUCTS + OWN, TILE), BF16)], "vvvvvv",
        (parts, ray_dual, traveltimes, pick, picked, rest.astype(BF16).reshape(OWN, TILE)),
    )
    shared = exchange(share, "ray")
    back, edge, partial_value = call(
        image_kernel, [((OWN, TILE), F32), ((2 * GX, TILE), F32), SUMS], "vvvv",
        (shared, gathered, picked_2, hot_2), (pltpu.VMEM((ALL, TILE), F32),),
    )
    parts = exchange(partial_value, "mp")

    field, image, far, near = call(
        second_edges_kernel, [grid, grid] + [((GY + 2 * GX, TILE), F32)] * 2, "vvvvv",
        (base, back, edge, accumulated, tv_back), busy=busy,
    )
    far, near = x_swaps(far, near)
    dual, tv_back = call(
        second_tv_kernel, [duals, grid], "vvvvvvv",
        (field, dual, dual_plane, dual_row, far, near, edge), busy=busy,
    )

    rays, share = call(
        back_kernel, [RAYS, ((N_RAY, OWN, TILE), BF16)], "vvvvvv",
        (parts, rays, traveltimes, pick_2, picked_2, hot_2),
    )
    back = jnp.sum(exchange(share, "ray").astype(F32), axis=0).reshape(GRID)
    image = image + back + tv_back
    image_bar = image + extrapolation * back + tv_back
    return (field, rays, dual, image, image_bar)


def solution(mesh):
    in_specs = (
        P("mp", "ray", None),
        P("mp", "ray", None),
        P("mp", "ray", None),
        P(None, "mp", "ray", None),
        P("ray", None),
        P("ray", None),
        P("ray", "mp", None, None),
        P("ray", "mp"),
        P(None, "ray"),
    )
    out_specs = (
        P("mp", "ray", None),
        P("ray", None),
        P(None, "mp", "ray", None),
        P("mp", "ray", None),
        P("mp", "ray", None),
    )
    return jax.shard_map(
        on_device, mesh=mesh, in_specs=in_specs, out_specs=out_specs, check_vma=False
    )
```

```python
import jax
import jax.numpy as jnp
from jax import lax
from jax.experimental import pallas as pl
from jax.experimental.pallas import tpu as pltpu
from jax.sharding import PartitionSpec as P

TILE = 128
GX = 4
GY = 8
RB_DEV = 16
CAP = 8
MAXSEL = 8
N_RAY = 16
N_MP = 32
OWN = GX * GY
ALL = N_RAY * OWN
PRODUCTS = MAXSEL * CAP
SENT = OWN + 16

primal_step = 0.5
dual_step = 0.5
tv_step = 0.25
tv_weight = 0.3
extrapolation = 2.0 * RB_DEV / (MAXSEL + 1)
gain = primal_step * (1.0 + extrapolation)

F32 = jnp.float32
BF16 = jnp.bfloat16
GRID = (GX, GY, TILE)
SUMS = ((N_MP, MAXSEL, TILE), F32)
RAYS = ((RB_DEV, TILE), F32)


def exchange(copies, axis):
    return lax.all_to_all(copies, axis, 0, 0, tiled=True)


def call(kernel, outs, places, args, scratch=(), busy=0, keep=False):
    spaces = {"v": pltpu.VMEM, "h": pltpu.HBM, "a": pl.ANY}
    cost = pl.CostEstimate(flops=0, bytes_accessed=busy, transcendentals=0) if busy else None
    args = [
        pltpu.with_memory_space_constraint(arg, pltpu.HBM) if place == "h" else arg
        for arg, place in zip(args, places)
    ]
    return pl.pallas_call(
        kernel,
        out_shape=[
            pltpu.VMEM(shape, dtype) if keep else jax.ShapeDtypeStruct(shape, dtype)
            for shape, dtype in outs
        ],
        in_specs=[pl.BlockSpec(memory_space=spaces[c]) for c in places],
        out_specs=[pl.BlockSpec(memory_space=pltpu.VMEM) for _ in outs],
        scratch_shapes=list(scratch),
        cost_estimate=cost,
        compiler_params=pltpu.CompilerParams(vmem_limit_bytes=20 * 1024 * 1024),
    )(*args)


SCALARS = (
    pltpu.SMEM((CAP, RB_DEV), jnp.int32),
    pltpu.SMEM((2, RB_DEV), jnp.int32),
    pltpu.SMEM((RB_DEV,), jnp.int32),
    pltpu.SemaphoreType.DMA((2,)),
)


def scalar_copies(pattern_hbm, selected_hbm, pattern_ref, selected_ref, sems):
    return [
        pltpu.make_async_copy(pattern_hbm, pattern_ref, sems.at[0]),
        pltpu.make_async_copy(selected_hbm, selected_ref, sems.at[1]),
    ]


def block_number(pattern):
    row = pattern & (GY * N_RAY - 1)
    plane = lax.shift_right_logical(pattern, 7)
    return lax.shift_right_logical(row, 3) * OWN + plane * GY + (row & (GY - 1))


def list_selected(selected_ref, step, list_ref):
    for n in range(MAXSEL):
        list_ref[n] = jnp.int32(0)
    count = jnp.int32(0)
    for r in range(RB_DEV):
        list_ref[count] = jnp.int32(r)
        count = count + selected_ref[step, r]
    return count


def start_kernel(
    slowness_hbm, bar_hbm, dual_hbm, pattern_hbm, selected_hbm, field_ref, sent_ref, up_ref, down_ref,
    slowness_ref, bar_ref, dual_ref, sems, pattern_ref, selected_ref, list_ref, scalar_sems,
):
    copies = scalar_copies(pattern_hbm, selected_hbm, pattern_ref, selected_ref, scalar_sems)
    copies.append(pltpu.make_async_copy(slowness_hbm, slowness_ref, sems.at[0]))
    copies.append(pltpu.make_async_copy(bar_hbm, bar_ref, sems.at[1]))
    copies.append(pltpu.make_async_copy(dual_hbm, dual_ref, sems.at[2]))
    for copy in copies:
        copy.start()
    copies[0].wait()
    copies[1].wait()
    list_selected(selected_ref, 0, list_ref)
    lane = lax.broadcasted_iota(jnp.int32, (16, TILE), 1) & (PRODUCTS - 1)
    sub = lax.broadcasted_iota(jnp.int32, (16, TILE), 0)
    numbers = jnp.zeros((16, TILE), jnp.int32)
    for n in range(MAXSEL):
        r = list_ref[n]
        for s in range(CAP):
            numbers = jnp.where(lane == n * CAP + s, block_number(pattern_ref[s, r]), numbers)
    numbers = jnp.where(sub == 0, lax.shift_right_logical(numbers, 5), numbers & (OWN - 1))
    numbers = numbers.astype(F32).astype(BF16)
    copies[2].wait()
    copies[3].wait()
    field = slowness_ref[...] - primal_step * bar_ref[...]
    field_ref[...] = field
    rounded = field.reshape(OWN, TILE).astype(BF16)
    for p in range(N_RAY):
        sent_ref[p, 0:OWN, :] = rounded
        sent_ref[p, OWN:SENT, :] = numbers
    up_ref[...] = jnp.zeros_like(up_ref)
    copies[4].wait()
    for x in range(GX):
        up_ref[x : x + 1] = field_ref[x, 0:1]
        down_ref[x : x + 1] = field_ref[x, GY - 1 : GY]
        for c in range(3):
            at = (c + 1) * GX + x
            down_ref[at : at + 1] = dual_ref[c, x, GY - 1 : GY]


def fetch_kernel(step):
    def kernel(
        tiles_hbm, pattern_hbm, selected_hbm, after_ref, picked_ref, hot_ref, pick_ref,
        pattern_ref, selected_ref, list_ref, scalar_sems, sems,
    ):
        for copy in scalar_copies(pattern_hbm, selected_hbm, pattern_ref, selected_ref, scalar_sems):
            copy.start()
            copy.wait()
        count = list_selected(selected_ref, step, list_ref)
        copies = [
            pltpu.make_async_copy(tiles_hbm.at[list_ref[n]], picked_ref.at[n], sems.at[n])
            for n in range(MAXSEL)
        ]
        for copy in copies:
            copy.start()
        sub = lax.broadcasted_iota(jnp.int32, (MAXSEL, TILE), 0)
        lane = lax.broadcasted_iota(jnp.int32, (2 * CAP, TILE), 1)
        for n in range(0, MAXSEL, 2):
            halves = []
            for m in (n, n + 1):
                r = list_ref[m]
                numbers = jnp.zeros((CAP, TILE), jnp.int32)
                for s in range(CAP):
                    numbers = jnp.where(sub == s, block_number(pattern_ref[s, r]), numbers)
                halves.append(numbers)
            numbers = jnp.concatenate(halves, axis=0)
            for c in range(ALL // TILE):
                hot = jnp.where(numbers == lane + c * TILE, 1.0, 0.0).astype(BF16)
                hot_ref[n * CAP : (n + 2) * CAP, c * TILE : (c + 1) * TILE] = hot
        listed = jnp.full((MAXSEL, TILE), RB_DEV, jnp.int32)
        for n in range(MAXSEL):
            listed = jnp.where((sub == n) & (sub < count), list_ref[n], listed)
        for r in range(RB_DEV):
            pick_ref[r] = jnp.where(listed == r, 1.0, 0.0)
        for copy in copies:
            copy.wait()

    return kernel


def fetch(step, tiles, pattern, selected, after):
    outs = [
        ((MAXSEL, CAP, TILE, TILE), BF16),
        ((PRODUCTS, ALL), BF16),
        ((RB_DEV, MAXSEL, TILE), F32),
    ]
    scratch = SCALARS + (pltpu.SemaphoreType.DMA((MAXSEL,)),)
    return call(
        fetch_kernel(step), outs, "hhha", (tiles, pattern, selected, after), scratch, 8 * 2**20, True
    )


def forward(hot_ref, blocks, picked_ref, out_ref):
    cells = jnp.dot(hot_ref[...], blocks, preferred_element_type=F32)
    sub = lax.broadcasted_iota(jnp.int32, (MAXSEL, TILE), 0)
    total = jnp.zeros((MAXSEL, TILE), F32)
    for n in range(MAXSEL):
        for s in range(CAP):
            row = cells[n * CAP + s : n * CAP + s + 1]
            lhs = jnp.where(sub == n, row, 0.0).astype(BF16)
            total = total + lax.dot_general(
                lhs, picked_ref[n, s], (((1,), (1,)), ((), ())), preferred_element_type=F32
            )
    for m in range(N_MP):
        out_ref[m] = total


def predict_kernel(gathered_ref, picked_ref, hot_ref, up_any, down_any, out_ref):
    blocks = jnp.concatenate([gathered_ref[p, 0:OWN, :] for p in range(N_RAY)], axis=0)
    forward(hot_ref, blocks, picked_ref, out_ref)


def dual_update(parts_ref, rays_ref, times_ref, pick_ref, new_rays_ref):
    predicted = parts_ref[0]
    for m in range(1, N_MP):
        predicted = predicted + parts_ref[m]
    rays = jnp.zeros((MAXSEL, TILE), F32)
    times = jnp.zeros((MAXSEL, TILE), F32)
    taken = jnp.zeros((MAXSEL, TILE), F32)
    for r in range(RB_DEV):
        pick = pick_ref[r]
        rays = rays + pick * rays_ref[r : r + 1, :]
        times = times + pick * times_ref[r : r + 1, :]
        taken = taken + pick
    fresh = (rays + dual_step * (predicted - times)) / (1.0 + dual_step)
    change = taken * (fresh - rays)
    for r in range(RB_DEV):
        new_rays_ref[r : r + 1, :] = rays_ref[r : r + 1, :] + jnp.sum(
            pick_ref[r] * change, axis=0, keepdims=True
        )
    return change


def products(change, picked_ref, n):
    sub = lax.broadcasted_iota(jnp.int32, (CAP, TILE), 0)
    row = change[n : n + 1]
    total = jnp.zeros((CAP, TILE), F32)
    for s in range(CAP):
        lhs = jnp.where(sub == s, row, 0.0).astype(BF16)
        total = total + jnp.dot(lhs, picked_ref[n, s], preferred_element_type=F32)
    return total


def share_kernel(
    parts_ref, rays_ref, times_ref, pick_ref, picked_ref, rest_ref, new_rays_ref, out_ref
):
    change = dual_update(parts_ref, rays_ref, times_ref, pick_ref, new_rays_ref)
    for n in range(0, MAXSEL, 2):
        pair = jnp.concatenate(
            [products(change, picked_ref, n), products(change, picked_ref, n + 1)], axis=0
        ).astype(BF16)
        for p in range(N_RAY):
            out_ref[p, n * CAP : (n + 2) * CAP, :] = pair
    rest = rest_ref[...]
    for p in range(N_RAY):
        out_ref[p, PRODUCTS : PRODUCTS + OWN, :] = rest


def image_kernel(
    shared_ref, gathered_ref, picked_ref, hot_ref, back_ref, edge_ref, out_ref, table_ref
):
    lane = lax.broadcasted_iota(jnp.int32, (1, TILE), 1)
    singles = []
    for p in range(N_RAY):
        rows = gathered_ref[p, OWN:SENT, :].astype(F32)
        singles.append(rows[0:1] * OWN + rows[1:2])
    pairs = [jnp.where(lane < PRODUCTS, singles[p], singles[p + 1]) for p in range(0, N_RAY, 2)]
    group = 4
    chunk = group * OWN
    numbers = []
    terms = []
    for g in range(0, N_RAY, group):
        numbers.append(jnp.concatenate(pairs[g // 2 : g // 2 + 2], axis=1).astype(jnp.int32))
        terms.append(
            jnp.concatenate([shared_ref[p, 0:PRODUCTS, :] for p in range(g, g + group)], axis=0)
        )
    place = lax.broadcasted_iota(jnp.int32, (chunk, group * PRODUCTS), 0)
    blocks = []
    for g in range(0, N_RAY, group):
        back = jnp.zeros((chunk, TILE), F32)
        for k in range(N_RAY // group):
            hot = jnp.where(place + g * OWN == numbers[k], 1.0, 0.0).astype(BF16)
            back = back + jnp.dot(hot, terms[k], preferred_element_type=F32)
        table_ref[g * OWN : g * OWN + chunk, :] = back
        before = jnp.concatenate([gathered_ref[p, 0:OWN, :] for p in range(g, g + group)], axis=0)
        rest = jnp.concatenate(
            [shared_ref[p, PRODUCTS : PRODUCTS + OWN, :] for p in range(g, g + group)], axis=0
        )
        blocks.append((before.astype(F32) + (rest.astype(F32) - gain * back)).astype(BF16))
    forward(hot_ref, jnp.concatenate(blocks, axis=0), picked_ref, out_ref)
    me = lax.axis_index("ray")
    back_ref[...] = table_ref[pl.ds(pl.multiple_of(me * OWN, OWN), OWN), :]
    for at, peer, row in ((0, jnp.maximum(me - 1, 0), GY - 1), (1, jnp.minimum(me + 1, N_RAY - 1), 0)):
        before = gathered_ref[peer, 0:OWN, :].astype(F32)
        rest = shared_ref[peer, PRODUCTS : PRODUCTS + OWN, :].astype(F32)
        back = table_ref[pl.ds(pl.multiple_of(peer * OWN, OWN), OWN), :]
        field = before + (rest - gain * back)
        for x in range(GX):
            edge_ref[at * GX + x : at * GX + x + 1, :] = field[x * GY + row : x * GY + row + 1]


def back_kernel(
    parts_ref, rays_ref, times_ref, pick_ref, picked_ref, hot_ref, far_any, near_any, new_rays_ref, out_ref
):
    change = dual_update(parts_ref, rays_ref, times_ref, pick_ref, new_rays_ref)
    terms = jnp.concatenate([products(change, picked_ref, n) for n in range(MAXSEL)], axis=0)
    high = terms.astype(BF16)
    low = (terms - high.astype(F32)).astype(BF16)
    turned = (((0,), (0,)), ((), ()))
    image = lax.dot_general(hot_ref[...], high, turned, preferred_element_type=F32)
    image = image + lax.dot_general(hot_ref[...], low, turned, preferred_element_type=F32)
    for p in range(N_RAY):
        out_ref[p] = image[p * OWN : (p + 1) * OWN].astype(BF16)


def x_swaps(far, near):
    far_route = [(m, m + 1) for m in range(1, N_MP - 1, 2)]
    near_route = [(m, m + 1) for m in range(0, N_MP - 1, 2)]
    far = lax.ppermute(far, "mp", far_route + [(b, a) for a, b in far_route])
    near = lax.ppermute(near, "mp", near_route + [(b, a) for a, b in near_route])
    return far, near


def first_edges_kernel(field_ref, dual_ref, up_ref, down_ref, after_any, far_ref, near_ref):
    odd = (lax.axis_index("mp") & 1) == 1
    first = jnp.concatenate([field_ref[0], jnp.broadcast_to(down_ref[0:1], (8, TILE))], axis=0)
    last = jnp.concatenate(
        [field_ref[GX - 1], jnp.broadcast_to(up_ref[GX - 1 : GX], (8, TILE))], axis=0
    )
    far_ref[0 : 2 * GY] = jnp.where(odd, last, first)
    near_ref[0 : 2 * GY] = jnp.where(odd, first, last)
    for c in range(3):
        rows = slice((c + 2) * GY, (c + 3) * GY)
        far_ref[rows] = dual_ref[c, GX - 1]
        near_ref[rows] = dual_ref[c, GX - 1]


def x_halos(far_ref, near_ref):
    odd = (lax.axis_index("mp") & 1) == 1
    far, near = far_ref[...], near_ref[...]
    return jnp.where(odd, near, far), jnp.where(odd, far, near)


def tv_cells(here, ahead_x, ahead_y, dual, no_x, no_y):
    lane = lax.broadcasted_iota(jnp.int32, here.shape, len(here.shape) - 1)
    ahead_z = pltpu.roll(here, TILE - 1, len(here.shape) - 1)
    steps = (
        jnp.where(no_x, 0.0, ahead_x - here),
        jnp.where(no_y, 0.0, ahead_y - here),
        jnp.where(lane == TILE - 1, 0.0, ahead_z - here),
    )
    moved = [d + tv_step * g for d, g in zip(dual, steps)]
    length = jnp.sqrt(moved[0] * moved[0] + moved[1] * moved[1] + moved[2] * moved[2])
    scale = jnp.maximum(1.0, length / tv_weight)
    fresh = [m / scale for m in moved]
    return fresh, [a - b for a, b in zip(fresh, dual)]


def up_one(plane, row):
    sub = lax.broadcasted_iota(jnp.int32, plane.shape, 0)
    return jnp.where(sub == GY - 1, row, pltpu.roll(plane, GY - 1, 0))


def tv_step_all(field, dual, before, before_next, dual_before, behind, corner, rows, dual_rows, next_rows):
    mp, ray = lax.axis_index("mp"), lax.axis_index("ray")
    sub = lax.broadcasted_iota(jnp.int32, (GY, TILE), 0)
    end_x = mp == N_MP - 1
    last_y = (sub == GY - 1) & (ray == N_RAY - 1)
    never = sub < 0
    lane = lax.broadcasted_iota(jnp.int32, (GY, TILE), 1)

    halo, halo_change = tv_cells(
        before, field[0], up_one(before, before_next), dual_before, never, last_y
    )
    from_x = jnp.where(mp == 0, 0.0, halo_change[0])
    fresh, backs, halo_rows = [], [], []
    for x in range(GX):
        ahead = field[x + 1] if x + 1 < GX else behind
        no_x = (end_x & (sub >= 0)) if x + 1 == GX else never
        new, change = tv_cells(
            field[x], ahead, up_one(field[x], next_rows[x]), [d[x] for d in dual], no_x, last_y
        )
        ahead_row = rows[x + 1] if x + 1 < GX else corner
        no_row = (end_x & (sub[0:1] >= 0)) if x + 1 == GX else never[0:1]
        new_row, row_change = tv_cells(
            rows[x], ahead_row, field[x][0:1], [d[x] for d in dual_rows], no_row, never[0:1]
        )
        from_y = jnp.where(ray == 0, 0.0, row_change[1])
        comp_x = jnp.where(no_x, 0.0, change[0])
        comp_y = jnp.where(last_y, 0.0, change[1])
        comp_z = jnp.where(lane == TILE - 1, 0.0, change[2])
        back = from_x - comp_x
        back = back + (jnp.where(sub == 0, from_y, pltpu.roll(comp_y, 1, 0)) - comp_y)
        back = back + (jnp.where(lane == 0, 0.0, pltpu.roll(comp_z, 1, 1)) - comp_z)
        from_x = comp_x
        fresh.append(new)
        backs.append(back)
        halo_rows.append(new_row)
    return fresh, backs, halo, halo_rows


def first_tv_kernel(
    field_ref, dual_ref, far_ref, near_ref, up_ref, down_ref, image_ref,
    new_dual_ref, plane_ref, row_ref, back_ref, base_ref, rest_ref,
):
    before, behind = x_halos(far_ref, near_ref)
    field = [field_ref[x] for x in range(GX)]
    dual = [[dual_ref[c, x] for x in range(GX)] for c in range(3)]
    up, down = up_ref[...], down_ref[...]
    rows = [down[x : x + 1] for x in range(GX)]
    dual_rows = [
        [down[(c + 1) * GX + x : (c + 1) * GX + x + 1] for x in range(GX)] for c in range(3)
    ]
    fresh, backs, halo, halo_rows = tv_step_all(
        field, dual, before[0:GY], before[GY : GY + 1],
        [before[(c + 2) * GY : (c + 3) * GY] for c in range(3)],
        behind[0:GY], behind[GY : GY + 1], rows, dual_rows, [up[x : x + 1] for x in range(GX)],
    )
    for x in range(GX):
        base = field[x] - primal_step * (image_ref[x] + 2.0 * backs[x])
        back_ref[x] = backs[x]
        base_ref[x] = base
        rest_ref[x] = base - field[x].astype(BF16).astype(F32)
        for c in range(3):
            new_dual_ref[c, x] = fresh[x][c]
            row_ref[c * GX + x : c * GX + x + 1] = halo_rows[x][c]
    for c in range(3):
        plane_ref[c] = halo[c]


def second_edges_kernel(base_ref, back_ref, edge_ref, image_ref, tv_ref, field_ref, new_image_ref, far_ref, near_ref):
    odd = (lax.axis_index("mp") & 1) == 1
    field = []
    for x in range(GX):
        back = back_ref[x * GY : (x + 1) * GY]
        field.append(base_ref[x] - gain * back)
        field_ref[x] = field[x]
        new_image_ref[x] = image_ref[x] + back + tv_ref[x]
    first = jnp.concatenate([field[0], edge_ref[...]], axis=0)
    last = jnp.concatenate([field[GX - 1], edge_ref[...]], axis=0)
    far_ref[...] = jnp.where(odd, last, first)
    near_ref[...] = jnp.where(odd, first, last)


def second_tv_kernel(
    field_ref, dual_ref, plane_ref, row_ref, far_ref, near_ref, edge_ref, new_dual_ref, back_ref
):
    before, behind = x_halos(far_ref, near_ref)
    edge = edge_ref[...]
    fresh, backs, _, _ = tv_step_all(
        [field_ref[x] for x in range(GX)],
        [[dual_ref[c, x] for x in range(GX)] for c in range(3)],
        before[0:GY], before[GY + 2 * GX - 1 : GY + 2 * GX],
        [plane_ref[c] for c in range(3)],
        behind[0:GY], behind[GY : GY + 1],
        [edge[x : x + 1] for x in range(GX)],
        [[row_ref[c * GX + x : c * GX + x + 1] for x in range(GX)] for c in range(3)],
        [edge[GX + x : GX + x + 1] for x in range(GX)],
    )
    for x in range(GX):
        back_ref[x] = backs[x]
        for c in range(3):
            new_dual_ref[c, x] = fresh[x][c]


def on_device(
    slowness, accumulated, extrapolated, tv_dual, ray_dual, traveltimes, tiles, pattern, selected
):
    pattern = pattern.T
    busy = 8 * 2**20
    grid = (GRID, F32)
    duals = ((3,) + GRID, F32)

    field, sent, up, down = call(
        start_kernel,
        [grid, ((N_RAY, SENT, TILE), BF16), ((8, TILE), F32), ((4 * GX, TILE), F32)], "hhhhh",
        (slowness, extrapolated, tv_dual, pattern, selected),
        (
            pltpu.VMEM(GRID, F32), pltpu.VMEM(GRID, F32), pltpu.VMEM((3,) + GRID, F32),
            pltpu.SemaphoreType.DMA((3,)),
        ) + SCALARS,
    )
    gathered = exchange(sent, "ray")
    up = lax.ppermute(up, "ray", [(i + 1, i) for i in range(N_RAY - 1)])
    down = lax.ppermute(down, "ray", [(i, i + 1) for i in range(N_RAY - 1)])
    picked, hot, pick = fetch(0, tiles, pattern, selected, field)
    (partial_value,) = call(
        predict_kernel, [SUMS], "vvvaa", (gathered, picked, hot, up, down)
    )
    parts = exchange(partial_value, "mp")

    far, near = call(
        first_edges_kernel, [((5 * GY, TILE), F32)] * 2, "vvvva",
        (field, tv_dual, up, down, partial_value), busy=busy,
    )
    far, near = x_swaps(far, near)
    dual, dual_plane, dual_row, tv_back, base, rest = call(
        first_tv_kernel,
        [duals, ((3, GY, TILE), F32), ((3 * GX, TILE), F32), grid, grid, grid],
        "vvvvvvv", (field, tv_dual, far, near, up, down, accumulated), busy=busy,
    )
    picked_2, hot_2, pick_2 = fetch(1, tiles, pattern, selected, partial_value)

    rays, share = call(
        share_kernel, [RAYS, ((N_RAY, PRODUCTS + OWN, TILE), BF16)], "vvvvvv",
        (parts, ray_dual, traveltimes, pick, picked, rest.astype(BF16).reshape(OWN, TILE)),
    )
    shared = exchange(share, "ray")
    back, edge, partial_value = call(
        image_kernel, [((OWN, TILE), F32), ((2 * GX, TILE), F32), SUMS], "vvvv",
        (shared, gathered, picked_2, hot_2), (pltpu.VMEM((ALL, TILE), F32),),
    )
    parts = exchange(partial_value, "mp")

    field, image, far, near = call(
        second_edges_kernel, [grid, grid] + [((GY + 2 * GX, TILE), F32)] * 2, "vvvvv",
        (base, back, edge, accumulated, tv_back), busy=busy,
    )
    far, near = x_swaps(far, near)
    dual, tv_back = call(
        second_tv_kernel, [duals, grid], "vvvvvvv",
        (field, dual, dual_plane, dual_row, far, near, edge), busy=busy,
    )

    rays, share = call(
        back_kernel, [RAYS, ((N_RAY, OWN, TILE), BF16)], "vvvvvvaa",
        (parts, rays, traveltimes, pick_2, picked_2, hot_2, far, near),
    )
    back = jnp.sum(exchange(share, "ray").astype(F32), axis=0).reshape(GRID)
    image = image + back + tv_back
    image_bar = image + extrapolation * back + tv_back
    return (field, rays, dual, image, image_bar)


def solution(mesh):
    in_specs = (
        P("mp", "ray", None),
        P("mp", "ray", None),
        P("mp", "ray", None),
        P(None, "mp", "ray", None),
        P("ray", None),
        P("ray", None),
        P("ray", "mp", None, None),
        P("ray", "mp"),
        P(None, "ray"),
    )
    out_specs = (
        P("mp", "ray", None),
        P("ray", None),
        P(None, "mp", "ray", None),
        P("mp", "ray", None),
        P("mp", "ray", None),
    )
    return jax.shard_map(
        on_device, mesh=mesh, in_specs=in_specs, out_specs=out_specs, check_vma=False
    )
```

```python
import jax
import jax.numpy as jnp
from jax import lax
from jax.experimental import pallas as pl
from jax.experimental.pallas import tpu as pltpu
from jax.sharding import PartitionSpec as P

TILE = 128
GX = 4
GY = 8
RB_DEV = 16
CAP = 8
MAXSEL = 8
N_RAY = 16
N_MP = 32
OWN = GX * GY
ALL = N_RAY * OWN
PRODUCTS = MAXSEL * CAP
SENT = OWN + 16
REST = OWN + 8
EXTRA = PRODUCTS + OWN
SHARED = EXTRA + 16

primal_step = 0.5
dual_step = 0.5
tv_step = 0.25
tv_weight = 0.3
extrapolation = 2.0 * RB_DEV / (MAXSEL + 1)
gain = primal_step * (1.0 + extrapolation)

F32 = jnp.float32
BF16 = jnp.bfloat16
GRID = (GX, GY, TILE)
SUMS = ((N_MP, MAXSEL, TILE), F32)
RAYS = ((RB_DEV, TILE), F32)


def exchange(copies, axis):
    return lax.all_to_all(copies, axis, 0, 0, tiled=True)


def call(kernel, outs, places, args, scratch=(), busy=0, keep=False):
    spaces = {"v": pltpu.VMEM, "h": pltpu.HBM, "a": pl.ANY}
    cost = pl.CostEstimate(flops=0, bytes_accessed=busy, transcendentals=0) if busy else None
    args = [
        pltpu.with_memory_space_constraint(arg, pltpu.HBM) if place == "h" else arg
        for arg, place in zip(args, places)
    ]
    return pl.pallas_call(
        kernel,
        out_shape=[
            pltpu.VMEM(shape, dtype) if keep else jax.ShapeDtypeStruct(shape, dtype)
            for shape, dtype in outs
        ],
        in_specs=[pl.BlockSpec(memory_space=spaces[c]) for c in places],
        out_specs=[pl.BlockSpec(memory_space=pltpu.VMEM) for _ in outs],
        scratch_shapes=list(scratch),
        cost_estimate=cost,
        compiler_params=pltpu.CompilerParams(vmem_limit_bytes=20 * 1024 * 1024),
    )(*args)


SCALARS = (
    pltpu.SMEM((CAP, RB_DEV), jnp.int32),
    pltpu.SMEM((2, RB_DEV), jnp.int32),
    pltpu.SMEM((RB_DEV,), jnp.int32),
    pltpu.SemaphoreType.DMA((2,)),
)


def scalar_copies(pattern_hbm, selected_hbm, pattern_ref, selected_ref, sems):
    return [
        pltpu.make_async_copy(pattern_hbm, pattern_ref, sems.at[0]),
        pltpu.make_async_copy(selected_hbm, selected_ref, sems.at[1]),
    ]


def block_number(pattern):
    row = pattern & (GY * N_RAY - 1)
    plane = lax.shift_right_logical(pattern, 7)
    return lax.shift_right_logical(row, 3) * OWN + plane * GY + (row & (GY - 1))


def list_selected(selected_ref, step, list_ref):
    for n in range(MAXSEL):
        list_ref[n] = jnp.int32(0)
    count = jnp.int32(0)
    for r in range(RB_DEV):
        list_ref[count] = jnp.int32(r)
        count = count + selected_ref[step, r]
    return count


def start_kernel(
    slowness_hbm, bar_hbm, pattern_hbm, selected_hbm, field_ref, sent_ref,
    slowness_ref, bar_ref, sems, pattern_ref, selected_ref, list_ref, scalar_sems,
):
    copies = scalar_copies(pattern_hbm, selected_hbm, pattern_ref, selected_ref, scalar_sems)
    copies.append(pltpu.make_async_copy(slowness_hbm, slowness_ref, sems.at[0]))
    copies.append(pltpu.make_async_copy(bar_hbm, bar_ref, sems.at[1]))
    for copy in copies:
        copy.start()
    copies[0].wait()
    copies[1].wait()
    list_selected(selected_ref, 0, list_ref)
    lane = lax.broadcasted_iota(jnp.int32, (8, TILE), 1) & (PRODUCTS - 1)
    sub = lax.broadcasted_iota(jnp.int32, (8, TILE), 0)
    numbers = jnp.zeros((8, TILE), jnp.int32)
    for n in range(MAXSEL):
        r = list_ref[n]
        for s in range(CAP):
            numbers = jnp.where(lane == n * CAP + s, block_number(pattern_ref[s, r]), numbers)
    numbers = jnp.where(sub == 0, lax.shift_right_logical(numbers, 5), numbers & (OWN - 1))
    copies[2].wait()
    copies[3].wait()
    field = slowness_ref[...] - primal_step * bar_ref[...]
    field_ref[...] = field
    field = field.reshape(OWN, TILE)
    rounded = field.astype(BF16)
    low = field - rounded.astype(F32)
    rest = jnp.zeros((8, TILE), F32)
    for x in range(GX):
        rest = jnp.where(sub == x, low[x * GY : x * GY + 1], rest)
    tail = jnp.concatenate([numbers.astype(F32), rest], axis=0).astype(BF16)
    for p in range(N_RAY):
        sent_ref[p, 0:OWN, :] = rounded
        sent_ref[p, OWN:SENT, :] = tail


def fetch_kernel(step):
    def kernel(
        tiles_hbm, pattern_hbm, selected_hbm, after_ref, picked_ref, hot_ref, pick_ref,
        pattern_ref, selected_ref, list_ref, scalar_sems, sems,
    ):
        scalars = scalar_copies(pattern_hbm, selected_hbm, pattern_ref, selected_ref, scalar_sems)
        for copy in scalars:
            copy.start()
        for copy in scalars:
            copy.wait()
        count = list_selected(selected_ref, step, list_ref)
        copies = [
            pltpu.make_async_copy(tiles_hbm.at[list_ref[n]], picked_ref.at[n], sems.at[n])
            for n in range(MAXSEL)
        ]
        for copy in copies:
            copy.start()
        sub = lax.broadcasted_iota(jnp.int32, (MAXSEL, TILE), 0)
        lane = lax.broadcasted_iota(jnp.int32, (2 * CAP, TILE), 1)
        for n in range(0, MAXSEL, 2):
            halves = []
            for m in (n, n + 1):
                r = list_ref[m]
                numbers = jnp.zeros((CAP, TILE), jnp.int32)
                for s in range(CAP):
                    numbers = jnp.where(sub == s, block_number(pattern_ref[s, r]), numbers)
                halves.append(numbers)
            numbers = jnp.concatenate(halves, axis=0)
            for c in range(ALL // TILE):
                hot = jnp.where(numbers == lane + c * TILE, 1.0, 0.0).astype(BF16)
                hot_ref[n * CAP : (n + 2) * CAP, c * TILE : (c + 1) * TILE] = hot
        listed = jnp.full((MAXSEL, TILE), RB_DEV, jnp.int32)
        for n in range(MAXSEL):
            listed = jnp.where((sub == n) & (sub < count), list_ref[n], listed)
        for r in range(RB_DEV):
            pick_ref[r] = jnp.where(listed == r, 1.0, 0.0)
        for copy in copies:
            copy.wait()

    return kernel


def fetch(step, tiles, pattern, selected, after):
    outs = [
        ((MAXSEL, CAP, TILE, TILE), BF16),
        ((PRODUCTS, ALL), BF16),
        ((RB_DEV, MAXSEL, TILE), F32),
    ]
    scratch = SCALARS + (pltpu.SemaphoreType.DMA((MAXSEL,)),)
    return call(
        fetch_kernel(step), outs, "hhha", (tiles, pattern, selected, after), scratch, 8 * 2**20, True
    )


def forward(hot_ref, blocks, picked_ref, out_ref):
    cells = jnp.dot(hot_ref[...], blocks, preferred_element_type=F32)
    sub = lax.broadcasted_iota(jnp.int32, (MAXSEL, TILE), 0)
    total = jnp.zeros((MAXSEL, TILE), F32)
    for n in range(MAXSEL):
        for s in range(CAP):
            row = cells[n * CAP + s : n * CAP + s + 1]
            lhs = jnp.where(sub == n, row, 0.0).astype(BF16)
            total = total + lax.dot_general(
                lhs, picked_ref[n, s], (((1,), (1,)), ((), ())), preferred_element_type=F32
            )
    for m in range(N_MP):
        out_ref[m] = total


def predict_kernel(gathered_ref, picked_ref, hot_ref, out_ref):
    blocks = jnp.concatenate([gathered_ref[p, 0:OWN, :] for p in range(N_RAY)], axis=0)
    forward(hot_ref, blocks, picked_ref, out_ref)


def dual_update(parts_ref, rays_ref, times_ref, pick_ref, new_rays_ref):
    predicted = parts_ref[0]
    for m in range(1, N_MP):
        predicted = predicted + parts_ref[m]
    rays = jnp.zeros((MAXSEL, TILE), F32)
    times = jnp.zeros((MAXSEL, TILE), F32)
    taken = jnp.zeros((MAXSEL, TILE), F32)
    for r in range(RB_DEV):
        pick = pick_ref[r]
        rays = rays + pick * rays_ref[r : r + 1, :]
        times = times + pick * times_ref[r : r + 1, :]
        taken = taken + pick
    fresh = (rays + dual_step * (predicted - times)) / (1.0 + dual_step)
    change = taken * (fresh - rays)
    for r in range(RB_DEV):
        new_rays_ref[r : r + 1, :] = rays_ref[r : r + 1, :] + jnp.sum(
            pick_ref[r] * change, axis=0, keepdims=True
        )
    return change


def products(change, picked_ref, n):
    sub = lax.broadcasted_iota(jnp.int32, (CAP, TILE), 0)
    row = change[n : n + 1]
    total = jnp.zeros((CAP, TILE), F32)
    for s in range(CAP):
        lhs = jnp.where(sub == s, row, 0.0).astype(BF16)
        total = total + jnp.dot(lhs, picked_ref[n, s], preferred_element_type=F32)
    return total


def share_kernel(
    parts_ref, rays_ref, times_ref, pick_ref, picked_ref, rest_ref, extra_ref, new_rays_ref, out_ref
):
    change = dual_update(parts_ref, rays_ref, times_ref, pick_ref, new_rays_ref)
    for n in range(0, MAXSEL, 2):
        pair = jnp.concatenate(
            [products(change, picked_ref, n), products(change, picked_ref, n + 1)], axis=0
        ).astype(BF16)
        for p in range(N_RAY):
            out_ref[p, n * CAP : (n + 2) * CAP, :] = pair
    rest = rest_ref[...].reshape(OWN, TILE).astype(BF16)
    extra = extra_ref[...].astype(BF16)
    for p in range(N_RAY):
        out_ref[p, PRODUCTS:EXTRA, :] = rest
        out_ref[p, EXTRA:SHARED, :] = extra


def image_kernel(
    shared_ref, gathered_ref, picked_ref, hot_ref, back_ref, edge_ref, out_ref, table_ref
):
    lane = lax.broadcasted_iota(jnp.int32, (1, TILE), 1)
    singles = []
    for p in range(N_RAY):
        rows = gathered_ref[p, OWN:SENT, :].astype(F32)
        singles.append(rows[0:1] * OWN + rows[1:2])
    pairs = [jnp.where(lane < PRODUCTS, singles[p], singles[p + 1]) for p in range(0, N_RAY, 2)]
    group = 4
    chunk = group * OWN
    numbers = []
    terms = []
    for g in range(0, N_RAY, group):
        numbers.append(jnp.concatenate(pairs[g // 2 : g // 2 + 2], axis=1).astype(jnp.int32))
        terms.append(
            jnp.concatenate([shared_ref[p, 0:PRODUCTS, :] for p in range(g, g + group)], axis=0)
        )
    place = lax.broadcasted_iota(jnp.int32, (chunk, group * PRODUCTS), 0)
    sub = lax.broadcasted_iota(jnp.int32, (GY, TILE), 0)
    blocks = []
    for g in range(0, N_RAY, group):
        back = jnp.zeros((chunk, TILE), F32)
        for k in range(N_RAY // group):
            hot = jnp.where(place + g * OWN == numbers[k], 1.0, 0.0).astype(BF16)
            back = back + jnp.dot(hot, terms[k], preferred_element_type=F32)
        table_ref[g * OWN : g * OWN + chunk, :] = back
        for p in range(g, g + group):
            rows = slice(p * OWN, (p + 1) * OWN)
            rest = shared_ref[p, PRODUCTS:EXTRA, :].astype(F32)
            field = gathered_ref[p, 0:OWN, :].astype(F32) + (rest - gain * table_ref[rows, :])
            if p > 0:
                change = shared_ref[p - 1, EXTRA:SHARED, :].astype(F32)
                field = field - (2.0 * primal_step) * jnp.concatenate(
                    [jnp.where(sub == 0, change[x : x + 1], 0.0) for x in range(GX)], axis=0
                )
            blocks.append(field)
    forward(
        hot_ref, jnp.concatenate([field.astype(BF16) for field in blocks], axis=0), picked_ref, out_ref
    )
    me = lax.axis_index("ray")
    back_ref[...] = table_ref[pl.ds(pl.multiple_of(me * OWN, OWN), OWN), :]
    for p in range(N_RAY):
        table_ref[p * OWN : (p + 1) * OWN, :] = blocks[p]
    before = jnp.maximum(me - 1, 0)
    for at, peer, row in ((0, before, GY - 1), (1, jnp.minimum(me + 1, N_RAY - 1), 0)):
        field = table_ref[pl.ds(pl.multiple_of(peer * OWN, OWN), OWN), :]
        for x in range(GX):
            edge_ref[at * GX + x : at * GX + x + 1, :] = field[x * GY + row : x * GY + row + 1]
    edge_ref[2 * GX : 6 * GX] = shared_ref[before, EXTRA:SHARED, :].astype(F32)


def back_kernel(
    parts_ref, rays_ref, times_ref, pick_ref, picked_ref, hot_ref, far_any, near_ref, new_rays_ref, out_ref, same_ref
):
    same_ref[...] = near_ref[...]
    change = dual_update(parts_ref, rays_ref, times_ref, pick_ref, new_rays_ref)
    terms = jnp.concatenate([products(change, picked_ref, n) for n in range(MAXSEL)], axis=0)
    high = terms.astype(BF16)
    low = (terms - high.astype(F32)).astype(BF16)
    turned = (((0,), (0,)), ((), ()))
    image = lax.dot_general(hot_ref[...], high, turned, preferred_element_type=F32)
    image = image + lax.dot_general(hot_ref[...], low, turned, preferred_element_type=F32)
    for p in range(N_RAY):
        out_ref[p] = image[p * OWN : (p + 1) * OWN].astype(BF16)


def swap(block, first):
    route = [(m, m + 1) for m in range(first, N_MP - 1, 2)]
    return lax.ppermute(block, "mp", route + [(b, a) for a, b in route])


def swap_far(block):
    return swap(block, 1)


def swap_near(block):
    return swap(block, 0)


def next_rows(gathered_ref):
    peer = jnp.minimum(lax.axis_index("ray") + 1, N_RAY - 1)
    high = gathered_ref[peer, 0:OWN, :].astype(F32)
    low = gathered_ref[peer, OWN:SENT, :].astype(F32)
    return [
        high[x * GY : x * GY + 1] + low[REST - OWN + x : REST - OWN + x + 1] for x in range(GX)
    ]


def first_edges_kernel(field_ref, dual_ref, gathered_ref, after_any, far_ref, near_ref):
    odd = (lax.axis_index("mp") & 1) == 1
    first = field_ref[0]
    last = field_ref[GX - 1]
    far_ref[0:GY] = jnp.where(odd, last, first)
    near_ref[0:GY] = jnp.where(odd, first, last)
    corner = jnp.broadcast_to(next_rows(gathered_ref)[GX - 1], (GY, TILE))
    far_ref[GY : 2 * GY] = corner
    near_ref[GY : 2 * GY] = corner
    for c in range(3):
        rows = slice((c + 2) * GY, (c + 3) * GY)
        far_ref[rows] = dual_ref[c, GX - 1]
        near_ref[rows] = dual_ref[c, GX - 1]


def x_halos(far_ref, near_ref):
    odd = (lax.axis_index("mp") & 1) == 1
    far, near = far_ref[...], near_ref[...]
    return jnp.where(odd, near, far), jnp.where(odd, far, near)


def tv_cells(here, ahead_x, ahead_y, dual, no_x, no_y):
    lane = lax.broadcasted_iota(jnp.int32, here.shape, len(here.shape) - 1)
    ahead_z = pltpu.roll(here, TILE - 1, len(here.shape) - 1)
    steps = (
        jnp.where(no_x, 0.0, ahead_x - here),
        jnp.where(no_y, 0.0, ahead_y - here),
        jnp.where(lane == TILE - 1, 0.0, ahead_z - here),
    )
    moved = [d + tv_step * g for d, g in zip(dual, steps)]
    length = jnp.sqrt(moved[0] * moved[0] + moved[1] * moved[1] + moved[2] * moved[2])
    scale = jnp.maximum(1.0, length / tv_weight)
    fresh = [m / scale for m in moved]
    return fresh, [a - b for a, b in zip(fresh, dual)]


def up_one(plane, row):
    sub = lax.broadcasted_iota(jnp.int32, plane.shape, 0)
    return jnp.where(sub == GY - 1, row, pltpu.roll(plane, GY - 1, 0))


def tv_step_all(field, dual, before, before_next, dual_before, behind, nexts, from_y):
    mp, ray = lax.axis_index("mp"), lax.axis_index("ray")
    sub = lax.broadcasted_iota(jnp.int32, (GY, TILE), 0)
    lane = lax.broadcasted_iota(jnp.int32, (GY, TILE), 1)
    end_x = (mp == N_MP - 1) & (sub >= 0)
    last_y = (sub == GY - 1) & (ray == N_RAY - 1)
    never = sub < 0

    halo, halo_change = tv_cells(
        before, field[0], up_one(before, before_next), dual_before, never, last_y
    )
    from_x = jnp.where(mp == 0, 0.0, halo_change[0])
    fresh, backs, second = [], [], []
    for x in range(GX):
        ahead = field[x + 1] if x + 1 < GX else behind
        no_x = end_x if x + 1 == GX else never
        new, change = tv_cells(
            field[x], ahead, up_one(field[x], nexts[x]), [d[x] for d in dual], no_x, last_y
        )
        comp_x = jnp.where(no_x, 0.0, change[0])
        comp_y = jnp.where(last_y, 0.0, change[1])
        comp_z = jnp.where(lane == TILE - 1, 0.0, change[2])
        back = from_x - comp_x
        back = back + (jnp.where(sub == 0, from_y[x], pltpu.roll(comp_y, 1, 0)) - comp_y)
        back = back + (jnp.where(lane == 0, 0.0, pltpu.roll(comp_z, 1, 1)) - comp_z)
        from_x = comp_x
        fresh.append(new)
        backs.append(back)
        second.append(comp_y)
    return fresh, backs, halo, second


def first_tv_kernel(
    field_ref, dual_ref, far_ref, near_ref, gathered_ref, image_ref,
    new_dual_ref, plane_ref, back_ref, base_ref, rest_ref, extra_ref,
):
    before, behind = x_halos(far_ref, near_ref)
    field = [field_ref[x] for x in range(GX)]
    fresh, backs, halo, second = tv_step_all(
        field,
        [[dual_ref[c, x] for x in range(GX)] for c in range(3)],
        before[0:GY], before[GY : GY + 1],
        [before[(c + 2) * GY : (c + 3) * GY] for c in range(3)],
        behind[0:GY], next_rows(gathered_ref), [0.0] * GX,
    )
    for x in range(GX):
        base = field[x] - primal_step * (image_ref[x] + 2.0 * backs[x])
        back_ref[x] = backs[x]
        base_ref[x] = base
        rest_ref[x] = base - field[x].astype(BF16).astype(F32)
        extra_ref[x : x + 1] = second[x][GY - 1 : GY]
        for c in range(3):
            new_dual_ref[c, x] = fresh[x][c]
            at = (c + 1) * GX + x
            extra_ref[at : at + 1] = fresh[x][c][GY - 1 : GY]
    for c in range(3):
        plane_ref[c] = halo[c]


def second_edges_kernel(
    base_ref, back_ref, edge_ref, image_ref, tv_ref, field_ref, new_image_ref, far_ref, near_ref
):
    odd = (lax.axis_index("mp") & 1) == 1
    sub = lax.broadcasted_iota(jnp.int32, (GY, TILE), 0)
    first_y = (sub == 0) & (lax.axis_index("ray") > 0)
    field = []
    for x in range(GX):
        back = back_ref[x * GY : (x + 1) * GY]
        from_y = jnp.where(first_y, edge_ref[2 * GX + x : 2 * GX + x + 1], 0.0)
        field.append(base_ref[x] - (gain * back + (2.0 * primal_step) * from_y))
        field_ref[x] = field[x]
        new_image_ref[x] = image_ref[x] + back + (tv_ref[x] + from_y)
    edge = edge_ref[0 : 2 * GX]
    first = jnp.concatenate([field[0], edge], axis=0)
    last = jnp.concatenate([field[GX - 1], edge], axis=0)
    far_ref[...] = jnp.where(odd, last, first)
    near_ref[...] = jnp.where(odd, first, last)


def second_tv_kernel(
    field_ref, dual_ref, plane_ref, far_ref, near_ref, edge_ref, new_dual_ref, back_ref
):
    before, behind = x_halos(far_ref, near_ref)
    edge = edge_ref[...]
    ray = lax.axis_index("ray")
    end_x = lax.axis_index("mp") == N_MP - 1
    field = [field_ref[x] for x in range(GX)]
    sub = lax.broadcasted_iota(jnp.int32, (2 * GX, TILE), 0)
    rows = edge[0 : 2 * GX]
    ahead_x = jnp.where(sub == GX - 1, behind[GY : GY + 1], pltpu.roll(rows, 2 * GX - 1, 0))
    ahead_y = jnp.concatenate([field[x][0:1] for x in range(GX)] * 2, axis=0)
    dual_rows = [
        jnp.concatenate([edge[(c + 3) * GX : (c + 4) * GX]] * 2, axis=0) for c in range(3)
    ]
    _, change = tv_cells(
        rows, ahead_x, ahead_y, dual_rows, (sub == GX - 1) & end_x, sub < 0
    )
    from_y = jnp.where(ray == 0, 0.0, change[1])
    fresh, backs, _, _ = tv_step_all(
        field,
        [[dual_ref[c, x] for x in range(GX)] for c in range(3)],
        before[0:GY], before[GY + 2 * GX - 1 : GY + 2 * GX],
        [plane_ref[c] for c in range(3)],
        behind[0:GY],
        [edge[GX + x : GX + x + 1] for x in range(GX)],
        [from_y[x : x + 1] for x in range(GX)],
    )
    for x in range(GX):
        back_ref[x] = backs[x]
        for c in range(3):
            new_dual_ref[c, x] = fresh[x][c]


def on_device(
    slowness, accumulated, extrapolated, tv_dual, ray_dual, traveltimes, tiles, pattern, selected
):
    pattern = pattern.T
    busy = 8 * 2**20
    grid = (GRID, F32)
    duals = ((3,) + GRID, F32)
    swapped = ((GY + 2 * GX, TILE), F32)

    field, sent = call(
        start_kernel, [grid, ((N_RAY, SENT, TILE), BF16)], "hhhh",
        (slowness, extrapolated, pattern, selected),
        (pltpu.VMEM(GRID, F32), pltpu.VMEM(GRID, F32), pltpu.SemaphoreType.DMA((2,))) + SCALARS,
    )
    gathered = exchange(sent, "ray")
    picked, hot, pick = fetch(0, tiles, pattern, selected, field)
    (partial_value,) = call(predict_kernel, [SUMS], "vvv", (gathered, picked, hot))
    parts = exchange(partial_value, "mp")

    far, near = call(
        first_edges_kernel, [((5 * GY, TILE), F32)] * 2, "vvva",
        (field, tv_dual, gathered, partial_value), busy=busy,
    )
    far, near = swap_far(far), swap_near(near)
    dual, dual_plane, tv_back, base, rest, extra = call(
        first_tv_kernel,
        [duals, ((3, GY, TILE), F32), grid, grid, grid, ((4 * GX, TILE), F32)],
        "vvvvvv", (field, tv_dual, far, near, gathered, accumulated), busy=busy,
    )
    picked_2, hot_2, pick_2 = fetch(1, tiles, pattern, selected, partial_value)

    rays, share = call(
        share_kernel, [RAYS, ((N_RAY, SHARED, TILE), BF16)], "vvvvvvv",
        (parts, ray_dual, traveltimes, pick, picked, rest, extra),
    )
    shared = exchange(share, "ray")
    back, edge, partial_value = call(
        image_kernel, [((OWN, TILE), F32), ((6 * GX, TILE), F32), SUMS], "vvvv",
        (shared, gathered, picked_2, hot_2), (pltpu.VMEM((ALL, TILE), F32),),
    )
    parts = exchange(partial_value, "mp")

    field, image, far, near = call(
        second_edges_kernel, [grid, grid, swapped, swapped], "vvvvv",
        (base, back, edge, accumulated, tv_back), busy=busy,
    )
    far = swap_far(far)
    rays, share, near = call(
        back_kernel, [RAYS, ((N_RAY, OWN, TILE), BF16), swapped], "vvvvvvav",
        (parts, rays, traveltimes, pick_2, picked_2, hot_2, far, near),
    )
    shared = exchange(share, "ray")
    near = swap_near(near)
    dual, tv_back = call(
        second_tv_kernel, [duals, grid], "vvvvvv",
        (field, dual, dual_plane, far, near, edge), busy=busy,
    )
    back = jnp.sum(shared.astype(F32), axis=0).reshape(GRID)
    image = image + back + tv_back
    image_bar = image + extrapolation * back + tv_back
    return (field, rays, dual, image, image_bar)


def solution(mesh):
    in_specs = (
        P("mp", "ray", None),
        P("mp", "ray", None),
        P("mp", "ray", None),
        P(None, "mp", "ray", None),
        P("ray", None),
        P("ray", None),
        P("ray", "mp", None, None),
        P("ray", "mp"),
        P(None, "ray"),
    )
    out_specs = (
        P("mp", "ray", None),
        P("ray", None),
        P(None, "mp", "ray", None),
        P("mp", "ray", None),
        P("mp", "ray", None),
    )
    return jax.shard_map(
        on_device, mesh=mesh, in_specs=in_specs, out_specs=out_specs, check_vma=False
    )
```

```python
import jax
import jax.numpy as jnp
from jax import lax
from jax.experimental import pallas as pl
from jax.experimental.pallas import tpu as pltpu
from jax.sharding import PartitionSpec as P

TILE = 128
GX = 4
GY = 8
RB_DEV = 16
CAP = 8
MAXSEL = 8
N_RAY = 16
N_MP = 32
OWN = GX * GY
ALL = N_RAY * OWN
PRODUCTS = MAXSEL * CAP
SENT = OWN + 16
REST = OWN + 8
EXTRA = PRODUCTS + OWN
SHARED = EXTRA + 16
GATHER, SUM_1, SHARE, SUM_2, LAST = 15, 18, 15, 18, 15

primal_step = 0.5
dual_step = 0.5
tv_step = 0.25
tv_weight = 0.3
extrapolation = 2.0 * RB_DEV / (MAXSEL + 1)
gain = primal_step * (1.0 + extrapolation)

F32 = jnp.float32
BF16 = jnp.bfloat16
GRID = (GX, GY, TILE)
SUMS = ((N_MP, MAXSEL, TILE), F32)
RAYS = ((RB_DEV, TILE), F32)


def exchange(copies, axis, first):
    size = N_RAY if axis == "ray" else N_MP
    groups = [[(first + i) % size for i in range(size)]]
    return lax.all_to_all(copies, axis, 0, 0, tiled=True, axis_index_groups=groups)


def at(peer, first):
    return (peer + (N_RAY - first)) & (N_RAY - 1)


def call(kernel, outs, places, args, scratch=(), busy=0, keep=False):
    spaces = {"v": pltpu.VMEM, "h": pltpu.HBM, "a": pl.ANY}
    cost = pl.CostEstimate(flops=0, bytes_accessed=busy, transcendentals=0) if busy else None
    args = [
        pltpu.with_memory_space_constraint(arg, pltpu.HBM) if place == "h" else arg
        for arg, place in zip(args, places)
    ]
    return pl.pallas_call(
        kernel,
        out_shape=[
            pltpu.VMEM(shape, dtype) if keep else jax.ShapeDtypeStruct(shape, dtype)
            for shape, dtype in outs
        ],
        in_specs=[pl.BlockSpec(memory_space=spaces[c]) for c in places],
        out_specs=[pl.BlockSpec(memory_space=pltpu.VMEM) for _ in outs],
        scratch_shapes=list(scratch),
        cost_estimate=cost,
        compiler_params=pltpu.CompilerParams(vmem_limit_bytes=20 * 1024 * 1024),
    )(*args)


SCALARS = (
    pltpu.SMEM((CAP, RB_DEV), jnp.int32),
    pltpu.SMEM((2, RB_DEV), jnp.int32),
    pltpu.SMEM((RB_DEV,), jnp.int32),
    pltpu.SemaphoreType.DMA((2,)),
)


def scalar_copies(pattern_hbm, selected_hbm, pattern_ref, selected_ref, sems):
    return [
        pltpu.make_async_copy(pattern_hbm, pattern_ref, sems.at[0]),
        pltpu.make_async_copy(selected_hbm, selected_ref, sems.at[1]),
    ]


def block_number(pattern):
    row = pattern & (GY * N_RAY - 1)
    plane = lax.shift_right_logical(pattern, 7)
    return lax.shift_right_logical(row, 3) * OWN + plane * GY + (row & (GY - 1))


def list_selected(selected_ref, step, list_ref):
    for n in range(MAXSEL):
        list_ref[n] = jnp.int32(0)
    count = jnp.int32(0)
    for r in range(RB_DEV):
        list_ref[count] = jnp.int32(r)
        count = count + selected_ref[step, r]
    return count


def start_kernel(
    slowness_hbm, bar_hbm, pattern_hbm, selected_hbm, field_ref, sent_ref,
    slowness_ref, bar_ref, sems, pattern_ref, selected_ref, list_ref, scalar_sems,
):
    copies = scalar_copies(pattern_hbm, selected_hbm, pattern_ref, selected_ref, scalar_sems)
    copies.append(pltpu.make_async_copy(slowness_hbm, slowness_ref, sems.at[0]))
    copies.append(pltpu.make_async_copy(bar_hbm, bar_ref, sems.at[1]))
    for copy in copies:
        copy.start()
    copies[0].wait()
    copies[1].wait()
    list_selected(selected_ref, 0, list_ref)
    lane = lax.broadcasted_iota(jnp.int32, (8, TILE), 1) & (PRODUCTS - 1)
    sub = lax.broadcasted_iota(jnp.int32, (8, TILE), 0)
    numbers = jnp.zeros((8, TILE), jnp.int32)
    for n in range(MAXSEL):
        r = list_ref[n]
        for s in range(CAP):
            numbers = jnp.where(lane == n * CAP + s, block_number(pattern_ref[s, r]), numbers)
    numbers = jnp.where(sub == 0, lax.shift_right_logical(numbers, 5), numbers & (OWN - 1))
    copies[2].wait()
    copies[3].wait()
    field = slowness_ref[...] - primal_step * bar_ref[...]
    field_ref[...] = field
    field = field.reshape(OWN, TILE)
    rounded = field.astype(BF16)
    low = field - rounded.astype(F32)
    rest = jnp.zeros((8, TILE), F32)
    for x in range(GX):
        rest = jnp.where(sub == x, low[x * GY : x * GY + 1], rest)
    tail = jnp.concatenate([numbers.astype(F32), rest], axis=0).astype(BF16)
    for p in range(N_RAY):
        sent_ref[p, 0:OWN, :] = rounded
        sent_ref[p, OWN:SENT, :] = tail


def fetch_kernel(step):
    def kernel(
        tiles_hbm, pattern_hbm, selected_hbm, after_ref, picked_ref, hot_ref, pick_ref,
        pattern_ref, selected_ref, list_ref, scalar_sems, sems,
    ):
        scalars = scalar_copies(pattern_hbm, selected_hbm, pattern_ref, selected_ref, scalar_sems)
        for copy in scalars:
            copy.start()
        for copy in scalars:
            copy.wait()
        count = list_selected(selected_ref, step, list_ref)
        copies = [
            pltpu.make_async_copy(tiles_hbm.at[list_ref[n]], picked_ref.at[n], sems.at[n])
            for n in range(MAXSEL)
        ]
        for copy in copies:
            copy.start()
        sub = lax.broadcasted_iota(jnp.int32, (MAXSEL, TILE), 0)
        lane = lax.broadcasted_iota(jnp.int32, (2 * CAP, TILE), 1)
        for n in range(0, MAXSEL, 2):
            halves = []
            for m in (n, n + 1):
                r = list_ref[m]
                numbers = jnp.zeros((CAP, TILE), jnp.int32)
                for s in range(CAP):
                    numbers = jnp.where(sub == s, block_number(pattern_ref[s, r]), numbers)
                halves.append(numbers)
            numbers = jnp.concatenate(halves, axis=0)
            for c in range(ALL // TILE):
                hot = jnp.where(numbers == lane + c * TILE, 1.0, 0.0).astype(BF16)
                hot_ref[n * CAP : (n + 2) * CAP, c * TILE : (c + 1) * TILE] = hot
        listed = jnp.full((MAXSEL, TILE), RB_DEV, jnp.int32)
        for n in range(MAXSEL):
            listed = jnp.where((sub == n) & (sub < count), list_ref[n], listed)
        for r in range(RB_DEV):
            pick_ref[r] = jnp.where(listed == r, 1.0, 0.0)
        for copy in copies:
            copy.wait()

    return kernel


def fetch(step, tiles, pattern, selected, after):
    outs = [
        ((MAXSEL, CAP, TILE, TILE), BF16),
        ((PRODUCTS, ALL), BF16),
        ((RB_DEV, MAXSEL, TILE), F32),
    ]
    scratch = SCALARS + (pltpu.SemaphoreType.DMA((MAXSEL,)),)
    return call(
        fetch_kernel(step), outs, "hhha", (tiles, pattern, selected, after), scratch, 8 * 2**20, True
    )


def forward(hot_ref, blocks, picked_ref, out_ref):
    cells = jnp.dot(hot_ref[...], blocks, preferred_element_type=F32)
    sub = lax.broadcasted_iota(jnp.int32, (MAXSEL, TILE), 0)
    total = jnp.zeros((MAXSEL, TILE), F32)
    for n in range(MAXSEL):
        for s in range(CAP):
            row = cells[n * CAP + s : n * CAP + s + 1]
            lhs = jnp.where(sub == n, row, 0.0).astype(BF16)
            total = total + lax.dot_general(
                lhs, picked_ref[n, s], (((1,), (1,)), ((), ())), preferred_element_type=F32
            )
    for m in range(N_MP):
        out_ref[m] = total


def predict_kernel(gathered_ref, picked_ref, hot_ref, out_ref):
    blocks = jnp.concatenate([gathered_ref[at(p, GATHER), 0:OWN, :] for p in range(N_RAY)], axis=0)
    forward(hot_ref, blocks, picked_ref, out_ref)


def dual_update(parts_ref, rays_ref, times_ref, pick_ref, new_rays_ref):
    predicted = parts_ref[0]
    for m in range(1, N_MP):
        predicted = predicted + parts_ref[m]
    rays = jnp.zeros((MAXSEL, TILE), F32)
    times = jnp.zeros((MAXSEL, TILE), F32)
    taken = jnp.zeros((MAXSEL, TILE), F32)
    for r in range(RB_DEV):
        pick = pick_ref[r]
        rays = rays + pick * rays_ref[r : r + 1, :]
        times = times + pick * times_ref[r : r + 1, :]
        taken = taken + pick
    fresh = (rays + dual_step * (predicted - times)) / (1.0 + dual_step)
    change = taken * (fresh - rays)
    for r in range(RB_DEV):
        new_rays_ref[r : r + 1, :] = rays_ref[r : r + 1, :] + jnp.sum(
            pick_ref[r] * change, axis=0, keepdims=True
        )
    return change


def products(change, picked_ref, n):
    sub = lax.broadcasted_iota(jnp.int32, (CAP, TILE), 0)
    row = change[n : n + 1]
    total = jnp.zeros((CAP, TILE), F32)
    for s in range(CAP):
        lhs = jnp.where(sub == s, row, 0.0).astype(BF16)
        total = total + jnp.dot(lhs, picked_ref[n, s], preferred_element_type=F32)
    return total


def share_kernel(
    parts_ref, rays_ref, times_ref, pick_ref, picked_ref, rest_ref, extra_ref, new_rays_ref, out_ref
):
    change = dual_update(parts_ref, rays_ref, times_ref, pick_ref, new_rays_ref)
    for n in range(0, MAXSEL, 2):
        pair = jnp.concatenate(
            [products(change, picked_ref, n), products(change, picked_ref, n + 1)], axis=0
        ).astype(BF16)
        for p in range(N_RAY):
            out_ref[p, n * CAP : (n + 2) * CAP, :] = pair
    rest = rest_ref[...].reshape(OWN, TILE).astype(BF16)
    extra = extra_ref[...].astype(BF16)
    for p in range(N_RAY):
        out_ref[p, PRODUCTS:EXTRA, :] = rest
        out_ref[p, EXTRA:SHARED, :] = extra


def image_kernel(
    shared_ref, gathered_ref, picked_ref, hot_ref, back_ref, edge_ref, out_ref, table_ref
):
    lane = lax.broadcasted_iota(jnp.int32, (1, TILE), 1)
    singles = []
    for p in range(N_RAY):
        rows = gathered_ref[at(p, GATHER), OWN:SENT, :].astype(F32)
        singles.append(rows[0:1] * OWN + rows[1:2])
    pairs = [jnp.where(lane < PRODUCTS, singles[p], singles[p + 1]) for p in range(0, N_RAY, 2)]
    group = 4
    chunk = group * OWN
    numbers = []
    terms = []
    for g in range(0, N_RAY, group):
        numbers.append(jnp.concatenate(pairs[g // 2 : g // 2 + 2], axis=1).astype(jnp.int32))
        terms.append(
            jnp.concatenate(
                [shared_ref[at(p, SHARE), 0:PRODUCTS, :] for p in range(g, g + group)], axis=0
            )
        )
    place = lax.broadcasted_iota(jnp.int32, (chunk, group * PRODUCTS), 0)
    sub = lax.broadcasted_iota(jnp.int32, (GY, TILE), 0)
    blocks = []
    for g in range(0, N_RAY, group):
        back = jnp.zeros((chunk, TILE), F32)
        for k in range(N_RAY // group):
            hot = jnp.where(place + g * OWN == numbers[k], 1.0, 0.0).astype(BF16)
            back = back + jnp.dot(hot, terms[k], preferred_element_type=F32)
        table_ref[g * OWN : g * OWN + chunk, :] = back
        for p in range(g, g + group):
            rows = slice(p * OWN, (p + 1) * OWN)
            rest = shared_ref[at(p, SHARE), PRODUCTS:EXTRA, :].astype(F32)
            field = gathered_ref[at(p, GATHER), 0:OWN, :].astype(F32) + (rest - gain * table_ref[rows, :])
            if p > 0:
                change = shared_ref[at(p - 1, SHARE), EXTRA:SHARED, :].astype(F32)
                field = field - (2.0 * primal_step) * jnp.concatenate(
                    [jnp.where(sub == 0, change[x : x + 1], 0.0) for x in range(GX)], axis=0
                )
            blocks.append(field)
    forward(
        hot_ref, jnp.concatenate([field.astype(BF16) for field in blocks], axis=0), picked_ref, out_ref
    )
    me = lax.axis_index("ray")
    back_ref[...] = table_ref[pl.ds(pl.multiple_of(me * OWN, OWN), OWN), :]
    for p in range(N_RAY):
        table_ref[p * OWN : (p + 1) * OWN, :] = blocks[p]
    before = jnp.maximum(me - 1, 0)
    for side, peer, row in ((0, before, GY - 1), (1, jnp.minimum(me + 1, N_RAY - 1), 0)):
        field = table_ref[pl.ds(pl.multiple_of(peer * OWN, OWN), OWN), :]
        for x in range(GX):
            edge_ref[side * GX + x : side * GX + x + 1, :] = field[x * GY + row : x * GY + row + 1]
    edge_ref[2 * GX : 6 * GX] = shared_ref[at(before, SHARE), EXTRA:SHARED, :].astype(F32)


def back_kernel(
    parts_ref, rays_ref, times_ref, pick_ref, picked_ref, hot_ref, far_any, near_ref, new_rays_ref, out_ref, same_ref
):
    same_ref[...] = near_ref[...]
    change = dual_update(parts_ref, rays_ref, times_ref, pick_ref, new_rays_ref)
    terms = jnp.concatenate([products(change, picked_ref, n) for n in range(MAXSEL)], axis=0)
    high = terms.astype(BF16)
    low = (terms - high.astype(F32)).astype(BF16)
    turned = (((0,), (0,)), ((), ()))
    image = lax.dot_general(hot_ref[...], high, turned, preferred_element_type=F32)
    image = image + lax.dot_general(hot_ref[...], low, turned, preferred_element_type=F32)
    for p in range(N_RAY):
        out_ref[at(p, LAST)] = image[p * OWN : (p + 1) * OWN].astype(BF16)


def swap(block, first):
    route = [(m, m + 1) for m in range(first, N_MP - 1, 2)]
    return lax.ppermute(block, "mp", route + [(b, a) for a, b in route])


def swap_far(block):
    return swap(block, 1)


def swap_near(block):
    return swap(block, 0)


def next_rows(gathered_ref):
    peer = jnp.minimum(lax.axis_index("ray") + 1, N_RAY - 1)
    high = gathered_ref[at(peer, GATHER), 0:OWN, :].astype(F32)
    low = gathered_ref[at(peer, GATHER), OWN:SENT, :].astype(F32)
    return [
        high[x * GY : x * GY + 1] + low[REST - OWN + x : REST - OWN + x + 1] for x in range(GX)
    ]


def first_edges_kernel(field_ref, dual_ref, gathered_ref, after_any, far_ref, near_ref):
    odd = (lax.axis_index("mp") & 1) == 1
    first = field_ref[0]
    last = field_ref[GX - 1]
    far_ref[0:GY] = jnp.where(odd, last, first)
    near_ref[0:GY] = jnp.where(odd, first, last)
    corner = jnp.broadcast_to(next_rows(gathered_ref)[GX - 1], (GY, TILE))
    far_ref[GY : 2 * GY] = corner
    near_ref[GY : 2 * GY] = corner
    for c in range(3):
        rows = slice((c + 2) * GY, (c + 3) * GY)
        far_ref[rows] = dual_ref[c, GX - 1]
        near_ref[rows] = dual_ref[c, GX - 1]


def x_halos(far_ref, near_ref):
    odd = (lax.axis_index("mp") & 1) == 1
    far, near = far_ref[...], near_ref[...]
    return jnp.where(odd, near, far), jnp.where(odd, far, near)


def tv_cells(here, ahead_x, ahead_y, dual, no_x, no_y):
    lane = lax.broadcasted_iota(jnp.int32, here.shape, len(here.shape) - 1)
    ahead_z = pltpu.roll(here, TILE - 1, len(here.shape) - 1)
    steps = (
        jnp.where(no_x, 0.0, ahead_x - here),
        jnp.where(no_y, 0.0, ahead_y - here),
        jnp.where(lane == TILE - 1, 0.0, ahead_z - here),
    )
    moved = [d + tv_step * g for d, g in zip(dual, steps)]
    length = jnp.sqrt(moved[0] * moved[0] + moved[1] * moved[1] + moved[2] * moved[2])
    scale = jnp.maximum(1.0, length / tv_weight)
    fresh = [m / scale for m in moved]
    return fresh, [a - b for a, b in zip(fresh, dual)]


def up_one(plane, row):
    sub = lax.broadcasted_iota(jnp.int32, plane.shape, 0)
    return jnp.where(sub == GY - 1, row, pltpu.roll(plane, GY - 1, 0))


def tv_step_all(field, dual, before, before_next, dual_before, behind, nexts, from_y):
    mp, ray = lax.axis_index("mp"), lax.axis_index("ray")
    sub = lax.broadcasted_iota(jnp.int32, (GY, TILE), 0)
    lane = lax.broadcasted_iota(jnp.int32, (GY, TILE), 1)
    end_x = (mp == N_MP - 1) & (sub >= 0)
    last_y = (sub == GY - 1) & (ray == N_RAY - 1)
    never = sub < 0

    halo, halo_change = tv_cells(
        before, field[0], up_one(before, before_next), dual_before, never, last_y
    )
    from_x = jnp.where(mp == 0, 0.0, halo_change[0])
    fresh, backs, second = [], [], []
    for x in range(GX):
        ahead = field[x + 1] if x + 1 < GX else behind
        no_x = end_x if x + 1 == GX else never
        new, change = tv_cells(
            field[x], ahead, up_one(field[x], nexts[x]), [d[x] for d in dual], no_x, last_y
        )
        comp_x = jnp.where(no_x, 0.0, change[0])
        comp_y = jnp.where(last_y, 0.0, change[1])
        comp_z = jnp.where(lane == TILE - 1, 0.0, change[2])
        back = from_x - comp_x
        back = back + (jnp.where(sub == 0, from_y[x], pltpu.roll(comp_y, 1, 0)) - comp_y)
        back = back + (jnp.where(lane == 0, 0.0, pltpu.roll(comp_z, 1, 1)) - comp_z)
        from_x = comp_x
        fresh.append(new)
        backs.append(back)
        second.append(comp_y)
    return fresh, backs, halo, second


def first_tv_kernel(
    field_ref, dual_ref, far_ref, near_ref, gathered_ref, image_ref,
    new_dual_ref, plane_ref, back_ref, base_ref, rest_ref, extra_ref,
):
    before, behind = x_halos(far_ref, near_ref)
    field = [field_ref[x] for x in range(GX)]
    fresh, backs, halo, second = tv_step_all(
        field,
        [[dual_ref[c, x] for x in range(GX)] for c in range(3)],
        before[0:GY], before[GY : GY + 1],
        [before[(c + 2) * GY : (c + 3) * GY] for c in range(3)],
        behind[0:GY], next_rows(gathered_ref), [0.0] * GX,
    )
    for x in range(GX):
        base = field[x] - primal_step * (image_ref[x] + 2.0 * backs[x])
        back_ref[x] = backs[x]
        base_ref[x] = base
        rest_ref[x] = base - field[x].astype(BF16).astype(F32)
        extra_ref[x : x + 1] = second[x][GY - 1 : GY]
        for c in range(3):
            new_dual_ref[c, x] = fresh[x][c]
            row = (c + 1) * GX + x
            extra_ref[row : row + 1] = fresh[x][c][GY - 1 : GY]
    for c in range(3):
        plane_ref[c] = halo[c]


def second_edges_kernel(
    base_ref, back_ref, edge_ref, image_ref, tv_ref, field_ref, new_image_ref, far_ref, near_ref
):
    odd = (lax.axis_index("mp") & 1) == 1
    sub = lax.broadcasted_iota(jnp.int32, (GY, TILE), 0)
    first_y = (sub == 0) & (lax.axis_index("ray") > 0)
    field = []
    for x in range(GX):
        back = back_ref[x * GY : (x + 1) * GY]
        from_y = jnp.where(first_y, edge_ref[2 * GX + x : 2 * GX + x + 1], 0.0)
        field.append(base_ref[x] - (gain * back + (2.0 * primal_step) * from_y))
        field_ref[x] = field[x]
        new_image_ref[x] = image_ref[x] + back + (tv_ref[x] + from_y)
    edge = edge_ref[0 : 2 * GX]
    first = jnp.concatenate([field[0], edge], axis=0)
    last = jnp.concatenate([field[GX - 1], edge], axis=0)
    far_ref[...] = jnp.where(odd, last, first)
    near_ref[...] = jnp.where(odd, first, last)


def second_tv_kernel(
    field_ref, dual_ref, plane_ref, far_ref, near_ref, edge_ref, new_dual_ref, back_ref
):
    before, behind = x_halos(far_ref, near_ref)
    edge = edge_ref[...]
    ray = lax.axis_index("ray")
    end_x = lax.axis_index("mp") == N_MP - 1
    field = [field_ref[x] for x in range(GX)]
    sub = lax.broadcasted_iota(jnp.int32, (2 * GX, TILE), 0)
    rows = edge[0 : 2 * GX]
    ahead_x = jnp.where(sub == GX - 1, behind[GY : GY + 1], pltpu.roll(rows, 2 * GX - 1, 0))
    ahead_y = jnp.concatenate([field[x][0:1] for x in range(GX)] * 2, axis=0)
    dual_rows = [
        jnp.concatenate([edge[(c + 3) * GX : (c + 4) * GX]] * 2, axis=0) for c in range(3)
    ]
    _, change = tv_cells(
        rows, ahead_x, ahead_y, dual_rows, (sub == GX - 1) & end_x, sub < 0
    )
    from_y = jnp.where(ray == 0, 0.0, change[1])
    fresh, backs, _, _ = tv_step_all(
        field,
        [[dual_ref[c, x] for x in range(GX)] for c in range(3)],
        before[0:GY], before[GY + 2 * GX - 1 : GY + 2 * GX],
        [plane_ref[c] for c in range(3)],
        behind[0:GY],
        [edge[GX + x : GX + x + 1] for x in range(GX)],
        [from_y[x : x + 1] for x in range(GX)],
    )
    for x in range(GX):
        back_ref[x] = backs[x]
        for c in range(3):
            new_dual_ref[c, x] = fresh[x][c]


def on_device(
    slowness, accumulated, extrapolated, tv_dual, ray_dual, traveltimes, tiles, pattern, selected
):
    pattern = pattern.T
    busy = 8 * 2**20
    grid = (GRID, F32)
    duals = ((3,) + GRID, F32)
    swapped = ((GY + 2 * GX, TILE), F32)

    field, sent = call(
        start_kernel, [grid, ((N_RAY, SENT, TILE), BF16)], "hhhh",
        (slowness, extrapolated, pattern, selected),
        (pltpu.VMEM(GRID, F32), pltpu.VMEM(GRID, F32), pltpu.SemaphoreType.DMA((2,))) + SCALARS,
    )
    gathered = exchange(sent, "ray", GATHER)
    picked, hot, pick = fetch(0, tiles, pattern, selected, field)
    (partial_value,) = call(predict_kernel, [SUMS], "vvv", (gathered, picked, hot))
    parts = exchange(partial_value, "mp", SUM_1)

    far, near = call(
        first_edges_kernel, [((5 * GY, TILE), F32)] * 2, "vvva",
        (field, tv_dual, gathered, partial_value), busy=busy,
    )
    far, near = swap_far(far), swap_near(near)
    dual, dual_plane, tv_back, base, rest, extra = call(
        first_tv_kernel,
        [duals, ((3, GY, TILE), F32), grid, grid, grid, ((4 * GX, TILE), F32)],
        "vvvvvv", (field, tv_dual, far, near, gathered, accumulated), busy=busy,
    )
    picked_2, hot_2, pick_2 = fetch(1, tiles, pattern, selected, partial_value)

    rays, share = call(
        share_kernel, [RAYS, ((N_RAY, SHARED, TILE), BF16)], "vvvvvvv",
        (parts, ray_dual, traveltimes, pick, picked, rest, extra),
    )
    shared = exchange(share, "ray", SHARE)
    back, edge, partial_value = call(
        image_kernel, [((OWN, TILE), F32), ((6 * GX, TILE), F32), SUMS], "vvvv",
        (shared, gathered, picked_2, hot_2), (pltpu.VMEM((ALL, TILE), F32),),
    )
    parts = exchange(partial_value, "mp", SUM_2)

    field, image, far, near = call(
        second_edges_kernel, [grid, grid, swapped, swapped], "vvvvv",
        (base, back, edge, accumulated, tv_back), busy=busy,
    )
    far = swap_far(far)
    rays, share, near = call(
        back_kernel, [RAYS, ((N_RAY, OWN, TILE), BF16), swapped], "vvvvvvav",
        (parts, rays, traveltimes, pick_2, picked_2, hot_2, far, near),
    )
    shared = exchange(share, "ray", LAST)
    near = swap_near(near)
    dual, tv_back = call(
        second_tv_kernel, [duals, grid], "vvvvvv",
        (field, dual, dual_plane, far, near, edge), busy=busy,
    )
    back = jnp.sum(shared.astype(F32), axis=0).reshape(GRID)
    image = image + back + tv_back
    image_bar = image + extrapolation * back + tv_back
    return (field, rays, dual, image, image_bar)


def solution(mesh):
    in_specs = (
        P("mp", "ray", None),
        P("mp", "ray", None),
        P("mp", "ray", None),
        P(None, "mp", "ray", None),
        P("ray", None),
        P("ray", None),
        P("ray", "mp", None, None),
        P("ray", "mp"),
        P(None, "ray"),
    )
    out_specs = (
        P("mp", "ray", None),
        P("ray", None),
        P(None, "mp", "ray", None),
        P("mp", "ray", None),
        P("mp", "ray", None),
    )
    return jax.shard_map(
        on_device, mesh=mesh, in_specs=in_specs, out_specs=out_specs, check_vma=False
    )
```

```python
import jax
import jax.numpy as jnp
from jax import lax
from jax.experimental import pallas as pl
from jax.experimental.pallas import tpu as pltpu
from jax.sharding import PartitionSpec as P

TILE = 128
GX = 4
GY = 8
RB_DEV = 16
CAP = 8
MAXSEL = 8
N_RAY = 16
N_MP = 32
OWN = GX * GY
ALL = N_RAY * OWN
PRODUCTS = MAXSEL * CAP
SENT = OWN + 16
REST = OWN + 8
EXTRA = PRODUCTS + OWN
SHARED = EXTRA + 16
GATHER, SUM_1, SHARE, SUM_2, LAST = 9, 19, 5, 3, 5

primal_step = 0.5
dual_step = 0.5
tv_step = 0.25
tv_weight = 0.3
extrapolation = 2.0 * RB_DEV / (MAXSEL + 1)
gain = primal_step * (1.0 + extrapolation)

F32 = jnp.float32
BF16 = jnp.bfloat16
GRID = (GX, GY, TILE)
SUMS = ((N_MP, MAXSEL, TILE), F32)
RAYS = ((RB_DEV, TILE), F32)


def exchange(copies, axis, first):
    size = N_RAY if axis == "ray" else N_MP
    groups = [[(first + i) % size for i in range(size)]]
    return lax.all_to_all(copies, axis, 0, 0, tiled=True, axis_index_groups=groups)


def at(peer, first):
    return (peer + (N_RAY - first)) & (N_RAY - 1)


def call(kernel, outs, places, args, scratch=(), busy=0, keep=False):
    spaces = {"v": pltpu.VMEM, "h": pltpu.HBM, "a": pl.ANY}
    cost = pl.CostEstimate(flops=0, bytes_accessed=busy, transcendentals=0) if busy else None
    args = [
        pltpu.with_memory_space_constraint(arg, pltpu.HBM) if place == "h" else arg
        for arg, place in zip(args, places)
    ]
    return pl.pallas_call(
        kernel,
        out_shape=[
            pltpu.VMEM(shape, dtype) if keep else jax.ShapeDtypeStruct(shape, dtype)
            for shape, dtype in outs
        ],
        in_specs=[pl.BlockSpec(memory_space=spaces[c]) for c in places],
        out_specs=[pl.BlockSpec(memory_space=pltpu.VMEM) for _ in outs],
        scratch_shapes=list(scratch),
        cost_estimate=cost,
        compiler_params=pltpu.CompilerParams(vmem_limit_bytes=20 * 1024 * 1024),
    )(*args)


SCALARS = (
    pltpu.SMEM((CAP, RB_DEV), jnp.int32),
    pltpu.SMEM((2, RB_DEV), jnp.int32),
    pltpu.SMEM((RB_DEV,), jnp.int32),
    pltpu.SemaphoreType.DMA((2,)),
)


def scalar_copies(pattern_hbm, selected_hbm, pattern_ref, selected_ref, sems):
    return [
        pltpu.make_async_copy(pattern_hbm, pattern_ref, sems.at[0]),
        pltpu.make_async_copy(selected_hbm, selected_ref, sems.at[1]),
    ]


def block_number(pattern):
    row = pattern & (GY * N_RAY - 1)
    plane = lax.shift_right_logical(pattern, 7)
    return lax.shift_right_logical(row, 3) * OWN + plane * GY + (row & (GY - 1))


def list_selected(selected_ref, step, list_ref):
    for n in range(MAXSEL):
        list_ref[n] = jnp.int32(0)
    count = jnp.int32(0)
    for r in range(RB_DEV):
        list_ref[count] = jnp.int32(r)
        count = count + selected_ref[step, r]
    return count


def start_kernel(
    slowness_hbm, bar_hbm, pattern_hbm, selected_hbm, field_ref, sent_ref,
    slowness_ref, bar_ref, sems, pattern_ref, selected_ref, list_ref, scalar_sems,
):
    copies = scalar_copies(pattern_hbm, selected_hbm, pattern_ref, selected_ref, scalar_sems)
    copies.append(pltpu.make_async_copy(slowness_hbm, slowness_ref, sems.at[0]))
    copies.append(pltpu.make_async_copy(bar_hbm, bar_ref, sems.at[1]))
    for copy in copies:
        copy.start()
    copies[0].wait()
    copies[1].wait()
    list_selected(selected_ref, 0, list_ref)
    lane = lax.broadcasted_iota(jnp.int32, (8, TILE), 1) & (PRODUCTS - 1)
    sub = lax.broadcasted_iota(jnp.int32, (8, TILE), 0)
    numbers = jnp.zeros((8, TILE), jnp.int32)
    for n in range(MAXSEL):
        r = list_ref[n]
        for s in range(CAP):
            numbers = jnp.where(lane == n * CAP + s, block_number(pattern_ref[s, r]), numbers)
    numbers = jnp.where(sub == 0, lax.shift_right_logical(numbers, 5), numbers & (OWN - 1))
    copies[2].wait()
    copies[3].wait()
    field = slowness_ref[...] - primal_step * bar_ref[...]
    field_ref[...] = field
    field = field.reshape(OWN, TILE)
    rounded = field.astype(BF16)
    low = field - rounded.astype(F32)
    rest = jnp.zeros((8, TILE), F32)
    for x in range(GX):
        rest = jnp.where(sub == x, low[x * GY : x * GY + 1], rest)
    tail = jnp.concatenate([numbers.astype(F32), rest], axis=0).astype(BF16)
    for p in range(N_RAY):
        sent_ref[p, 0:OWN, :] = rounded
        sent_ref[p, OWN:SENT, :] = tail


def fetch_kernel(step):
    def kernel(
        tiles_hbm, pattern_hbm, selected_hbm, after_ref, picked_ref, hot_ref, pick_ref,
        pattern_ref, selected_ref, list_ref, scalar_sems, sems,
    ):
        scalars = scalar_copies(pattern_hbm, selected_hbm, pattern_ref, selected_ref, scalar_sems)
        for copy in scalars:
            copy.start()
        for copy in scalars:
            copy.wait()
        count = list_selected(selected_ref, step, list_ref)
        copies = [
            pltpu.make_async_copy(tiles_hbm.at[list_ref[n]], picked_ref.at[n], sems.at[n])
            for n in range(MAXSEL)
        ]
        for copy in copies:
            copy.start()
        sub = lax.broadcasted_iota(jnp.int32, (MAXSEL, TILE), 0)
        lane = lax.broadcasted_iota(jnp.int32, (2 * CAP, TILE), 1)
        for n in range(0, MAXSEL, 2):
            halves = []
            for m in (n, n + 1):
                r = list_ref[m]
                numbers = jnp.zeros((CAP, TILE), jnp.int32)
                for s in range(CAP):
                    numbers = jnp.where(sub == s, block_number(pattern_ref[s, r]), numbers)
                halves.append(numbers)
            numbers = jnp.concatenate(halves, axis=0)
            for c in range(ALL // TILE):
                hot = jnp.where(numbers == lane + c * TILE, 1.0, 0.0).astype(BF16)
                hot_ref[n * CAP : (n + 2) * CAP, c * TILE : (c + 1) * TILE] = hot
        listed = jnp.full((MAXSEL, TILE), RB_DEV, jnp.int32)
        for n in range(MAXSEL):
            listed = jnp.where((sub == n) & (sub < count), list_ref[n], listed)
        for r in range(RB_DEV):
            pick_ref[r] = jnp.where(listed == r, 1.0, 0.0)
        for copy in copies:
            copy.wait()

    return kernel


def fetch(step, tiles, pattern, selected, after):
    outs = [
        ((MAXSEL, CAP, TILE, TILE), BF16),
        ((PRODUCTS, ALL), BF16),
        ((RB_DEV, MAXSEL, TILE), F32),
    ]
    scratch = SCALARS + (pltpu.SemaphoreType.DMA((MAXSEL,)),)
    return call(
        fetch_kernel(step), outs, "hhha", (tiles, pattern, selected, after), scratch, 8 * 2**20, True
    )


def forward(hot_ref, blocks, picked_ref, out_ref):
    cells = jnp.dot(hot_ref[...], blocks, preferred_element_type=F32)
    sub = lax.broadcasted_iota(jnp.int32, (MAXSEL, TILE), 0)
    total = jnp.zeros((MAXSEL, TILE), F32)
    for n in range(MAXSEL):
        for s in range(0, CAP, 8):
            rows = [cells[n * CAP + t : n * CAP + t + 1] for t in range(s, s + 8)]
            lhs = jnp.concatenate([jnp.where(sub == n, row, 0.0) for row in rows], axis=1).astype(BF16)
            rhs = jnp.concatenate([picked_ref[n, t] for t in range(s, s + 8)], axis=1)
            total = total + lax.dot_general(
                lhs, rhs, (((1,), (1,)), ((), ())), preferred_element_type=F32
            )
    for m in range(N_MP):
        out_ref[m] = total


def predict_kernel(gathered_ref, picked_ref, hot_ref, out_ref):
    blocks = jnp.concatenate([gathered_ref[at(p, GATHER), 0:OWN, :] for p in range(N_RAY)], axis=0)
    forward(hot_ref, blocks, picked_ref, out_ref)


def dual_update(parts_ref, rays_ref, times_ref, pick_ref, new_rays_ref):
    predicted = parts_ref[0]
    for m in range(1, N_MP):
        predicted = predicted + parts_ref[m]
    rays = jnp.zeros((MAXSEL, TILE), F32)
    times = jnp.zeros((MAXSEL, TILE), F32)
    taken = jnp.zeros((MAXSEL, TILE), F32)
    for r in range(RB_DEV):
        pick = pick_ref[r]
        rays = rays + pick * rays_ref[r : r + 1, :]
        times = times + pick * times_ref[r : r + 1, :]
        taken = taken + pick
    fresh = (rays + dual_step * (predicted - times)) / (1.0 + dual_step)
    change = taken * (fresh - rays)
    for r in range(RB_DEV):
        new_rays_ref[r : r + 1, :] = rays_ref[r : r + 1, :] + jnp.sum(
            pick_ref[r] * change, axis=0, keepdims=True
        )
    return change


def products(change, picked_ref, n):
    sub = lax.broadcasted_iota(jnp.int32, (CAP, TILE), 0)
    row = change[n : n + 1]
    total = jnp.zeros((CAP, TILE), F32)
    for s in range(0, CAP, 8):
        lhs = jnp.concatenate(
            [jnp.where(sub == t, row, 0.0) for t in range(s, s + 8)], axis=1
        ).astype(BF16)
        rhs = picked_ref[n, s : s + 8].reshape(8 * TILE, TILE)
        total = total + jnp.dot(lhs, rhs, preferred_element_type=F32)
    return total


def share_kernel(
    parts_ref, rays_ref, times_ref, pick_ref, picked_ref, rest_ref, extra_ref, new_rays_ref, out_ref
):
    change = dual_update(parts_ref, rays_ref, times_ref, pick_ref, new_rays_ref)
    for n in range(0, MAXSEL, 2):
        pair = jnp.concatenate(
            [products(change, picked_ref, n), products(change, picked_ref, n + 1)], axis=0
        ).astype(BF16)
        for p in range(N_RAY):
            out_ref[p, n * CAP : (n + 2) * CAP, :] = pair
    rest = rest_ref[...].reshape(OWN, TILE).astype(BF16)
    extra = extra_ref[...].astype(BF16)
    for p in range(N_RAY):
        out_ref[p, PRODUCTS:EXTRA, :] = rest
        out_ref[p, EXTRA:SHARED, :] = extra


def image_kernel(
    shared_ref, gathered_ref, picked_ref, hot_ref, back_ref, edge_ref, out_ref, table_ref
):
    lane = lax.broadcasted_iota(jnp.int32, (1, TILE), 1)
    singles = []
    for p in range(N_RAY):
        rows = gathered_ref[at(p, GATHER), OWN:SENT, :].astype(F32)
        singles.append(rows[0:1] * OWN + rows[1:2])
    pairs = [jnp.where(lane < PRODUCTS, singles[p], singles[p + 1]) for p in range(0, N_RAY, 2)]
    group = 4
    chunk = group * OWN
    numbers = []
    terms = []
    for g in range(0, N_RAY, group):
        numbers.append(jnp.concatenate(pairs[g // 2 : g // 2 + 2], axis=1).astype(jnp.int32))
        terms.append(
            jnp.concatenate(
                [shared_ref[at(p, SHARE), 0:PRODUCTS, :] for p in range(g, g + group)], axis=0
            )
        )
    place = lax.broadcasted_iota(jnp.int32, (chunk, group * PRODUCTS), 0)
    sub = lax.broadcasted_iota(jnp.int32, (GY, TILE), 0)
    blocks = []
    for g in range(0, N_RAY, group):
        back = jnp.zeros((chunk, TILE), F32)
        for k in range(N_RAY // group):
            hot = jnp.where(place + g * OWN == numbers[k], 1.0, 0.0).astype(BF16)
            back = back + jnp.dot(hot, terms[k], preferred_element_type=F32)
        table_ref[g * OWN : g * OWN + chunk, :] = back
        for p in range(g, g + group):
            rows = slice(p * OWN, (p + 1) * OWN)
            rest = shared_ref[at(p, SHARE), PRODUCTS:EXTRA, :].astype(F32)
            field = gathered_ref[at(p, GATHER), 0:OWN, :].astype(F32) + (rest - gain * table_ref[rows, :])
            if p > 0:
                change = shared_ref[at(p - 1, SHARE), EXTRA:SHARED, :].astype(F32)
                field = field - (2.0 * primal_step) * jnp.concatenate(
                    [jnp.where(sub == 0, change[x : x + 1], 0.0) for x in range(GX)], axis=0
                )
            blocks.append(field)
    forward(
        hot_ref, jnp.concatenate([field.astype(BF16) for field in blocks], axis=0), picked_ref, out_ref
    )
    me = lax.axis_index("ray")
    back_ref[...] = table_ref[pl.ds(pl.multiple_of(me * OWN, OWN), OWN), :]
    for p in range(N_RAY):
        table_ref[p * OWN : (p + 1) * OWN, :] = blocks[p]
    before = jnp.maximum(me - 1, 0)
    for side, peer, row in ((0, before, GY - 1), (1, jnp.minimum(me + 1, N_RAY - 1), 0)):
        field = table_ref[pl.ds(pl.multiple_of(peer * OWN, OWN), OWN), :]
        for x in range(GX):
            edge_ref[side * GX + x : side * GX + x + 1, :] = field[x * GY + row : x * GY + row + 1]
    edge_ref[2 * GX : 6 * GX] = shared_ref[at(before, SHARE), EXTRA:SHARED, :].astype(F32)


def back_kernel(
    parts_ref, rays_ref, times_ref, pick_ref, picked_ref, hot_ref, far_any, near_ref, new_rays_ref, out_ref, same_ref
):
    same_ref[...] = near_ref[...]
    change = dual_update(parts_ref, rays_ref, times_ref, pick_ref, new_rays_ref)
    terms = jnp.concatenate([products(change, picked_ref, n) for n in range(MAXSEL)], axis=0)
    high = terms.astype(BF16)
    low = (terms - high.astype(F32)).astype(BF16)
    turned = (((0,), (0,)), ((), ()))
    image = lax.dot_general(hot_ref[...], high, turned, preferred_element_type=F32)
    image = image + lax.dot_general(hot_ref[...], low, turned, preferred_element_type=F32)
    for p in range(N_RAY):
        out_ref[at(p, LAST)] = image[p * OWN : (p + 1) * OWN].astype(BF16)


def swap(block, first):
    route = [(m, m + 1) for m in range(first, N_MP - 1, 2)]
    return lax.ppermute(block, "mp", route + [(b, a) for a, b in route])


def swap_far(block):
    return swap(block, 1)


def swap_near(block):
    return swap(block, 0)


def next_rows(gathered_ref):
    peer = jnp.minimum(lax.axis_index("ray") + 1, N_RAY - 1)
    high = gathered_ref[at(peer, GATHER), 0:OWN, :].astype(F32)
    low = gathered_ref[at(peer, GATHER), OWN:SENT, :].astype(F32)
    return [
        high[x * GY : x * GY + 1] + low[REST - OWN + x : REST - OWN + x + 1] for x in range(GX)
    ]


def first_edges_kernel(field_ref, dual_ref, gathered_ref, after_any, far_ref, near_ref):
    odd = (lax.axis_index("mp") & 1) == 1
    first = field_ref[0]
    last = field_ref[GX - 1]
    far_ref[0:GY] = jnp.where(odd, last, first)
    near_ref[0:GY] = jnp.where(odd, first, last)
    corner = jnp.broadcast_to(next_rows(gathered_ref)[GX - 1], (GY, TILE))
    far_ref[GY : 2 * GY] = corner
    near_ref[GY : 2 * GY] = corner
    for c in range(3):
        rows = slice((c + 2) * GY, (c + 3) * GY)
        far_ref[rows] = dual_ref[c, GX - 1]
        near_ref[rows] = dual_ref[c, GX - 1]


def x_halos(far_ref, near_ref):
    odd = (lax.axis_index("mp") & 1) == 1
    far, near = far_ref[...], near_ref[...]
    return jnp.where(odd, near, far), jnp.where(odd, far, near)


def tv_cells(here, ahead_x, ahead_y, dual, no_x, no_y):
    lane = lax.broadcasted_iota(jnp.int32, here.shape, len(here.shape) - 1)
    ahead_z = pltpu.roll(here, TILE - 1, len(here.shape) - 1)
    steps = (
        jnp.where(no_x, 0.0, ahead_x - here),
        jnp.where(no_y, 0.0, ahead_y - here),
        jnp.where(lane == TILE - 1, 0.0, ahead_z - here),
    )
    moved = [d + tv_step * g for d, g in zip(dual, steps)]
    length = jnp.sqrt(moved[0] * moved[0] + moved[1] * moved[1] + moved[2] * moved[2])
    scale = jnp.maximum(1.0, length / tv_weight)
    fresh = [m / scale for m in moved]
    return fresh, [a - b for a, b in zip(fresh, dual)]


def up_one(plane, row):
    sub = lax.broadcasted_iota(jnp.int32, plane.shape, 0)
    return jnp.where(sub == GY - 1, row, pltpu.roll(plane, GY - 1, 0))


def tv_step_all(field, dual, before, before_next, dual_before, behind, nexts, from_y):
    mp, ray = lax.axis_index("mp"), lax.axis_index("ray")
    sub = lax.broadcasted_iota(jnp.int32, (GY, TILE), 0)
    lane = lax.broadcasted_iota(jnp.int32, (GY, TILE), 1)
    end_x = (mp == N_MP - 1) & (sub >= 0)
    last_y = (sub == GY - 1) & (ray == N_RAY - 1)
    never = sub < 0

    halo, halo_change = tv_cells(
        before, field[0], up_one(before, before_next), dual_before, never, last_y
    )
    from_x = jnp.where(mp == 0, 0.0, halo_change[0])
    fresh, backs, second = [], [], []
    for x in range(GX):
        ahead = field[x + 1] if x + 1 < GX else behind
        no_x = end_x if x + 1 == GX else never
        new, change = tv_cells(
            field[x], ahead, up_one(field[x], nexts[x]), [d[x] for d in dual], no_x, last_y
        )
        comp_x = jnp.where(no_x, 0.0, change[0])
        comp_y = jnp.where(last_y, 0.0, change[1])
        comp_z = jnp.where(lane == TILE - 1, 0.0, change[2])
        back = from_x - comp_x
        back = back + (jnp.where(sub == 0, from_y[x], pltpu.roll(comp_y, 1, 0)) - comp_y)
        back = back + (jnp.where(lane == 0, 0.0, pltpu.roll(comp_z, 1, 1)) - comp_z)
        from_x = comp_x
        fresh.append(new)
        backs.append(back)
        second.append(comp_y)
    return fresh, backs, halo, second


def first_tv_kernel(
    field_ref, dual_ref, far_ref, near_ref, gathered_ref, image_ref,
    new_dual_ref, plane_ref, back_ref, base_ref, rest_ref, extra_ref,
):
    before, behind = x_halos(far_ref, near_ref)
    field = [field_ref[x] for x in range(GX)]
    fresh, backs, halo, second = tv_step_all(
        field,
        [[dual_ref[c, x] for x in range(GX)] for c in range(3)],
        before[0:GY], before[GY : GY + 1],
        [before[(c + 2) * GY : (c + 3) * GY] for c in range(3)],
        behind[0:GY], next_rows(gathered_ref), [0.0] * GX,
    )
    for x in range(GX):
        base = field[x] - primal_step * (image_ref[x] + 2.0 * backs[x])
        back_ref[x] = backs[x]
        base_ref[x] = base
        rest_ref[x] = base - field[x].astype(BF16).astype(F32)
        extra_ref[x : x + 1] = second[x][GY - 1 : GY]
        for c in range(3):
            new_dual_ref[c, x] = fresh[x][c]
            row = (c + 1) * GX + x
            extra_ref[row : row + 1] = fresh[x][c][GY - 1 : GY]
    for c in range(3):
        plane_ref[c] = halo[c]


def second_edges_kernel(
    base_ref, back_ref, edge_ref, image_ref, tv_ref, field_ref, new_image_ref, far_ref, near_ref
):
    odd = (lax.axis_index("mp") & 1) == 1
    sub = lax.broadcasted_iota(jnp.int32, (GY, TILE), 0)
    first_y = (sub == 0) & (lax.axis_index("ray") > 0)
    field = []
    for x in range(GX):
        back = back_ref[x * GY : (x + 1) * GY]
        from_y = jnp.where(first_y, edge_ref[2 * GX + x : 2 * GX + x + 1], 0.0)
        field.append(base_ref[x] - (gain * back + (2.0 * primal_step) * from_y))
        field_ref[x] = field[x]
        new_image_ref[x] = image_ref[x] + back + (tv_ref[x] + from_y)
    edge = edge_ref[0 : 2 * GX]
    first = jnp.concatenate([field[0], edge], axis=0)
    last = jnp.concatenate([field[GX - 1], edge], axis=0)
    far_ref[...] = jnp.where(odd, last, first)
    near_ref[...] = jnp.where(odd, first, last)


def second_tv_kernel(
    field_ref, dual_ref, plane_ref, far_ref, near_ref, edge_ref, new_dual_ref, back_ref
):
    before, behind = x_halos(far_ref, near_ref)
    edge = edge_ref[...]
    ray = lax.axis_index("ray")
    end_x = lax.axis_index("mp") == N_MP - 1
    field = [field_ref[x] for x in range(GX)]
    sub = lax.broadcasted_iota(jnp.int32, (2 * GX, TILE), 0)
    rows = edge[0 : 2 * GX]
    ahead_x = jnp.where(sub == GX - 1, behind[GY : GY + 1], pltpu.roll(rows, 2 * GX - 1, 0))
    ahead_y = jnp.concatenate([field[x][0:1] for x in range(GX)] * 2, axis=0)
    dual_rows = [
        jnp.concatenate([edge[(c + 3) * GX : (c + 4) * GX]] * 2, axis=0) for c in range(3)
    ]
    _, change = tv_cells(
        rows, ahead_x, ahead_y, dual_rows, (sub == GX - 1) & end_x, sub < 0
    )
    from_y = jnp.where(ray == 0, 0.0, change[1])
    fresh, backs, _, _ = tv_step_all(
        field,
        [[dual_ref[c, x] for x in range(GX)] for c in range(3)],
        before[0:GY], before[GY + 2 * GX - 1 : GY + 2 * GX],
        [plane_ref[c] for c in range(3)],
        behind[0:GY],
        [edge[GX + x : GX + x + 1] for x in range(GX)],
        [from_y[x : x + 1] for x in range(GX)],
    )
    for x in range(GX):
        back_ref[x] = backs[x]
        for c in range(3):
            new_dual_ref[c, x] = fresh[x][c]


def on_device(
    slowness, accumulated, extrapolated, tv_dual, ray_dual, traveltimes, tiles, pattern, selected
):
    pattern = pattern.T
    busy = 8 * 2**20
    grid = (GRID, F32)
    duals = ((3,) + GRID, F32)
    swapped = ((GY + 2 * GX, TILE), F32)

    field, sent = call(
        start_kernel, [grid, ((N_RAY, SENT, TILE), BF16)], "hhhh",
        (slowness, extrapolated, pattern, selected),
        (pltpu.VMEM(GRID, F32), pltpu.VMEM(GRID, F32), pltpu.SemaphoreType.DMA((2,))) + SCALARS,
    )
    gathered = exchange(sent, "ray", GATHER)
    picked, hot, pick = fetch(0, tiles, pattern, selected, field)
    (partial_value,) = call(predict_kernel, [SUMS], "vvv", (gathered, picked, hot))
    parts = exchange(partial_value, "mp", SUM_1)

    far, near = call(
        first_edges_kernel, [((5 * GY, TILE), F32)] * 2, "vvva",
        (field, tv_dual, gathered, partial_value), busy=busy,
    )
    far, near = swap_far(far), swap_near(near)
    dual, dual_plane, tv_back, base, rest, extra = call(
        first_tv_kernel,
        [duals, ((3, GY, TILE), F32), grid, grid, grid, ((4 * GX, TILE), F32)],
        "vvvvvv", (field, tv_dual, far, near, gathered, accumulated), busy=busy,
    )
    picked_2, hot_2, pick_2 = fetch(1, tiles, pattern, selected, partial_value)

    rays, share = call(
        share_kernel, [RAYS, ((N_RAY, SHARED, TILE), BF16)], "vvvvvvv",
        (parts, ray_dual, traveltimes, pick, picked, rest, extra),
    )
    shared = exchange(share, "ray", SHARE)
    back, edge, partial_value = call(
        image_kernel, [((OWN, TILE), F32), ((6 * GX, TILE), F32), SUMS], "vvvv",
        (shared, gathered, picked_2, hot_2), (pltpu.VMEM((ALL, TILE), F32),),
    )
    parts = exchange(partial_value, "mp", SUM_2)

    field, image, far, near = call(
        second_edges_kernel, [grid, grid, swapped, swapped], "vvvvv",
        (base, back, edge, accumulated, tv_back), busy=busy,
    )
    far = swap_far(far)
    rays, share, near = call(
        back_kernel, [RAYS, ((N_RAY, OWN, TILE), BF16), swapped], "vvvvvvav",
        (parts, rays, traveltimes, pick_2, picked_2, hot_2, far, near),
    )
    shared = exchange(share, "ray", LAST)
    near = swap_near(near)
    dual, tv_back = call(
        second_tv_kernel, [duals, grid], "vvvvvv",
        (field, dual, dual_plane, far, near, edge), busy=busy,
    )
    back = jnp.sum(shared.astype(F32), axis=0).reshape(GRID)
    image = image + back + tv_back
    image_bar = image + extrapolation * back + tv_back
    return (field, rays, dual, image, image_bar)


def solution(mesh):
    in_specs = (
        P("mp", "ray", None),
        P("mp", "ray", None),
        P("mp", "ray", None),
        P(None, "mp", "ray", None),
        P("ray", None),
        P("ray", None),
        P("ray", "mp", None, None),
        P("ray", "mp"),
        P(None, "ray"),
    )
    out_specs = (
        P("mp", "ray", None),
        P("ray", None),
        P(None, "mp", "ray", None),
        P("mp", "ray", None),
        P("mp", "ray", None),
    )
    return jax.shard_map(
        on_device, mesh=mesh, in_specs=in_specs, out_specs=out_specs, check_vma=False
    )
```

```python
import jax
import jax.numpy as jnp
from jax import lax
from jax.experimental import pallas as pl
from jax.experimental.pallas import tpu as pltpu
from jax.sharding import PartitionSpec as P

TILE = 128
GX = 4
GY = 8
RB_DEV = 16
CAP = 8
MAXSEL = 8
N_RAY = 16
N_MP = 32
OWN = GX * GY
ALL = N_RAY * OWN
PRODUCTS = MAXSEL * CAP
SENT = OWN + 16
REST = OWN + 8
EXTRA = PRODUCTS + OWN
SHARED = EXTRA + 16
GATHER, SUM_1, SHARE, SUM_2, LAST = 9, 19, 5, 19, 10

primal_step = 0.5
dual_step = 0.5
tv_step = 0.25
tv_weight = 0.3
extrapolation = 2.0 * RB_DEV / (MAXSEL + 1)
gain = primal_step * (1.0 + extrapolation)

F32 = jnp.float32
BF16 = jnp.bfloat16
GRID = (GX, GY, TILE)
SUMS = ((N_MP, MAXSEL, TILE), F32)
RAYS = ((RB_DEV, TILE), F32)


def exchange(copies, axis, first):
    size = N_RAY if axis == "ray" else N_MP
    groups = [[(first + i) % size for i in range(size)]]
    return lax.all_to_all(copies, axis, 0, 0, tiled=True, axis_index_groups=groups)


def at(peer, first):
    return (peer + (N_RAY - first)) & (N_RAY - 1)


def call(kernel, outs, places, args, scratch=(), busy=0, keep=False):
    spaces = {"v": pltpu.VMEM, "h": pltpu.HBM, "a": pl.ANY}
    cost = pl.CostEstimate(flops=0, bytes_accessed=busy, transcendentals=0) if busy else None
    args = [
        pltpu.with_memory_space_constraint(arg, pltpu.HBM) if place == "h" else arg
        for arg, place in zip(args, places)
    ]
    return pl.pallas_call(
        kernel,
        out_shape=[
            pltpu.VMEM(shape, dtype) if keep else jax.ShapeDtypeStruct(shape, dtype)
            for shape, dtype in outs
        ],
        in_specs=[pl.BlockSpec(memory_space=spaces[c]) for c in places],
        out_specs=[pl.BlockSpec(memory_space=pltpu.VMEM) for _ in outs],
        scratch_shapes=list(scratch),
        cost_estimate=cost,
        compiler_params=pltpu.CompilerParams(vmem_limit_bytes=20 * 1024 * 1024),
    )(*args)


SCALARS = (
    pltpu.SMEM((CAP, RB_DEV), jnp.int32),
    pltpu.SMEM((2, RB_DEV), jnp.int32),
    pltpu.SMEM((RB_DEV,), jnp.int32),
    pltpu.SemaphoreType.DMA((2,)),
)


def scalar_copies(pattern_hbm, selected_hbm, pattern_ref, selected_ref, sems):
    return [
        pltpu.make_async_copy(pattern_hbm, pattern_ref, sems.at[0]),
        pltpu.make_async_copy(selected_hbm, selected_ref, sems.at[1]),
    ]


def block_number(pattern):
    row = pattern & (GY * N_RAY - 1)
    plane = lax.shift_right_logical(pattern, 7)
    return lax.shift_right_logical(row, 3) * OWN + plane * GY + (row & (GY - 1))


def list_selected(selected_ref, step, list_ref):
    for n in range(MAXSEL):
        list_ref[n] = jnp.int32(0)
    count = jnp.int32(0)
    for r in range(RB_DEV):
        list_ref[count] = jnp.int32(r)
        count = count + selected_ref[step, r]
    return count


def start_kernel(
    slowness_hbm, bar_hbm, pattern_hbm, selected_hbm, field_ref, sent_ref,
    slowness_ref, bar_ref, sems, pattern_ref, selected_ref, list_ref, scalar_sems,
):
    copies = scalar_copies(pattern_hbm, selected_hbm, pattern_ref, selected_ref, scalar_sems)
    copies.append(pltpu.make_async_copy(slowness_hbm, slowness_ref, sems.at[0]))
    copies.append(pltpu.make_async_copy(bar_hbm, bar_ref, sems.at[1]))
    for copy in copies:
        copy.start()
    copies[0].wait()
    copies[1].wait()
    list_selected(selected_ref, 0, list_ref)
    lane = lax.broadcasted_iota(jnp.int32, (8, TILE), 1) & (PRODUCTS - 1)
    sub = lax.broadcasted_iota(jnp.int32, (8, TILE), 0)
    numbers = jnp.zeros((8, TILE), jnp.int32)
    for n in range(MAXSEL):
        r = list_ref[n]
        for s in range(CAP):
            numbers = jnp.where(lane == n * CAP + s, block_number(pattern_ref[s, r]), numbers)
    numbers = jnp.where(sub == 0, lax.shift_right_logical(numbers, 5), numbers & (OWN - 1))
    copies[2].wait()
    copies[3].wait()
    field = slowness_ref[...] - primal_step * bar_ref[...]
    field_ref[...] = field
    field = field.reshape(OWN, TILE)
    rounded = field.astype(BF16)
    low = field - rounded.astype(F32)
    rest = jnp.zeros((8, TILE), F32)
    for x in range(GX):
        rest = jnp.where(sub == x, low[x * GY : x * GY + 1], rest)
    tail = jnp.concatenate([numbers.astype(F32), rest], axis=0).astype(BF16)
    for p in range(N_RAY):
        sent_ref[p, 0:OWN, :] = rounded
        sent_ref[p, OWN:SENT, :] = tail


def fetch_kernel(step):
    def kernel(
        tiles_hbm, pattern_hbm, selected_hbm, after_ref, picked_ref, hot_ref, pick_ref,
        pattern_ref, selected_ref, list_ref, scalar_sems, sems,
    ):
        scalars = scalar_copies(pattern_hbm, selected_hbm, pattern_ref, selected_ref, scalar_sems)
        for copy in scalars:
            copy.start()
        for copy in scalars:
            copy.wait()
        count = list_selected(selected_ref, step, list_ref)
        copies = [
            pltpu.make_async_copy(tiles_hbm.at[list_ref[n]], picked_ref.at[n], sems.at[n])
            for n in range(MAXSEL)
        ]
        for copy in copies:
            copy.start()
        sub = lax.broadcasted_iota(jnp.int32, (MAXSEL, TILE), 0)
        lane = lax.broadcasted_iota(jnp.int32, (2 * CAP, TILE), 1)
        for n in range(0, MAXSEL, 2):
            halves = []
            for m in (n, n + 1):
                r = list_ref[m]
                numbers = jnp.zeros((CAP, TILE), jnp.int32)
                for s in range(CAP):
                    numbers = jnp.where(sub == s, block_number(pattern_ref[s, r]), numbers)
                halves.append(numbers)
            numbers = jnp.concatenate(halves, axis=0)
            for c in range(ALL // TILE):
                hot = jnp.where(numbers == lane + c * TILE, 1.0, 0.0).astype(BF16)
                hot_ref[n * CAP : (n + 2) * CAP, c * TILE : (c + 1) * TILE] = hot
        listed = jnp.full((MAXSEL, TILE), RB_DEV, jnp.int32)
        for n in range(MAXSEL):
            listed = jnp.where((sub == n) & (sub < count), list_ref[n], listed)
        for r in range(RB_DEV):
            pick_ref[r] = jnp.where(listed == r, 1.0, 0.0)
        for copy in copies:
            copy.wait()

    return kernel


def fetch(step, tiles, pattern, selected, after):
    outs = [
        ((MAXSEL, CAP, TILE, TILE), BF16),
        ((PRODUCTS, ALL), BF16),
        ((RB_DEV, MAXSEL, TILE), F32),
    ]
    scratch = SCALARS + (pltpu.SemaphoreType.DMA((MAXSEL,)),)
    return call(
        fetch_kernel(step), outs, "hhha", (tiles, pattern, selected, after), scratch, 8 * 2**20, True
    )


def forward(hot_ref, blocks, picked_ref):
    cells = jnp.dot(hot_ref[...], blocks, preferred_element_type=F32)
    sub = lax.broadcasted_iota(jnp.int32, (MAXSEL, TILE), 0)
    total = jnp.zeros((MAXSEL, TILE), F32)
    for n in range(MAXSEL):
        for s in range(0, CAP, 8):
            rows = [cells[n * CAP + t : n * CAP + t + 1] for t in range(s, s + 8)]
            lhs = jnp.concatenate([jnp.where(sub == n, row, 0.0) for row in rows], axis=1).astype(BF16)
            rhs = jnp.concatenate([picked_ref[n, t] for t in range(s, s + 8)], axis=1)
            total = total + lax.dot_general(
                lhs, rhs, (((1,), (1,)), ((), ())), preferred_element_type=F32
            )
    return total


def predict_kernel(gathered_ref, picked_ref, hot_ref, out_ref):
    blocks = jnp.concatenate([gathered_ref[at(p, GATHER), 0:OWN, :] for p in range(N_RAY)], axis=0)
    total = forward(hot_ref, blocks, picked_ref)
    for m in range(N_MP):
        out_ref[m] = total


def dual_update(predicted, rays_ref, times_ref, pick_ref, new_rays_ref):
    rays = jnp.zeros((MAXSEL, TILE), F32)
    times = jnp.zeros((MAXSEL, TILE), F32)
    taken = jnp.zeros((MAXSEL, TILE), F32)
    for r in range(RB_DEV):
        pick = pick_ref[r]
        rays = rays + pick * rays_ref[r : r + 1, :]
        times = times + pick * times_ref[r : r + 1, :]
        taken = taken + pick
    fresh = (rays + dual_step * (predicted - times)) / (1.0 + dual_step)
    change = taken * (fresh - rays)
    for r in range(RB_DEV):
        new_rays_ref[r : r + 1, :] = rays_ref[r : r + 1, :] + jnp.sum(
            pick_ref[r] * change, axis=0, keepdims=True
        )
    return change


def products(change, picked_ref, n):
    sub = lax.broadcasted_iota(jnp.int32, (CAP, TILE), 0)
    row = change[n : n + 1]
    total = jnp.zeros((CAP, TILE), F32)
    for s in range(0, CAP, 8):
        lhs = jnp.concatenate(
            [jnp.where(sub == t, row, 0.0) for t in range(s, s + 8)], axis=1
        ).astype(BF16)
        rhs = picked_ref[n, s : s + 8].reshape(8 * TILE, TILE)
        total = total + jnp.dot(lhs, rhs, preferred_element_type=F32)
    return total


def share_kernel(
    parts_ref, rays_ref, times_ref, pick_ref, picked_ref, rest_ref, extra_ref, new_rays_ref, out_ref
):
    predicted = parts_ref[0]
    for m in range(1, N_MP):
        predicted = predicted + parts_ref[m]
    change = dual_update(predicted, rays_ref, times_ref, pick_ref, new_rays_ref)
    for n in range(0, MAXSEL, 2):
        pair = jnp.concatenate(
            [products(change, picked_ref, n), products(change, picked_ref, n + 1)], axis=0
        ).astype(BF16)
        for p in range(N_RAY):
            out_ref[p, n * CAP : (n + 2) * CAP, :] = pair
    rest = rest_ref[...].reshape(OWN, TILE).astype(BF16)
    extra = extra_ref[...].astype(BF16)
    for p in range(N_RAY):
        out_ref[p, PRODUCTS:EXTRA, :] = rest
        out_ref[p, EXTRA:SHARED, :] = extra


def image_kernel(
    shared_ref, gathered_ref, picked_ref, hot_ref, first_ref, base_ref, image_ref, tv_ref,
    field_ref, new_image_ref, edge_ref, out_ref, table_ref,
):
    lane = lax.broadcasted_iota(jnp.int32, (1, TILE), 1)
    singles = []
    for p in range(N_RAY):
        rows = gathered_ref[at(p, GATHER), OWN:SENT, :].astype(F32)
        singles.append(rows[0:1] * OWN + rows[1:2])
    pairs = [jnp.where(lane < PRODUCTS, singles[p], singles[p + 1]) for p in range(0, N_RAY, 2)]
    group = 4
    chunk = group * OWN
    numbers = []
    terms = []
    for g in range(0, N_RAY, group):
        numbers.append(jnp.concatenate(pairs[g // 2 : g // 2 + 2], axis=1).astype(jnp.int32))
        terms.append(
            jnp.concatenate(
                [shared_ref[at(p, SHARE), 0:PRODUCTS, :] for p in range(g, g + group)], axis=0
            )
        )
    place = lax.broadcasted_iota(jnp.int32, (chunk, group * PRODUCTS), 0)
    sub = lax.broadcasted_iota(jnp.int32, (GY, TILE), 0)
    blocks = []
    for g in range(0, N_RAY, group):
        back = jnp.zeros((chunk, TILE), F32)
        for k in range(N_RAY // group):
            hot = jnp.where(place + g * OWN == numbers[k], 1.0, 0.0).astype(BF16)
            back = back + jnp.dot(hot, terms[k], preferred_element_type=F32)
        table_ref[g * OWN : g * OWN + chunk, :] = back
        for p in range(g, g + group):
            rows = slice(p * OWN, (p + 1) * OWN)
            rest = shared_ref[at(p, SHARE), PRODUCTS:EXTRA, :].astype(F32)
            field = gathered_ref[at(p, GATHER), 0:OWN, :].astype(F32) + (rest - gain * table_ref[rows, :])
            if p > 0:
                change = shared_ref[at(p - 1, SHARE), EXTRA:SHARED, :].astype(F32)
                field = field - (2.0 * primal_step) * jnp.concatenate(
                    [jnp.where(sub == 0, change[x : x + 1], 0.0) for x in range(GX)], axis=0
                )
            blocks.append(field)
    total = forward(
        hot_ref, jnp.concatenate([field.astype(BF16) for field in blocks], axis=0), picked_ref
    )
    me, mp = lax.axis_index("ray"), lax.axis_index("mp")
    back = table_ref[pl.ds(pl.multiple_of(me * OWN, OWN), OWN), :]
    for p in range(N_RAY):
        table_ref[p * OWN : (p + 1) * OWN, :] = blocks[p]
    before = jnp.maximum(me - 1, 0)
    for side, peer, row in ((0, before, GY - 1), (1, jnp.minimum(me + 1, N_RAY - 1), 0)):
        field = table_ref[pl.ds(pl.multiple_of(peer * OWN, OWN), OWN), :]
        for x in range(GX):
            edge_ref[side * GX + x : side * GX + x + 1, :] = field[x * GY + row : x * GY + row + 1]
    extra = shared_ref[at(before, SHARE), EXTRA:SHARED, :].astype(F32)
    edge_ref[2 * GX : 6 * GX] = extra
    first_y = (sub == 0) & (me > 0)
    field = []
    for x in range(GX):
        own = back[x * GY : (x + 1) * GY]
        from_y = jnp.where(first_y, extra[x : x + 1], 0.0)
        field.append(base_ref[x] - (gain * own + (2.0 * primal_step) * from_y))
        field_ref[x] = field[x]
        new_image_ref[x] = image_ref[x] + own + (tv_ref[x] + from_y)
    high = total.astype(BF16).astype(F32)
    ends = [
        jnp.concatenate([high, total - high, field[x] - first_ref[x]], axis=0) for x in (0, GX - 1)
    ]
    for j in range(N_MP):
        out_ref[j] = jnp.where((SUM_2 + j) % N_MP == mp + 1, ends[1], ends[0]).astype(BF16)


def back_kernel(
    parts_ref, rays_ref, times_ref, pick_ref, picked_ref, hot_ref, far_ref, near_ref, new_rays_ref, out_ref, planes_ref
):
    mp = lax.axis_index("mp")
    before, behind = x_halos(far_ref, near_ref)
    step = parts_ref[(mp + (N_MP - 1 - SUM_2)) & (N_MP - 1)].astype(F32)
    before = before[0:GY] + step[2 * MAXSEL :]
    step = parts_ref[(mp + (N_MP + 1 - SUM_2)) & (N_MP - 1)].astype(F32)
    behind = behind[0:GY] + step[2 * MAXSEL :]
    planes_ref[0] = before
    planes_ref[1] = behind
    corners = [before[0:1], behind[GY - 1 : GY]]
    highs = [corner.astype(BF16).astype(F32) for corner in corners]
    sub = lax.broadcasted_iota(jnp.int32, (16, TILE), 0)
    tail = jnp.zeros((16, TILE), F32)
    for i in range(2):
        tail = jnp.where(sub == 2 * i, highs[i], tail)
        tail = jnp.where(sub == 2 * i + 1, corners[i] - highs[i], tail)
    tail = tail.astype(BF16)
    halves = parts_ref[0].astype(F32)
    for m in range(1, N_MP):
        halves = halves + parts_ref[m].astype(F32)
    predicted = halves[0:MAXSEL] + halves[MAXSEL : 2 * MAXSEL]
    change = dual_update(predicted, rays_ref, times_ref, pick_ref, new_rays_ref)
    terms = jnp.concatenate([products(change, picked_ref, n) for n in range(MAXSEL)], axis=0)
    high = terms.astype(BF16)
    low = (terms - high.astype(F32)).astype(BF16)
    turned = (((0,), (0,)), ((), ()))
    image = lax.dot_general(hot_ref[...], high, turned, preferred_element_type=F32)
    image = image + lax.dot_general(hot_ref[...], low, turned, preferred_element_type=F32)
    for p in range(N_RAY):
        out_ref[at(p, LAST), 0:OWN] = image[p * OWN : (p + 1) * OWN].astype(BF16)
        out_ref[at(p, LAST), OWN:] = tail


def swap(block, first):
    route = [(m, m + 1) for m in range(first, N_MP - 1, 2)]
    return lax.ppermute(block, "mp", route + [(b, a) for a, b in route])


def swap_far(block):
    return swap(block, 1)


def swap_near(block):
    return swap(block, 0)


def next_rows(gathered_ref):
    peer = jnp.minimum(lax.axis_index("ray") + 1, N_RAY - 1)
    high = gathered_ref[at(peer, GATHER), 0:OWN, :].astype(F32)
    low = gathered_ref[at(peer, GATHER), OWN:SENT, :].astype(F32)
    return [
        high[x * GY : x * GY + 1] + low[REST - OWN + x : REST - OWN + x + 1] for x in range(GX)
    ]


def first_edges_kernel(field_ref, dual_ref, gathered_ref, after_any, far_ref, near_ref):
    odd = (lax.axis_index("mp") & 1) == 1
    first = field_ref[0]
    last = field_ref[GX - 1]
    far_ref[0:GY] = jnp.where(odd, last, first)
    near_ref[0:GY] = jnp.where(odd, first, last)
    corner = jnp.broadcast_to(next_rows(gathered_ref)[GX - 1], (GY, TILE))
    far_ref[GY : 2 * GY] = corner
    near_ref[GY : 2 * GY] = corner
    for c in range(3):
        rows = slice((c + 2) * GY, (c + 3) * GY)
        far_ref[rows] = dual_ref[c, GX - 1]
        near_ref[rows] = dual_ref[c, GX - 1]


def x_halos(far_ref, near_ref):
    odd = (lax.axis_index("mp") & 1) == 1
    far, near = far_ref[...], near_ref[...]
    return jnp.where(odd, near, far), jnp.where(odd, far, near)


def tv_cells(here, ahead_x, ahead_y, dual, no_x, no_y):
    lane = lax.broadcasted_iota(jnp.int32, here.shape, len(here.shape) - 1)
    ahead_z = pltpu.roll(here, TILE - 1, len(here.shape) - 1)
    steps = (
        jnp.where(no_x, 0.0, ahead_x - here),
        jnp.where(no_y, 0.0, ahead_y - here),
        jnp.where(lane == TILE - 1, 0.0, ahead_z - here),
    )
    moved = [d + tv_step * g for d, g in zip(dual, steps)]
    length = jnp.sqrt(moved[0] * moved[0] + moved[1] * moved[1] + moved[2] * moved[2])
    scale = jnp.maximum(1.0, length / tv_weight)
    fresh = [m / scale for m in moved]
    return fresh, [a - b for a, b in zip(fresh, dual)]


def up_one(plane, row):
    sub = lax.broadcasted_iota(jnp.int32, plane.shape, 0)
    return jnp.where(sub == GY - 1, row, pltpu.roll(plane, GY - 1, 0))


def plane_before(before, before_next, dual, first):
    sub = lax.broadcasted_iota(jnp.int32, (GY, TILE), 0)
    last_y = (sub == GY - 1) & (lax.axis_index("ray") == N_RAY - 1)
    fresh, change = tv_cells(before, first, up_one(before, before_next), dual, sub < 0, last_y)
    return fresh, jnp.where(lax.axis_index("mp") == 0, 0.0, change[0])


def tv_step_all(field, dual, behind, nexts, from_x):
    mp, ray = lax.axis_index("mp"), lax.axis_index("ray")
    sub = lax.broadcasted_iota(jnp.int32, (GY, TILE), 0)
    lane = lax.broadcasted_iota(jnp.int32, (GY, TILE), 1)
    end_x = (mp == N_MP - 1) & (sub >= 0)
    last_y = (sub == GY - 1) & (ray == N_RAY - 1)
    never = sub < 0
    fresh, backs, second = [], [], []
    for x in range(GX):
        ahead = field[x + 1] if x + 1 < GX else behind
        no_x = end_x if x + 1 == GX else never
        new, change = tv_cells(
            field[x], ahead, up_one(field[x], nexts[x]), [d[x] for d in dual], no_x, last_y
        )
        comp_x = jnp.where(no_x, 0.0, change[0])
        comp_y = jnp.where(last_y, 0.0, change[1])
        comp_z = jnp.where(lane == TILE - 1, 0.0, change[2])
        back = from_x - comp_x
        back = back + (jnp.where(sub == 0, 0.0, pltpu.roll(comp_y, 1, 0)) - comp_y)
        back = back + (jnp.where(lane == 0, 0.0, pltpu.roll(comp_z, 1, 1)) - comp_z)
        from_x = comp_x
        fresh.append(new)
        backs.append(back)
        second.append(comp_y)
    return fresh, backs, second


def first_tv_kernel(
    field_ref, dual_ref, far_ref, near_ref, gathered_ref, image_ref,
    new_dual_ref, plane_ref, back_ref, base_ref, rest_ref, extra_ref,
):
    before, behind = x_halos(far_ref, near_ref)
    field = [field_ref[x] for x in range(GX)]
    halo, from_x = plane_before(
        before[0:GY], before[GY : GY + 1],
        [before[(c + 2) * GY : (c + 3) * GY] for c in range(3)], field[0],
    )
    fresh, backs, second = tv_step_all(
        field,
        [[dual_ref[c, x] for x in range(GX)] for c in range(3)],
        behind[0:GY], next_rows(gathered_ref), from_x,
    )
    for x in range(GX):
        base = field[x] - primal_step * (image_ref[x] + 2.0 * backs[x])
        back_ref[x] = backs[x]
        base_ref[x] = base
        rest_ref[x] = base - field[x].astype(BF16).astype(F32)
        extra_ref[x : x + 1] = second[x][GY - 1 : GY]
        for c in range(3):
            new_dual_ref[c, x] = fresh[x][c]
            row = (c + 1) * GX + x
            extra_ref[row : row + 1] = fresh[x][c][GY - 1 : GY]
    for c in range(3):
        plane_ref[c] = halo[c]


def second_tv_kernel(field_ref, dual_ref, planes_ref, edge_ref, new_dual_ref, back_ref):
    edge = edge_ref[...]
    fresh, backs, _ = tv_step_all(
        [field_ref[x] for x in range(GX)],
        [[dual_ref[c, x] for x in range(GX)] for c in range(3)],
        planes_ref[1], [edge[GX + x : GX + x + 1] for x in range(GX)], 0.0,
    )
    for x in range(GX):
        back_ref[x] = backs[x]
        for c in range(3):
            new_dual_ref[c, x] = fresh[x][c]


def last_kernel(
    shared_ref, field_ref, planes_ref, dual_plane_ref, edge_ref, image_ref, tv_ref, out_ref, bar_ref
):
    ray = lax.axis_index("ray")
    above = shared_ref[at(jnp.minimum(ray + 1, N_RAY - 1), LAST), OWN:].astype(F32)
    below = shared_ref[at(jnp.maximum(ray - 1, 0), LAST), OWN:].astype(F32)
    field = [field_ref[x] for x in range(GX)]
    _, from_x = plane_before(
        planes_ref[0], above[0:1] + above[1:2], [dual_plane_ref[c] for c in range(3)], field[0]
    )
    edge = edge_ref[...]
    sub = lax.broadcasted_iota(jnp.int32, (2 * GX, TILE), 0)
    rows = edge[0 : 2 * GX]
    ahead_x = jnp.where(sub == GX - 1, below[2:3] + below[3:4], pltpu.roll(rows, 2 * GX - 1, 0))
    ahead_y = jnp.concatenate([field[x][0:1] for x in range(GX)] * 2, axis=0)
    dual_rows = [
        jnp.concatenate([edge[(c + 3) * GX : (c + 4) * GX]] * 2, axis=0) for c in range(3)
    ]
    end_x = lax.axis_index("mp") == N_MP - 1
    _, change = tv_cells(rows, ahead_x, ahead_y, dual_rows, (sub == GX - 1) & end_x, sub < 0)
    from_y = jnp.where(ray == 0, 0.0, change[1])

    back = shared_ref[0, 0:OWN].astype(F32)
    for p in range(1, N_RAY):
        back = back + shared_ref[p, 0:OWN].astype(F32)
    for x in range(GX):
        tv_back = tv_ref[x] + jnp.where(sub == 0, from_y[x : x + 1], 0.0)
        if x == 0:
            tv_back = tv_back + from_x
        own = back[x * GY : (x + 1) * GY]
        image = image_ref[x] + own + tv_back
        out_ref[x] = image
        bar_ref[x] = image + extrapolation * own + tv_back


def on_device(
    slowness, accumulated, extrapolated, tv_dual, ray_dual, traveltimes, tiles, pattern, selected
):
    pattern = pattern.T
    busy = 8 * 2**20
    grid = (GRID, F32)
    duals = ((3,) + GRID, F32)

    field, sent = call(
        start_kernel, [grid, ((N_RAY, SENT, TILE), BF16)], "hhhh",
        (slowness, extrapolated, pattern, selected),
        (pltpu.VMEM(GRID, F32), pltpu.VMEM(GRID, F32), pltpu.SemaphoreType.DMA((2,))) + SCALARS,
    )
    gathered = exchange(sent, "ray", GATHER)
    picked, hot, pick = fetch(0, tiles, pattern, selected, field)
    (partial_value,) = call(predict_kernel, [SUMS], "vvv", (gathered, picked, hot))
    parts = exchange(partial_value, "mp", SUM_1)

    far, near = call(
        first_edges_kernel, [((5 * GY, TILE), F32)] * 2, "vvva",
        (field, tv_dual, gathered, partial_value), busy=busy,
    )
    far, near = swap_far(far), swap_near(near)
    dual, dual_plane, tv_back, base, rest, extra = call(
        first_tv_kernel,
        [duals, ((3, GY, TILE), F32), grid, grid, grid, ((4 * GX, TILE), F32)],
        "vvvvvv", (field, tv_dual, far, near, gathered, accumulated), busy=busy,
    )
    picked_2, hot_2, pick_2 = fetch(1, tiles, pattern, selected, partial_value)

    rays, share = call(
        share_kernel, [RAYS, ((N_RAY, SHARED, TILE), BF16)], "vvvvvvv",
        (parts, ray_dual, traveltimes, pick, picked, rest, extra),
    )
    shared = exchange(share, "ray", SHARE)
    field, image, edge, partial_value = call(
        image_kernel,
        [grid, grid, ((6 * GX, TILE), F32), ((N_MP, 2 * MAXSEL + GY, TILE), BF16)], "vvvvvvvv",
        (shared, gathered, picked_2, hot_2, field, base, accumulated, tv_back),
        (pltpu.VMEM((ALL, TILE), F32),),
    )
    parts = exchange(partial_value, "mp", SUM_2)
    rays, share, planes = call(
        back_kernel, [RAYS, ((N_RAY, OWN + 16, TILE), BF16), ((2, GY, TILE), F32)], "vvvvvvvv",
        (parts, rays, traveltimes, pick_2, picked_2, hot_2, far, near),
    )
    shared = exchange(share, "ray", LAST)
    dual, tv_back = call(
        second_tv_kernel, [duals, grid], "vvvv", (field, dual, planes, edge), busy=busy
    )
    image, image_bar = call(
        last_kernel, [grid, grid], "vvvvvvv",
        (shared, field, planes, dual_plane, edge, image, tv_back),
    )
    return (field, rays, dual, image, image_bar)


def solution(mesh):
    in_specs = (
        P("mp", "ray", None),
        P("mp", "ray", None),
        P("mp", "ray", None),
        P(None, "mp", "ray", None),
        P("ray", None),
        P("ray", None),
        P("ray", "mp", None, None),
        P("ray", "mp"),
        P(None, "ray"),
    )
    out_specs = (
        P("mp", "ray", None),
        P("ray", None),
        P(None, "mp", "ray", None),
        P("mp", "ray", None),
        P("mp", "ray", None),
    )
    return jax.shard_map(
        on_device, mesh=mesh, in_specs=in_specs, out_specs=out_specs, check_vma=False
    )
```

```python
import jax
import jax.numpy as jnp
from jax import lax
from jax.experimental import pallas as pl
from jax.experimental.pallas import tpu as pltpu
from jax.sharding import PartitionSpec as P

TILE = 128
GX = 4
GY = 8
RB_DEV = 16
CAP = 8
MAXSEL = 8
N_RAY = 16
N_MP = 32
OWN = GX * GY
ALL = N_RAY * OWN
PRODUCTS = MAXSEL * CAP
SENT = OWN + 8
REST = OWN + 4
EXTRA = PRODUCTS + OWN
SHARED = EXTRA + 8
GATHER, SUM_1, SHARE, SUM_2, LAST = 9, 19, 5, 19, 10

primal_step = 0.5
dual_step = 0.5
tv_step = 0.25
tv_weight = 0.3
extrapolation = 2.0 * RB_DEV / (MAXSEL + 1)
gain = primal_step * (1.0 + extrapolation)

F32 = jnp.float32
BF16 = jnp.bfloat16
GRID = (GX, GY, TILE)
SUMS = ((N_MP, MAXSEL, TILE), F32)
RAYS = ((RB_DEV, TILE), F32)


def exchange(copies, axis, first):
    size = N_RAY if axis == "ray" else N_MP
    groups = [[(first + i) % size for i in range(size)]]
    return lax.all_to_all(copies, axis, 0, 0, tiled=True, axis_index_groups=groups)


def at(peer, first):
    return (peer + (N_RAY - first)) & (N_RAY - 1)


def call(kernel, outs, places, args, scratch=(), busy=0, keep=False):
    spaces = {"v": pltpu.VMEM, "h": pltpu.HBM, "a": pl.ANY}
    cost = pl.CostEstimate(flops=0, bytes_accessed=busy, transcendentals=0) if busy else None
    args = [
        pltpu.with_memory_space_constraint(arg, pltpu.HBM) if place == "h" else arg
        for arg, place in zip(args, places)
    ]
    return pl.pallas_call(
        kernel,
        out_shape=[
            pltpu.VMEM(shape, dtype) if keep else jax.ShapeDtypeStruct(shape, dtype)
            for shape, dtype in outs
        ],
        in_specs=[pl.BlockSpec(memory_space=spaces[c]) for c in places],
        out_specs=[pl.BlockSpec(memory_space=pltpu.VMEM) for _ in outs],
        scratch_shapes=list(scratch),
        cost_estimate=cost,
        compiler_params=pltpu.CompilerParams(vmem_limit_bytes=20 * 1024 * 1024),
    )(*args)


SCALARS = (
    pltpu.SMEM((CAP, RB_DEV), jnp.int32),
    pltpu.SMEM((2, RB_DEV), jnp.int32),
    pltpu.SMEM((RB_DEV,), jnp.int32),
    pltpu.SemaphoreType.DMA((2,)),
)


def scalar_copies(pattern_hbm, selected_hbm, pattern_ref, selected_ref, sems):
    return [
        pltpu.make_async_copy(pattern_hbm, pattern_ref, sems.at[0]),
        pltpu.make_async_copy(selected_hbm, selected_ref, sems.at[1]),
    ]


def block_number(pattern):
    row = pattern & (GY * N_RAY - 1)
    plane = lax.shift_right_logical(pattern, 7)
    return lax.shift_right_logical(row, 3) * OWN + plane * GY + (row & (GY - 1))


def list_selected(selected_ref, step, list_ref):
    for n in range(MAXSEL):
        list_ref[n] = jnp.int32(0)
    count = jnp.int32(0)
    for r in range(RB_DEV):
        list_ref[count] = jnp.int32(r)
        count = count + selected_ref[step, r]
    return count


def start_kernel(
    slowness_hbm, bar_hbm, pattern_hbm, selected_hbm, field_ref, sent_ref,
    slowness_ref, bar_ref, sems, pattern_ref, selected_ref, list_ref, scalar_sems,
):
    copies = scalar_copies(pattern_hbm, selected_hbm, pattern_ref, selected_ref, scalar_sems)
    copies.append(pltpu.make_async_copy(slowness_hbm, slowness_ref, sems.at[0]))
    copies.append(pltpu.make_async_copy(bar_hbm, bar_ref, sems.at[1]))
    for copy in copies:
        copy.start()
    copies[0].wait()
    copies[1].wait()
    list_selected(selected_ref, 0, list_ref)
    lane = lax.broadcasted_iota(jnp.int32, (8, TILE), 1) & (PRODUCTS - 1)
    sub = lax.broadcasted_iota(jnp.int32, (8, TILE), 0)
    numbers = jnp.zeros((8, TILE), jnp.int32)
    for n in range(MAXSEL):
        r = list_ref[n]
        for s in range(CAP):
            numbers = jnp.where(lane == n * CAP + s, block_number(pattern_ref[s, r]), numbers)
    numbers = jnp.where(sub == 0, lax.shift_right_logical(numbers, 5), numbers & (OWN - 1))
    copies[2].wait()
    copies[3].wait()
    field = slowness_ref[...] - primal_step * bar_ref[...]
    field_ref[...] = field
    field = field.reshape(OWN, TILE)
    rounded = field.astype(BF16)
    low = field - rounded.astype(F32)
    tail = numbers.astype(F32)
    for x in range(GX):
        tail = jnp.where(sub == REST - OWN + x, low[x * GY : x * GY + 1], tail)
    sent = jnp.concatenate([rounded.astype(F32), tail], axis=0).astype(BF16)
    for p in range(N_RAY):
        sent_ref[p] = sent


def fetch_kernel(step):
    def kernel(
        tiles_hbm, pattern_hbm, selected_hbm, after_ref, picked_ref, hot_ref, pick_ref,
        pattern_ref, selected_ref, list_ref, scalar_sems, sems,
    ):
        scalars = scalar_copies(pattern_hbm, selected_hbm, pattern_ref, selected_ref, scalar_sems)
        for copy in scalars:
            copy.start()
        for copy in scalars:
            copy.wait()
        count = list_selected(selected_ref, step, list_ref)
        copies = [
            pltpu.make_async_copy(tiles_hbm.at[list_ref[n]], picked_ref.at[n], sems.at[n])
            for n in range(MAXSEL)
        ]
        for copy in copies:
            copy.start()
        sub = lax.broadcasted_iota(jnp.int32, (MAXSEL, TILE), 0)
        lane = lax.broadcasted_iota(jnp.int32, (2 * CAP, TILE), 1)
        for n in range(0, MAXSEL, 2):
            halves = []
            for m in (n, n + 1):
                r = list_ref[m]
                numbers = jnp.zeros((CAP, TILE), jnp.int32)
                for s in range(CAP):
                    numbers = jnp.where(sub == s, block_number(pattern_ref[s, r]), numbers)
                halves.append(numbers)
            numbers = jnp.concatenate(halves, axis=0)
            for c in range(ALL // TILE):
                hot = jnp.where(numbers == lane + c * TILE, 1.0, 0.0).astype(BF16)
                hot_ref[n * CAP : (n + 2) * CAP, c * TILE : (c + 1) * TILE] = hot
        listed = jnp.full((MAXSEL, TILE), RB_DEV, jnp.int32)
        for n in range(MAXSEL):
            listed = jnp.where((sub == n) & (sub < count), list_ref[n], listed)
        for r in range(RB_DEV):
            pick_ref[r] = jnp.where(listed == r, 1.0, 0.0)
        for copy in copies:
            copy.wait()

    return kernel


def fetch(step, tiles, pattern, selected, after):
    outs = [
        ((MAXSEL, CAP, TILE, TILE), BF16),
        ((PRODUCTS, ALL), BF16),
        ((RB_DEV, MAXSEL, TILE), F32),
    ]
    scratch = SCALARS + (pltpu.SemaphoreType.DMA((MAXSEL,)),)
    return call(
        fetch_kernel(step), outs, "hhha", (tiles, pattern, selected, after), scratch, 8 * 2**20, True
    )


def forward(hot_ref, blocks, picked_ref):
    cells = jnp.dot(hot_ref[...], blocks, preferred_element_type=F32)
    sub = lax.broadcasted_iota(jnp.int32, (MAXSEL, TILE), 0)
    total = jnp.zeros((MAXSEL, TILE), F32)
    for n in range(MAXSEL):
        for s in range(0, CAP, 8):
            rows = [cells[n * CAP + t : n * CAP + t + 1] for t in range(s, s + 8)]
            lhs = jnp.concatenate([jnp.where(sub == n, row, 0.0) for row in rows], axis=1).astype(BF16)
            rhs = jnp.concatenate([picked_ref[n, t] for t in range(s, s + 8)], axis=1)
            total = total + lax.dot_general(
                lhs, rhs, (((1,), (1,)), ((), ())), preferred_element_type=F32
            )
    return total


def predict_kernel(gathered_ref, picked_ref, hot_ref, out_ref):
    blocks = jnp.concatenate([gathered_ref[at(p, GATHER), 0:OWN, :] for p in range(N_RAY)], axis=0)
    total = forward(hot_ref, blocks, picked_ref)
    for m in range(N_MP):
        out_ref[m] = total


def dual_update(predicted, rays_ref, times_ref, pick_ref, new_rays_ref):
    rays = jnp.zeros((MAXSEL, TILE), F32)
    times = jnp.zeros((MAXSEL, TILE), F32)
    taken = jnp.zeros((MAXSEL, TILE), F32)
    for r in range(RB_DEV):
        pick = pick_ref[r]
        rays = rays + pick * rays_ref[r : r + 1, :]
        times = times + pick * times_ref[r : r + 1, :]
        taken = taken + pick
    fresh = (rays + dual_step * (predicted - times)) / (1.0 + dual_step)
    change = taken * (fresh - rays)
    for r in range(RB_DEV):
        new_rays_ref[r : r + 1, :] = rays_ref[r : r + 1, :] + jnp.sum(
            pick_ref[r] * change, axis=0, keepdims=True
        )
    return change


def products(change, picked_ref, n):
    sub = lax.broadcasted_iota(jnp.int32, (CAP, TILE), 0)
    row = change[n : n + 1]
    total = jnp.zeros((CAP, TILE), F32)
    for s in range(0, CAP, 8):
        lhs = jnp.concatenate(
            [jnp.where(sub == t, row, 0.0) for t in range(s, s + 8)], axis=1
        ).astype(BF16)
        rhs = picked_ref[n, s : s + 8].reshape(8 * TILE, TILE)
        total = total + jnp.dot(lhs, rhs, preferred_element_type=F32)
    return total


def share_kernel(
    parts_ref, rays_ref, times_ref, pick_ref, picked_ref, rest_ref, extra_ref, new_rays_ref, out_ref
):
    predicted = parts_ref[0]
    for m in range(1, N_MP):
        predicted = predicted + parts_ref[m]
    change = dual_update(predicted, rays_ref, times_ref, pick_ref, new_rays_ref)
    for n in range(0, MAXSEL, 2):
        pair = jnp.concatenate(
            [products(change, picked_ref, n), products(change, picked_ref, n + 1)], axis=0
        ).astype(BF16)
        for p in range(N_RAY):
            out_ref[p, n * CAP : (n + 2) * CAP, :] = pair
    rest = jnp.concatenate([rest_ref[...].reshape(OWN, TILE), extra_ref[...]], axis=0).astype(BF16)
    for p in range(N_RAY):
        out_ref[p, PRODUCTS:SHARED, :] = rest


def image_kernel(
    shared_ref, gathered_ref, picked_ref, hot_ref, first_ref, base_ref, image_ref, tv_ref,
    field_ref, new_image_ref, edge_ref, out_ref, table_ref,
):
    lane = lax.broadcasted_iota(jnp.int32, (1, TILE), 1)
    singles = []
    for p in range(N_RAY):
        rows = gathered_ref[at(p, GATHER)].astype(F32)[OWN:SENT]
        singles.append(rows[0:1] * OWN + rows[1:2])
    pairs = [jnp.where(lane < PRODUCTS, singles[p], singles[p + 1]) for p in range(0, N_RAY, 2)]
    group = 4
    chunk = group * OWN
    numbers = []
    terms = []
    for g in range(0, N_RAY, group):
        numbers.append(jnp.concatenate(pairs[g // 2 : g // 2 + 2], axis=1).astype(jnp.int32))
        terms.append(
            jnp.concatenate(
                [shared_ref[at(p, SHARE), 0:PRODUCTS, :] for p in range(g, g + group)], axis=0
            )
        )
    place = lax.broadcasted_iota(jnp.int32, (chunk, group * PRODUCTS), 0)
    sub = lax.broadcasted_iota(jnp.int32, (GY, TILE), 0)
    blocks = []
    for g in range(0, N_RAY, group):
        back = jnp.zeros((chunk, TILE), F32)
        for k in range(N_RAY // group):
            hot = jnp.where(place + g * OWN == numbers[k], 1.0, 0.0).astype(BF16)
            back = back + jnp.dot(hot, terms[k], preferred_element_type=F32)
        table_ref[g * OWN : g * OWN + chunk, :] = back
        for p in range(g, g + group):
            rows = slice(p * OWN, (p + 1) * OWN)
            rest = shared_ref[at(p, SHARE), PRODUCTS:EXTRA, :].astype(F32)
            field = gathered_ref[at(p, GATHER), 0:OWN, :].astype(F32) + (rest - gain * table_ref[rows, :])
            if p > 0:
                change = shared_ref[at(p - 1, SHARE), PRODUCTS:SHARED, :].astype(F32)[OWN:]
                field = field - (2.0 * primal_step) * jnp.concatenate(
                    [jnp.where(sub == 0, change[x : x + 1], 0.0) for x in range(GX)], axis=0
                )
            blocks.append(field)
    total = forward(
        hot_ref, jnp.concatenate([field.astype(BF16) for field in blocks], axis=0), picked_ref
    )
    me, mp = lax.axis_index("ray"), lax.axis_index("mp")
    back = table_ref[pl.ds(pl.multiple_of(me * OWN, OWN), OWN), :]
    for p in range(N_RAY):
        table_ref[p * OWN : (p + 1) * OWN, :] = blocks[p]
    before = jnp.maximum(me - 1, 0)
    for side, peer, row in ((0, before, GY - 1), (1, jnp.minimum(me + 1, N_RAY - 1), 0)):
        field = table_ref[pl.ds(pl.multiple_of(peer * OWN, OWN), OWN), :]
        for x in range(GX):
            edge_ref[side * GX + x : side * GX + x + 1, :] = field[x * GY + row : x * GY + row + 1]
    extra = shared_ref[at(before, SHARE), PRODUCTS:SHARED, :].astype(F32)[OWN:]
    first_y = (sub == 0) & (me > 0)
    edge_ref[2 * GX :] = jnp.zeros((2 * GX, TILE), F32)
    field = []
    for x in range(GX):
        own = back[x * GY : (x + 1) * GY]
        from_y = jnp.where(first_y, extra[x : x + 1], 0.0)
        field.append(base_ref[x] - (gain * own + (2.0 * primal_step) * from_y))
        field_ref[x] = field[x]
        edge_ref[2 * GX + x : 2 * GX + x + 1] = field[x][GY - 1 : GY]
        new_image_ref[x] = image_ref[x] + own + (tv_ref[x] + from_y)
    high = total.astype(BF16).astype(F32)
    ends = [
        jnp.concatenate([high, total - high, field[x] - first_ref[x]], axis=0) for x in (0, GX - 1)
    ]
    for j in range(N_MP):
        out_ref[j] = jnp.where((SUM_2 + j) % N_MP == mp + 1, ends[1], ends[0]).astype(BF16)


def back_kernel(
    parts_ref, rays_ref, times_ref, pick_ref, picked_ref, hot_ref, far_ref, near_ref, dual_ref, edge_ref,
    new_rays_ref, out_ref, planes_ref,
):
    mp = lax.axis_index("mp")
    before, behind = x_halos(far_ref, near_ref)
    step = parts_ref[(mp + (N_MP - 1 - SUM_2)) & (N_MP - 1)].astype(F32)
    before = before[0:GY] + step[2 * MAXSEL :]
    step = parts_ref[(mp + (N_MP + 1 - SUM_2)) & (N_MP - 1)].astype(F32)
    behind = behind[0:GY] + step[2 * MAXSEL :]
    planes_ref[0] = before
    planes_ref[1] = behind
    sub = lax.broadcasted_iota(jnp.int32, (2 * GX, TILE), 0)

    own = [edge_ref[2 * GX + x : 2 * GX + x + 1] for x in range(GX)]
    last_ray = lax.axis_index("ray") == N_RAY - 1
    _, change = tv_cells(
        jnp.concatenate(own * 2, axis=0),
        jnp.concatenate((own[1:] + [behind[GY - 1 : GY]]) * 2, axis=0),
        jnp.concatenate([edge_ref[GX : 2 * GX]] * 2, axis=0),
        [
            jnp.concatenate([dual_ref[c, x][GY - 1 : GY] for x in range(GX)] * 2, axis=0)
            for c in range(3)
        ],
        ((sub & (GX - 1)) == GX - 1) & (mp == N_MP - 1), (sub >= 0) & last_ray,
    )
    high = before[0:1].astype(BF16).astype(F32)
    tail = jnp.where(last_ray, 0.0, change[1])
    tail = jnp.where(sub == 0, high, jnp.where(sub == 1, before[0:1] - high, tail))
    halves = parts_ref[0].astype(F32)
    for m in range(1, N_MP):
        halves = halves + parts_ref[m].astype(F32)
    predicted = halves[0:MAXSEL] + halves[MAXSEL : 2 * MAXSEL]
    change = dual_update(predicted, rays_ref, times_ref, pick_ref, new_rays_ref)
    terms = jnp.concatenate([products(change, picked_ref, n) for n in range(MAXSEL)], axis=0)
    high = terms.astype(BF16)
    low = (terms - high.astype(F32)).astype(BF16)
    turned = (((0,), (0,)), ((), ()))
    image = lax.dot_general(hot_ref[...], high, turned, preferred_element_type=F32)
    image = image + lax.dot_general(hot_ref[...], low, turned, preferred_element_type=F32)
    for p in range(N_RAY):
        out_ref[at(p, LAST)] = jnp.concatenate(
            [image[p * OWN : (p + 1) * OWN], tail], axis=0
        ).astype(BF16)


def swap(block, first):
    route = [(m, m + 1) for m in range(first, N_MP - 1, 2)]
    return lax.ppermute(block, "mp", route + [(b, a) for a, b in route])


def swap_far(block):
    return swap(block, 1)


def swap_near(block):
    return swap(block, 0)


def next_rows(gathered_ref):
    peer = jnp.minimum(lax.axis_index("ray") + 1, N_RAY - 1)
    rows = gathered_ref[at(peer, GATHER)].astype(F32)
    return [
        rows[x * GY : x * GY + 1] + rows[REST + x : REST + x + 1] for x in range(GX)
    ]


def first_edges_kernel(field_ref, dual_ref, gathered_ref, after_any, far_ref, near_ref):
    odd = (lax.axis_index("mp") & 1) == 1
    first = field_ref[0]
    last = field_ref[GX - 1]
    far_ref[0:GY] = jnp.where(odd, last, first)
    near_ref[0:GY] = jnp.where(odd, first, last)
    corner = jnp.broadcast_to(next_rows(gathered_ref)[GX - 1], (GY, TILE))
    far_ref[GY : 2 * GY] = corner
    near_ref[GY : 2 * GY] = corner
    for c in range(3):
        rows = slice((c + 2) * GY, (c + 3) * GY)
        far_ref[rows] = dual_ref[c, GX - 1]
        near_ref[rows] = dual_ref[c, GX - 1]


def x_halos(far_ref, near_ref):
    odd = (lax.axis_index("mp") & 1) == 1
    far, near = far_ref[...], near_ref[...]
    return jnp.where(odd, near, far), jnp.where(odd, far, near)


def tv_cells(here, ahead_x, ahead_y, dual, no_x, no_y):
    lane = lax.broadcasted_iota(jnp.int32, here.shape, len(here.shape) - 1)
    ahead_z = pltpu.roll(here, TILE - 1, len(here.shape) - 1)
    steps = (
        jnp.where(no_x, 0.0, ahead_x - here),
        jnp.where(no_y, 0.0, ahead_y - here),
        jnp.where(lane == TILE - 1, 0.0, ahead_z - here),
    )
    moved = [d + tv_step * g for d, g in zip(dual, steps)]
    length = jnp.sqrt(moved[0] * moved[0] + moved[1] * moved[1] + moved[2] * moved[2])
    scale = jnp.maximum(1.0, length / tv_weight)
    fresh = [m / scale for m in moved]
    return fresh, [a - b for a, b in zip(fresh, dual)]


def up_one(plane, row):
    sub = lax.broadcasted_iota(jnp.int32, plane.shape, 0)
    return jnp.where(sub == GY - 1, row, pltpu.roll(plane, GY - 1, 0))


def plane_before(before, before_next, dual, first):
    sub = lax.broadcasted_iota(jnp.int32, (GY, TILE), 0)
    last_y = (sub == GY - 1) & (lax.axis_index("ray") == N_RAY - 1)
    fresh, change = tv_cells(before, first, up_one(before, before_next), dual, sub < 0, last_y)
    return fresh, jnp.where(lax.axis_index("mp") == 0, 0.0, change[0])


def tv_step_all(field, dual, behind, nexts, from_x):
    mp, ray = lax.axis_index("mp"), lax.axis_index("ray")
    sub = lax.broadcasted_iota(jnp.int32, (GY, TILE), 0)
    lane = lax.broadcasted_iota(jnp.int32, (GY, TILE), 1)
    end_x = (mp == N_MP - 1) & (sub >= 0)
    last_y = (sub == GY - 1) & (ray == N_RAY - 1)
    never = sub < 0
    fresh, backs, second = [], [], []
    for x in range(GX):
        ahead = field[x + 1] if x + 1 < GX else behind
        no_x = end_x if x + 1 == GX else never
        new, change = tv_cells(
            field[x], ahead, up_one(field[x], nexts[x]), [d[x] for d in dual], no_x, last_y
        )
        comp_x = jnp.where(no_x, 0.0, change[0])
        comp_y = jnp.where(last_y, 0.0, change[1])
        comp_z = jnp.where(lane == TILE - 1, 0.0, change[2])
        back = from_x - comp_x
        back = back + (jnp.where(sub == 0, 0.0, pltpu.roll(comp_y, 1, 0)) - comp_y)
        back = back + (jnp.where(lane == 0, 0.0, pltpu.roll(comp_z, 1, 1)) - comp_z)
        from_x = comp_x
        fresh.append(new)
        backs.append(back)
        second.append(comp_y)
    return fresh, backs, second


def first_tv_kernel(
    field_ref, dual_ref, far_ref, near_ref, gathered_ref, image_ref,
    new_dual_ref, plane_ref, back_ref, base_ref, rest_ref, extra_ref,
):
    before, behind = x_halos(far_ref, near_ref)
    field = [field_ref[x] for x in range(GX)]
    halo, from_x = plane_before(
        before[0:GY], before[GY : GY + 1],
        [before[(c + 2) * GY : (c + 3) * GY] for c in range(3)], field[0],
    )
    fresh, backs, second = tv_step_all(
        field,
        [[dual_ref[c, x] for x in range(GX)] for c in range(3)],
        behind[0:GY], next_rows(gathered_ref), from_x,
    )
    extra_ref[...] = jnp.zeros_like(extra_ref)
    for x in range(GX):
        base = field[x] - primal_step * (image_ref[x] + 2.0 * backs[x])
        back_ref[x] = backs[x]
        base_ref[x] = base
        rest_ref[x] = base - field[x].astype(BF16).astype(F32)
        extra_ref[x : x + 1] = second[x][GY - 1 : GY]
        for c in range(3):
            new_dual_ref[c, x] = fresh[x][c]
    for c in range(3):
        plane_ref[c] = halo[c]


def second_tv_kernel(field_ref, dual_ref, planes_ref, edge_ref, new_dual_ref, back_ref):
    edge = edge_ref[...]
    fresh, backs, _ = tv_step_all(
        [field_ref[x] for x in range(GX)],
        [[dual_ref[c, x] for x in range(GX)] for c in range(3)],
        planes_ref[1], [edge[GX + x : GX + x + 1] for x in range(GX)], 0.0,
    )
    for x in range(GX):
        back_ref[x] = backs[x]
        for c in range(3):
            new_dual_ref[c, x] = fresh[x][c]


def last_kernel(
    shared_ref, field_ref, planes_ref, dual_plane_ref, image_ref, tv_ref, out_ref, bar_ref
):
    ray = lax.axis_index("ray")
    above = shared_ref[at(jnp.minimum(ray + 1, N_RAY - 1), LAST)].astype(F32)[OWN:]
    below = shared_ref[at(jnp.maximum(ray - 1, 0), LAST)].astype(F32)[OWN:]
    _, from_x = plane_before(
        planes_ref[0], above[0:1] + above[1:2], [dual_plane_ref[c] for c in range(3)], field_ref[0]
    )
    sub = lax.broadcasted_iota(jnp.int32, (GY, TILE), 0)
    first_y = (sub == 0) & (ray > 0)
    back = shared_ref[0].astype(F32)
    for p in range(1, N_RAY):
        back = back + shared_ref[p].astype(F32)
    for x in range(GX):
        tv_back = tv_ref[x] + jnp.where(first_y, below[GX + x : GX + x + 1], 0.0)
        if x == 0:
            tv_back = tv_back + from_x
        own = back[x * GY : (x + 1) * GY]
        image = image_ref[x] + own + tv_back
        out_ref[x] = image
        bar_ref[x] = image + extrapolation * own + tv_back


def on_device(
    slowness, accumulated, extrapolated, tv_dual, ray_dual, traveltimes, tiles, pattern, selected
):
    pattern = pattern.T
    busy = 8 * 2**20
    grid = (GRID, F32)
    duals = ((3,) + GRID, F32)

    field, sent = call(
        start_kernel, [grid, ((N_RAY, SENT, TILE), BF16)], "hhhh",
        (slowness, extrapolated, pattern, selected),
        (pltpu.VMEM(GRID, F32), pltpu.VMEM(GRID, F32), pltpu.SemaphoreType.DMA((2,))) + SCALARS,
    )
    gathered = exchange(sent, "ray", GATHER)
    picked, hot, pick = fetch(0, tiles, pattern, selected, field)
    (partial_value,) = call(predict_kernel, [SUMS], "vvv", (gathered, picked, hot))
    parts = exchange(partial_value, "mp", SUM_1)

    far, near = call(
        first_edges_kernel, [((5 * GY, TILE), F32)] * 2, "vvva",
        (field, tv_dual, gathered, partial_value), busy=busy,
    )
    far, near = swap_far(far), swap_near(near)
    dual, dual_plane, tv_back, base, rest, extra = call(
        first_tv_kernel,
        [duals, ((3, GY, TILE), F32), grid, grid, grid, ((8, TILE), F32)],
        "vvvvvv", (field, tv_dual, far, near, gathered, accumulated), busy=busy,
    )
    picked_2, hot_2, pick_2 = fetch(1, tiles, pattern, selected, partial_value)

    rays, share = call(
        share_kernel, [RAYS, ((N_RAY, SHARED, TILE), BF16)], "vvvvvvv",
        (parts, ray_dual, traveltimes, pick, picked, rest, extra),
    )
    shared = exchange(share, "ray", SHARE)
    field, image, edge, partial_value = call(
        image_kernel,
        [grid, grid, ((4 * GX, TILE), F32), ((N_MP, 2 * MAXSEL + GY, TILE), BF16)], "vvvvvvvv",
        (shared, gathered, picked_2, hot_2, field, base, accumulated, tv_back),
        (pltpu.VMEM((ALL, TILE), F32),),
    )
    parts = exchange(partial_value, "mp", SUM_2)
    rays, share, planes = call(
        back_kernel, [RAYS, ((N_RAY, OWN + 8, TILE), BF16), ((2, GY, TILE), F32)], "vvvvvvvvvv",
        (parts, rays, traveltimes, pick_2, picked_2, hot_2, far, near, dual, edge),
    )
    shared = exchange(share, "ray", LAST)
    dual, tv_back = call(
        second_tv_kernel, [duals, grid], "vvvv", (field, dual, planes, edge), busy=busy
    )
    image, image_bar = call(
        last_kernel, [grid, grid], "vvvvvv",
        (shared, field, planes, dual_plane, image, tv_back),
    )
    return (field, rays, dual, image, image_bar)


def solution(mesh):
    in_specs = (
        P("mp", "ray", None),
        P("mp", "ray", None),
        P("mp", "ray", None),
        P(None, "mp", "ray", None),
        P("ray", None),
        P("ray", None),
        P("ray", "mp", None, None),
        P("ray", "mp"),
        P(None, "ray"),
    )
    out_specs = (
        P("mp", "ray", None),
        P("ray", None),
        P(None, "mp", "ray", None),
        P("mp", "ray", None),
        P("mp", "ray", None),
    )
    return jax.shard_map(
        on_device, mesh=mesh, in_specs=in_specs, out_specs=out_specs, check_vma=False
    )
```

```python
import jax
import jax.numpy as jnp
from jax import lax
from jax.experimental import pallas as pl
from jax.experimental.pallas import tpu as pltpu
from jax.sharding import PartitionSpec as P

TILE = 128
GX = 4
GY = 8
RB_DEV = 16
CAP = 8
MAXSEL = 8
N_RAY = 16
N_MP = 32
OWN = GX * GY
ALL = N_RAY * OWN
PRODUCTS = MAXSEL * CAP
SENT = OWN + 8
EXTRA = PRODUCTS + OWN
SHARED = EXTRA + 8
GATHER, SUM_1, SHARE, SUM_2, LAST = 9, 19, 5, 19, 10

primal_step = 0.5
dual_step = 0.5
tv_step = 0.25
tv_weight = 0.3
extrapolation = 2.0 * RB_DEV / (MAXSEL + 1)
gain = primal_step * (1.0 + extrapolation)

F32 = jnp.float32
BF16 = jnp.bfloat16
GRID = (GX, GY, TILE)
SUMS = ((N_MP, MAXSEL, TILE), F32)
RAYS = ((RB_DEV, TILE), F32)


def exchange(copies, axis, first):
    size = N_RAY if axis == "ray" else N_MP
    groups = [[(first + i) % size for i in range(size)]]
    return lax.all_to_all(copies, axis, 0, 0, tiled=True, axis_index_groups=groups)


def at(peer, first):
    return (peer + (N_RAY - first)) & (N_RAY - 1)


def call(kernel, outs, places, args, scratch=(), busy=0, keep=False):
    spaces = {"v": pltpu.VMEM, "h": pltpu.HBM, "a": pl.ANY}
    cost = pl.CostEstimate(flops=0, bytes_accessed=busy, transcendentals=0) if busy else None
    args = [
        pltpu.with_memory_space_constraint(arg, pltpu.HBM) if place == "h" else arg
        for arg, place in zip(args, places)
    ]
    return pl.pallas_call(
        kernel,
        out_shape=[
            pltpu.VMEM(shape, dtype) if keep else jax.ShapeDtypeStruct(shape, dtype)
            for shape, dtype in outs
        ],
        in_specs=[pl.BlockSpec(memory_space=spaces[c]) for c in places],
        out_specs=[pl.BlockSpec(memory_space=pltpu.VMEM) for _ in outs],
        scratch_shapes=list(scratch),
        cost_estimate=cost,
        compiler_params=pltpu.CompilerParams(vmem_limit_bytes=20 * 1024 * 1024),
    )(*args)


SCALARS = (
    pltpu.SMEM((CAP, RB_DEV), jnp.int32),
    pltpu.SMEM((2, RB_DEV), jnp.int32),
    pltpu.SMEM((RB_DEV,), jnp.int32),
    pltpu.SemaphoreType.DMA((2,)),
)


def scalar_copies(pattern_hbm, selected_hbm, pattern_ref, selected_ref, sems):
    return [
        pltpu.make_async_copy(pattern_hbm, pattern_ref, sems.at[0]),
        pltpu.make_async_copy(selected_hbm, selected_ref, sems.at[1]),
    ]


def block_number(pattern):
    row = pattern & (GY * N_RAY - 1)
    plane = lax.shift_right_logical(pattern, 7)
    return lax.shift_right_logical(row, 3) * OWN + plane * GY + (row & (GY - 1))


def list_selected(selected_ref, step, list_ref):
    for n in range(MAXSEL):
        list_ref[n] = jnp.int32(0)
    count = jnp.int32(0)
    for r in range(RB_DEV):
        list_ref[count] = jnp.int32(r)
        count = count + selected_ref[step, r]
    return count


def start_kernel(slowness_hbm, bar_hbm, field_ref, sent_ref, slowness_ref, bar_ref, sems):
    copies = [
        pltpu.make_async_copy(slowness_hbm, slowness_ref, sems.at[0]),
        pltpu.make_async_copy(bar_hbm, bar_ref, sems.at[1]),
    ]
    for copy in copies:
        copy.start()
    for copy in copies:
        copy.wait()
    field = slowness_ref[...] - primal_step * bar_ref[...]
    field_ref[...] = field
    field = field.reshape(OWN, TILE)
    rounded = field.astype(BF16).astype(F32)
    low = field - rounded
    sub = lax.broadcasted_iota(jnp.int32, (8, TILE), 0)
    tail = jnp.zeros((8, TILE), F32)
    for x in range(GX):
        tail = jnp.where(sub == x, low[x * GY : x * GY + 1], tail)
    sent = jnp.concatenate([rounded, tail], axis=0).astype(BF16)
    for p in range(N_RAY):
        sent_ref[p] = sent


def fetch_kernel(step):
    def kernel(
        tiles_hbm, pattern_hbm, selected_hbm, after_ref, picked_ref, hot_ref, pick_ref, numbers_ref,
        pattern_ref, selected_ref, list_ref, scalar_sems, sems,
    ):
        scalars = scalar_copies(pattern_hbm, selected_hbm, pattern_ref, selected_ref, scalar_sems)
        for copy in scalars:
            copy.start()
        for copy in scalars:
            copy.wait()
        count = list_selected(selected_ref, step, list_ref)
        copies = [
            pltpu.make_async_copy(tiles_hbm.at[list_ref[n]], picked_ref.at[n], sems.at[n])
            for n in range(MAXSEL)
        ]
        for copy in copies:
            copy.start()
        sub = lax.broadcasted_iota(jnp.int32, (MAXSEL, TILE), 0)
        lane = lax.broadcasted_iota(jnp.int32, (2 * CAP, TILE), 1)
        slot = lax.broadcasted_iota(jnp.int32, (8, TILE), 1) & (PRODUCTS - 1)
        line = jnp.zeros((8, TILE), jnp.int32)
        for n in range(0, MAXSEL, 2):
            halves = []
            for m in (n, n + 1):
                r = list_ref[m]
                numbers = jnp.zeros((CAP, TILE), jnp.int32)
                for s in range(CAP):
                    number = block_number(pattern_ref[s, r])
                    numbers = jnp.where(sub == s, number, numbers)
                    line = jnp.where(slot == m * CAP + s, number, line)
                halves.append(numbers)
            numbers = jnp.concatenate(halves, axis=0)
            for c in range(ALL // TILE):
                hot = jnp.where(numbers == lane + c * TILE, 1.0, 0.0).astype(BF16)
                hot_ref[n * CAP : (n + 2) * CAP, c * TILE : (c + 1) * TILE] = hot
        line = jnp.where(sub == 4, lax.shift_right_logical(line, 5), line & (OWN - 1))
        numbers_ref[...] = jnp.where((sub == 4) | (sub == 5), line.astype(F32), 0.0)
        listed = jnp.full((MAXSEL, TILE), RB_DEV, jnp.int32)
        for n in range(MAXSEL):
            listed = jnp.where((sub == n) & (sub < count), list_ref[n], listed)
        for r in range(RB_DEV):
            pick_ref[r] = jnp.where(listed == r, 1.0, 0.0)
        for copy in copies:
            copy.wait()

    return kernel


def fetch(step, tiles, pattern, selected, after):
    outs = [
        ((MAXSEL, CAP, TILE, TILE), BF16),
        ((PRODUCTS, ALL), BF16),
        ((RB_DEV, MAXSEL, TILE), F32),
        ((8, TILE), F32),
    ]
    scratch = SCALARS + (pltpu.SemaphoreType.DMA((MAXSEL,)),)
    return call(
        fetch_kernel(step), outs, "hhha", (tiles, pattern, selected, after), scratch, 8 * 2**20, True
    )


def forward(hot_ref, blocks, picked_ref):
    cells = jnp.dot(hot_ref[...], blocks, preferred_element_type=F32)
    sub = lax.broadcasted_iota(jnp.int32, (MAXSEL, TILE), 0)
    total = jnp.zeros((MAXSEL, TILE), F32)
    for n in range(MAXSEL):
        for s in range(0, CAP, 8):
            rows = [cells[n * CAP + t : n * CAP + t + 1] for t in range(s, s + 8)]
            lhs = jnp.concatenate([jnp.where(sub == n, row, 0.0) for row in rows], axis=1).astype(BF16)
            rhs = jnp.concatenate([picked_ref[n, t] for t in range(s, s + 8)], axis=1)
            total = total + lax.dot_general(
                lhs, rhs, (((1,), (1,)), ((), ())), preferred_element_type=F32
            )
    return total


def predict_kernel(gathered_ref, picked_ref, hot_ref, out_ref):
    blocks = jnp.concatenate([gathered_ref[at(p, GATHER), 0:OWN, :] for p in range(N_RAY)], axis=0)
    total = forward(hot_ref, blocks, picked_ref)
    for m in range(N_MP):
        out_ref[m] = total


def dual_update(predicted, rays_ref, times_ref, pick_ref, new_rays_ref):
    rays = jnp.zeros((MAXSEL, TILE), F32)
    times = jnp.zeros((MAXSEL, TILE), F32)
    taken = jnp.zeros((MAXSEL, TILE), F32)
    for r in range(RB_DEV):
        pick = pick_ref[r]
        rays = rays + pick * rays_ref[r : r + 1, :]
        times = times + pick * times_ref[r : r + 1, :]
        taken = taken + pick
    fresh = (rays + dual_step * (predicted - times)) / (1.0 + dual_step)
    change = taken * (fresh - rays)
    for r in range(RB_DEV):
        new_rays_ref[r : r + 1, :] = rays_ref[r : r + 1, :] + jnp.sum(
            pick_ref[r] * change, axis=0, keepdims=True
        )
    return change


def products(change, picked_ref, n):
    sub = lax.broadcasted_iota(jnp.int32, (CAP, TILE), 0)
    row = change[n : n + 1]
    total = jnp.zeros((CAP, TILE), F32)
    for s in range(0, CAP, 8):
        lhs = jnp.concatenate(
            [jnp.where(sub == t, row, 0.0) for t in range(s, s + 8)], axis=1
        ).astype(BF16)
        rhs = picked_ref[n, s : s + 8].reshape(8 * TILE, TILE)
        total = total + jnp.dot(lhs, rhs, preferred_element_type=F32)
    return total


def share_kernel(
    parts_ref, rays_ref, times_ref, pick_ref, picked_ref, rest_ref, extra_ref, numbers_ref,
    new_rays_ref, out_ref,
):
    predicted = parts_ref[0]
    for m in range(1, N_MP):
        predicted = predicted + parts_ref[m]
    change = dual_update(predicted, rays_ref, times_ref, pick_ref, new_rays_ref)
    for n in range(0, MAXSEL, 2):
        pair = jnp.concatenate(
            [products(change, picked_ref, n), products(change, picked_ref, n + 1)], axis=0
        ).astype(BF16)
        for p in range(N_RAY):
            out_ref[p, n * CAP : (n + 2) * CAP, :] = pair
    extra = extra_ref[...] + numbers_ref[...]
    rest = jnp.concatenate([rest_ref[...].reshape(OWN, TILE), extra], axis=0).astype(BF16)
    for p in range(N_RAY):
        out_ref[p, PRODUCTS:SHARED, :] = rest


def image_kernel(
    shared_ref, gathered_ref, picked_ref, hot_ref, first_ref, base_ref, image_ref, tv_ref,
    field_ref, new_image_ref, edge_ref, out_ref, table_ref,
):
    lane = lax.broadcasted_iota(jnp.int32, (1, TILE), 1)
    singles = []
    for p in range(N_RAY):
        rows = shared_ref[at(p, SHARE), PRODUCTS:SHARED, :].astype(F32)[OWN:]
        singles.append(rows[4:5] * OWN + rows[5:6])
    pairs = [jnp.where(lane < PRODUCTS, singles[p], singles[p + 1]) for p in range(0, N_RAY, 2)]
    group = 4
    chunk = group * OWN
    numbers = []
    terms = []
    for g in range(0, N_RAY, group):
        numbers.append(jnp.concatenate(pairs[g // 2 : g // 2 + 2], axis=1).astype(jnp.int32))
        terms.append(
            jnp.concatenate(
                [shared_ref[at(p, SHARE), 0:PRODUCTS, :] for p in range(g, g + group)], axis=0
            )
        )
    place = lax.broadcasted_iota(jnp.int32, (chunk, group * PRODUCTS), 0)
    sub = lax.broadcasted_iota(jnp.int32, (GY, TILE), 0)
    blocks = []
    for g in range(0, N_RAY, group):
        back = jnp.zeros((chunk, TILE), F32)
        for k in range(N_RAY // group):
            hot = jnp.where(place + g * OWN == numbers[k], 1.0, 0.0).astype(BF16)
            back = back + jnp.dot(hot, terms[k], preferred_element_type=F32)
        table_ref[g * OWN : g * OWN + chunk, :] = back
        for p in range(g, g + group):
            rows = slice(p * OWN, (p + 1) * OWN)
            rest = shared_ref[at(p, SHARE), PRODUCTS:EXTRA, :].astype(F32)
            field = gathered_ref[at(p, GATHER), 0:OWN, :].astype(F32) + (rest - gain * table_ref[rows, :])
            if p > 0:
                change = shared_ref[at(p - 1, SHARE), PRODUCTS:SHARED, :].astype(F32)[OWN:]
                field = field - (2.0 * primal_step) * jnp.concatenate(
                    [jnp.where(sub == 0, change[x : x + 1], 0.0) for x in range(GX)], axis=0
                )
            blocks.append(field)
    total = forward(
        hot_ref, jnp.concatenate([field.astype(BF16) for field in blocks], axis=0), picked_ref
    )
    me, mp = lax.axis_index("ray"), lax.axis_index("mp")
    back = table_ref[pl.ds(pl.multiple_of(me * OWN, OWN), OWN), :]
    for p in range(N_RAY):
        table_ref[p * OWN : (p + 1) * OWN, :] = blocks[p]
    before = jnp.maximum(me - 1, 0)
    for side, peer, row in ((0, before, GY - 1), (1, jnp.minimum(me + 1, N_RAY - 1), 0)):
        field = table_ref[pl.ds(pl.multiple_of(peer * OWN, OWN), OWN), :]
        for x in range(GX):
            edge_ref[side * GX + x : side * GX + x + 1, :] = field[x * GY + row : x * GY + row + 1]
    extra = shared_ref[at(before, SHARE), PRODUCTS:SHARED, :].astype(F32)[OWN:]
    first_y = (sub == 0) & (me > 0)
    edge_ref[2 * GX :] = jnp.zeros((2 * GX, TILE), F32)
    field = []
    for x in range(GX):
        own = back[x * GY : (x + 1) * GY]
        from_y = jnp.where(first_y, extra[x : x + 1], 0.0)
        field.append(base_ref[x] - (gain * own + (2.0 * primal_step) * from_y))
        field_ref[x] = field[x]
        edge_ref[2 * GX + x : 2 * GX + x + 1] = field[x][GY - 1 : GY]
        new_image_ref[x] = image_ref[x] + own + (tv_ref[x] + from_y)
    high = total.astype(BF16).astype(F32)
    ends = [
        jnp.concatenate([high, total - high, field[x] - first_ref[x]], axis=0) for x in (0, GX - 1)
    ]
    for j in range(N_MP):
        out_ref[j] = jnp.where((SUM_2 + j) % N_MP == mp + 1, ends[1], ends[0]).astype(BF16)


def back_kernel(
    parts_ref, rays_ref, times_ref, pick_ref, picked_ref, hot_ref, far_ref, near_ref, dual_ref, edge_ref,
    new_rays_ref, out_ref, planes_ref,
):
    mp = lax.axis_index("mp")
    before, behind = x_halos(far_ref, near_ref)
    step = parts_ref[(mp + (N_MP - 1 - SUM_2)) & (N_MP - 1)].astype(F32)
    before = before[0:GY] + step[2 * MAXSEL :]
    step = parts_ref[(mp + (N_MP + 1 - SUM_2)) & (N_MP - 1)].astype(F32)
    behind = behind[0:GY] + step[2 * MAXSEL :]
    planes_ref[0] = before
    planes_ref[1] = behind
    sub = lax.broadcasted_iota(jnp.int32, (2 * GX, TILE), 0)

    own = [edge_ref[2 * GX + x : 2 * GX + x + 1] for x in range(GX)]
    last_ray = lax.axis_index("ray") == N_RAY - 1
    _, change = tv_cells(
        jnp.concatenate(own * 2, axis=0),
        jnp.concatenate((own[1:] + [behind[GY - 1 : GY]]) * 2, axis=0),
        jnp.concatenate([edge_ref[GX : 2 * GX]] * 2, axis=0),
        [
            jnp.concatenate([dual_ref[c, x][GY - 1 : GY] for x in range(GX)] * 2, axis=0)
            for c in range(3)
        ],
        ((sub & (GX - 1)) == GX - 1) & (mp == N_MP - 1), (sub >= 0) & last_ray,
    )
    high = before[0:1].astype(BF16).astype(F32)
    tail = jnp.where(last_ray, 0.0, change[1])
    tail = jnp.where(sub == 0, high, jnp.where(sub == 1, before[0:1] - high, tail))
    halves = parts_ref[0].astype(F32)
    for m in range(1, N_MP):
        halves = halves + parts_ref[m].astype(F32)
    predicted = halves[0:MAXSEL] + halves[MAXSEL : 2 * MAXSEL]
    change = dual_update(predicted, rays_ref, times_ref, pick_ref, new_rays_ref)
    terms = jnp.concatenate([products(change, picked_ref, n) for n in range(MAXSEL)], axis=0)
    high = terms.astype(BF16)
    low = (terms - high.astype(F32)).astype(BF16)
    turned = (((0,), (0,)), ((), ()))
    image = lax.dot_general(hot_ref[...], high, turned, preferred_element_type=F32)
    image = image + lax.dot_general(hot_ref[...], low, turned, preferred_element_type=F32)
    for p in range(N_RAY):
        out_ref[at(p, LAST)] = jnp.concatenate(
            [image[p * OWN : (p + 1) * OWN], tail], axis=0
        ).astype(BF16)


def swap(block, first):
    route = [(m, m + 1) for m in range(first, N_MP - 1, 2)]
    return lax.ppermute(block, "mp", route + [(b, a) for a, b in route])


def swap_far(block):
    return swap(block, 1)


def swap_near(block):
    return swap(block, 0)


def next_rows(gathered_ref):
    peer = jnp.minimum(lax.axis_index("ray") + 1, N_RAY - 1)
    rows = gathered_ref[at(peer, GATHER)].astype(F32)
    return [
        rows[x * GY : x * GY + 1] + rows[OWN + x : OWN + x + 1] for x in range(GX)
    ]


def first_edges_kernel(field_ref, dual_ref, gathered_ref, after_any, far_ref, near_ref):
    odd = (lax.axis_index("mp") & 1) == 1
    first = field_ref[0]
    last = field_ref[GX - 1]
    far_ref[0:GY] = jnp.where(odd, last, first)
    near_ref[0:GY] = jnp.where(odd, first, last)
    corner = jnp.broadcast_to(next_rows(gathered_ref)[GX - 1], (GY, TILE))
    far_ref[GY : 2 * GY] = corner
    near_ref[GY : 2 * GY] = corner
    for c in range(3):
        rows = slice((c + 2) * GY, (c + 3) * GY)
        far_ref[rows] = dual_ref[c, GX - 1]
        near_ref[rows] = dual_ref[c, GX - 1]


def x_halos(far_ref, near_ref):
    odd = (lax.axis_index("mp") & 1) == 1
    far, near = far_ref[...], near_ref[...]
    return jnp.where(odd, near, far), jnp.where(odd, far, near)


def tv_cells(here, ahead_x, ahead_y, dual, no_x, no_y):
    lane = lax.broadcasted_iota(jnp.int32, here.shape, len(here.shape) - 1)
    ahead_z = pltpu.roll(here, TILE - 1, len(here.shape) - 1)
    steps = (
        jnp.where(no_x, 0.0, ahead_x - here),
        jnp.where(no_y, 0.0, ahead_y - here),
        jnp.where(lane == TILE - 1, 0.0, ahead_z - here),
    )
    moved = [d + tv_step * g for d, g in zip(dual, steps)]
    length = jnp.sqrt(moved[0] * moved[0] + moved[1] * moved[1] + moved[2] * moved[2])
    scale = jnp.maximum(1.0, length / tv_weight)
    fresh = [m / scale for m in moved]
    return fresh, [a - b for a, b in zip(fresh, dual)]


def up_one(plane, row):
    sub = lax.broadcasted_iota(jnp.int32, plane.shape, 0)
    return jnp.where(sub == GY - 1, row, pltpu.roll(plane, GY - 1, 0))


def plane_before(before, before_next, dual, first):
    sub = lax.broadcasted_iota(jnp.int32, (GY, TILE), 0)
    last_y = (sub == GY - 1) & (lax.axis_index("ray") == N_RAY - 1)
    fresh, change = tv_cells(before, first, up_one(before, before_next), dual, sub < 0, last_y)
    return fresh, jnp.where(lax.axis_index("mp") == 0, 0.0, change[0])


def tv_step_all(field, dual, behind, nexts, from_x):
    mp, ray = lax.axis_index("mp"), lax.axis_index("ray")
    sub = lax.broadcasted_iota(jnp.int32, (GY, TILE), 0)
    lane = lax.broadcasted_iota(jnp.int32, (GY, TILE), 1)
    end_x = (mp == N_MP - 1) & (sub >= 0)
    last_y = (sub == GY - 1) & (ray == N_RAY - 1)
    never = sub < 0
    fresh, backs, second = [], [], []
    for x in range(GX):
        ahead = field[x + 1] if x + 1 < GX else behind
        no_x = end_x if x + 1 == GX else never
        new, change = tv_cells(
            field[x], ahead, up_one(field[x], nexts[x]), [d[x] for d in dual], no_x, last_y
        )
        comp_x = jnp.where(no_x, 0.0, change[0])
        comp_y = jnp.where(last_y, 0.0, change[1])
        comp_z = jnp.where(lane == TILE - 1, 0.0, change[2])
        back = from_x - comp_x
        back = back + (jnp.where(sub == 0, 0.0, pltpu.roll(comp_y, 1, 0)) - comp_y)
        back = back + (jnp.where(lane == 0, 0.0, pltpu.roll(comp_z, 1, 1)) - comp_z)
        from_x = comp_x
        fresh.append(new)
        backs.append(back)
        second.append(comp_y)
    return fresh, backs, second


def first_tv_kernel(
    field_ref, dual_ref, far_ref, near_ref, gathered_ref, image_ref,
    new_dual_ref, plane_ref, back_ref, base_ref, rest_ref, extra_ref,
):
    before, behind = x_halos(far_ref, near_ref)
    field = [field_ref[x] for x in range(GX)]
    halo, from_x = plane_before(
        before[0:GY], before[GY : GY + 1],
        [before[(c + 2) * GY : (c + 3) * GY] for c in range(3)], field[0],
    )
    fresh, backs, second = tv_step_all(
        field,
        [[dual_ref[c, x] for x in range(GX)] for c in range(3)],
        behind[0:GY], next_rows(gathered_ref), from_x,
    )
    extra_ref[...] = jnp.zeros_like(extra_ref)
    for x in range(GX):
        base = field[x] - primal_step * (image_ref[x] + 2.0 * backs[x])
        back_ref[x] = backs[x]
        base_ref[x] = base
        rest_ref[x] = base - field[x].astype(BF16).astype(F32)
        extra_ref[x : x + 1] = second[x][GY - 1 : GY]
        for c in range(3):
            new_dual_ref[c, x] = fresh[x][c]
    for c in range(3):
        plane_ref[c] = halo[c]


def second_tv_kernel(field_ref, dual_ref, planes_ref, edge_ref, new_dual_ref, back_ref):
    edge = edge_ref[...]
    fresh, backs, _ = tv_step_all(
        [field_ref[x] for x in range(GX)],
        [[dual_ref[c, x] for x in range(GX)] for c in range(3)],
        planes_ref[1], [edge[GX + x : GX + x + 1] for x in range(GX)], 0.0,
    )
    for x in range(GX):
        back_ref[x] = backs[x]
        for c in range(3):
            new_dual_ref[c, x] = fresh[x][c]


def last_kernel(
    shared_ref, field_ref, planes_ref, dual_plane_ref, image_ref, tv_ref, out_ref, bar_ref
):
    ray = lax.axis_index("ray")
    above = shared_ref[at(jnp.minimum(ray + 1, N_RAY - 1), LAST)].astype(F32)[OWN:]
    below = shared_ref[at(jnp.maximum(ray - 1, 0), LAST)].astype(F32)[OWN:]
    _, from_x = plane_before(
        planes_ref[0], above[0:1] + above[1:2], [dual_plane_ref[c] for c in range(3)], field_ref[0]
    )
    sub = lax.broadcasted_iota(jnp.int32, (GY, TILE), 0)
    first_y = (sub == 0) & (ray > 0)
    back = shared_ref[0].astype(F32)
    for p in range(1, N_RAY):
        back = back + shared_ref[p].astype(F32)
    for x in range(GX):
        tv_back = tv_ref[x] + jnp.where(first_y, below[GX + x : GX + x + 1], 0.0)
        if x == 0:
            tv_back = tv_back + from_x
        own = back[x * GY : (x + 1) * GY]
        image = image_ref[x] + own + tv_back
        out_ref[x] = image
        bar_ref[x] = image + extrapolation * own + tv_back


def on_device(
    slowness, accumulated, extrapolated, tv_dual, ray_dual, traveltimes, tiles, pattern, selected
):
    pattern = pattern.T
    busy = 8 * 2**20
    grid = (GRID, F32)
    duals = ((3,) + GRID, F32)

    field, sent = call(
        start_kernel, [grid, ((N_RAY, SENT, TILE), BF16)], "hh", (slowness, extrapolated),
        (pltpu.VMEM(GRID, F32), pltpu.VMEM(GRID, F32), pltpu.SemaphoreType.DMA((2,))),
    )
    gathered = exchange(sent, "ray", GATHER)
    picked, hot, pick, numbers = fetch(0, tiles, pattern, selected, field)
    (partial_value,) = call(predict_kernel, [SUMS], "vvv", (gathered, picked, hot))
    parts = exchange(partial_value, "mp", SUM_1)

    far, near = call(
        first_edges_kernel, [((5 * GY, TILE), F32)] * 2, "vvva",
        (field, tv_dual, gathered, partial_value), busy=busy,
    )
    far, near = swap_far(far), swap_near(near)
    dual, dual_plane, tv_back, base, rest, extra = call(
        first_tv_kernel,
        [duals, ((3, GY, TILE), F32), grid, grid, grid, ((8, TILE), F32)],
        "vvvvvv", (field, tv_dual, far, near, gathered, accumulated), busy=busy,
    )
    picked_2, hot_2, pick_2, _ = fetch(1, tiles, pattern, selected, partial_value)

    rays, share = call(
        share_kernel, [RAYS, ((N_RAY, SHARED, TILE), BF16)], "vvvvvvvv",
        (parts, ray_dual, traveltimes, pick, picked, rest, extra, numbers),
    )
    shared = exchange(share, "ray", SHARE)
    field, image, edge, partial_value = call(
        image_kernel,
        [grid, grid, ((4 * GX, TILE), F32), ((N_MP, 2 * MAXSEL + GY, TILE), BF16)], "vvvvvvvv",
        (shared, gathered, picked_2, hot_2, field, base, accumulated, tv_back),
        (pltpu.VMEM((ALL, TILE), F32),),
    )
    parts = exchange(partial_value, "mp", SUM_2)
    rays, share, planes = call(
        back_kernel, [RAYS, ((N_RAY, OWN + 8, TILE), BF16), ((2, GY, TILE), F32)], "vvvvvvvvvv",
        (parts, rays, traveltimes, pick_2, picked_2, hot_2, far, near, dual, edge),
    )
    shared = exchange(share, "ray", LAST)
    dual, tv_back = call(
        second_tv_kernel, [duals, grid], "vvvv", (field, dual, planes, edge), busy=busy
    )
    image, image_bar = call(
        last_kernel, [grid, grid], "vvvvvv",
        (shared, field, planes, dual_plane, image, tv_back),
    )
    return (field, rays, dual, image, image_bar)


def solution(mesh):
    in_specs = (
        P("mp", "ray", None),
        P("mp", "ray", None),
        P("mp", "ray", None),
        P(None, "mp", "ray", None),
        P("ray", None),
        P("ray", None),
        P("ray", "mp", None, None),
        P("ray", "mp"),
        P(None, "ray"),
    )
    out_specs = (
        P("mp", "ray", None),
        P("ray", None),
        P(None, "mp", "ray", None),
        P("mp", "ray", None),
        P("mp", "ray", None),
    )
    return jax.shard_map(
        on_device, mesh=mesh, in_specs=in_specs, out_specs=out_specs, check_vma=False
    )
```

```python
import jax
import jax.numpy as jnp
from jax import lax
from jax.experimental import pallas as pl
from jax.experimental.pallas import tpu as pltpu
from jax.sharding import PartitionSpec as P

TILE = 128
GX = 4
GY = 8
RB_DEV = 16
CAP = 8
MAXSEL = 8
N_RAY = 16
N_MP = 32
OWN = GX * GY
ALL = N_RAY * OWN
PRODUCTS = MAXSEL * CAP
SENT = OWN + 8
EXTRA = PRODUCTS + OWN
SHARED = EXTRA + 8
GATHER, SUM_1, SHARE, SUM_2, LAST = 9, 19, 9, 19, 10

primal_step = 0.5
dual_step = 0.5
tv_step = 0.25
tv_weight = 0.3
extrapolation = 2.0 * RB_DEV / (MAXSEL + 1)
gain = primal_step * (1.0 + extrapolation)

F32 = jnp.float32
BF16 = jnp.bfloat16
GRID = (GX, GY, TILE)
SUMS = ((N_MP, MAXSEL, TILE), F32)
RAYS = ((RB_DEV, TILE), F32)


def exchange(copies, axis, first):
    size = N_RAY if axis == "ray" else N_MP
    groups = [[(first + i) % size for i in range(size)]]
    return lax.all_to_all(copies, axis, 0, 0, tiled=True, axis_index_groups=groups)


def at(peer, first):
    return (peer + (N_RAY - first)) & (N_RAY - 1)


def call(kernel, outs, places, args, scratch=(), busy=0, keep=False):
    spaces = {"v": pltpu.VMEM, "h": pltpu.HBM, "a": pl.ANY}
    cost = pl.CostEstimate(flops=0, bytes_accessed=busy, transcendentals=0) if busy else None
    args = [
        pltpu.with_memory_space_constraint(arg, pltpu.HBM) if place == "h" else arg
        for arg, place in zip(args, places)
    ]
    return pl.pallas_call(
        kernel,
        out_shape=[
            pltpu.VMEM(shape, dtype) if keep else jax.ShapeDtypeStruct(shape, dtype)
            for shape, dtype in outs
        ],
        in_specs=[pl.BlockSpec(memory_space=spaces[c]) for c in places],
        out_specs=[pl.BlockSpec(memory_space=pltpu.VMEM) for _ in outs],
        scratch_shapes=list(scratch),
        cost_estimate=cost,
        compiler_params=pltpu.CompilerParams(vmem_limit_bytes=20 * 1024 * 1024),
    )(*args)


SCALARS = (
    pltpu.SMEM((CAP, RB_DEV), jnp.int32),
    pltpu.SMEM((2, RB_DEV), jnp.int32),
    pltpu.SMEM((RB_DEV,), jnp.int32),
    pltpu.SemaphoreType.DMA((2,)),
)


def scalar_copies(pattern_hbm, selected_hbm, pattern_ref, selected_ref, sems):
    return [
        pltpu.make_async_copy(pattern_hbm, pattern_ref, sems.at[0]),
        pltpu.make_async_copy(selected_hbm, selected_ref, sems.at[1]),
    ]


def block_number(pattern):
    row = pattern & (GY * N_RAY - 1)
    plane = lax.shift_right_logical(pattern, 7)
    return lax.shift_right_logical(row, 3) * OWN + plane * GY + (row & (GY - 1))


def list_selected(selected_ref, step, list_ref):
    for n in range(MAXSEL):
        list_ref[n] = jnp.int32(0)
    count = jnp.int32(0)
    for r in range(RB_DEV):
        list_ref[count] = jnp.int32(r)
        count = count + selected_ref[step, r]
    return count


def start_kernel(slowness_hbm, bar_hbm, field_ref, sent_ref, slowness_ref, bar_ref, sems):
    copies = [
        pltpu.make_async_copy(slowness_hbm, slowness_ref, sems.at[0]),
        pltpu.make_async_copy(bar_hbm, bar_ref, sems.at[1]),
    ]
    for copy in copies:
        copy.start()
    for copy in copies:
        copy.wait()
    field = slowness_ref[...] - primal_step * bar_ref[...]
    field_ref[...] = field
    field = field.reshape(OWN, TILE)
    rounded = field.astype(BF16).astype(F32)
    low = field - rounded
    sub = lax.broadcasted_iota(jnp.int32, (8, TILE), 0)
    tail = jnp.zeros((8, TILE), F32)
    for x in range(GX):
        tail = jnp.where(sub == x, low[x * GY : x * GY + 1], tail)
    sent = jnp.concatenate([rounded, tail], axis=0).astype(BF16)
    for p in range(N_RAY):
        sent_ref[p] = sent


def fetch_kernel(step):
    def kernel(
        tiles_hbm, pattern_hbm, selected_hbm, after_ref, picked_ref, hot_ref, pick_ref, numbers_ref,
        pattern_ref, selected_ref, list_ref, scalar_sems, sems,
    ):
        scalars = scalar_copies(pattern_hbm, selected_hbm, pattern_ref, selected_ref, scalar_sems)
        for copy in scalars:
            copy.start()
        for copy in scalars:
            copy.wait()
        count = list_selected(selected_ref, step, list_ref)
        copies = [
            pltpu.make_async_copy(tiles_hbm.at[list_ref[n]], picked_ref.at[n], sems.at[n])
            for n in range(MAXSEL)
        ]
        for copy in copies:
            copy.start()
        sub = lax.broadcasted_iota(jnp.int32, (MAXSEL, TILE), 0)
        lane = lax.broadcasted_iota(jnp.int32, (2 * CAP, TILE), 1)
        slot = lax.broadcasted_iota(jnp.int32, (8, TILE), 1) & (PRODUCTS - 1)
        line = jnp.zeros((8, TILE), jnp.int32)
        for n in range(0, MAXSEL, 2):
            halves = []
            for m in (n, n + 1):
                r = list_ref[m]
                numbers = jnp.zeros((CAP, TILE), jnp.int32)
                for s in range(CAP):
                    number = block_number(pattern_ref[s, r])
                    numbers = jnp.where(sub == s, number, numbers)
                    line = jnp.where(slot == m * CAP + s, number, line)
                halves.append(numbers)
            numbers = jnp.concatenate(halves, axis=0)
            for c in range(ALL // TILE):
                hot = jnp.where(numbers == lane + c * TILE, 1.0, 0.0).astype(BF16)
                hot_ref[n * CAP : (n + 2) * CAP, c * TILE : (c + 1) * TILE] = hot
        line = jnp.where(sub == 4, lax.shift_right_logical(line, 5), line & (OWN - 1))
        numbers_ref[...] = jnp.where((sub == 4) | (sub == 5), line.astype(F32), 0.0)
        listed = jnp.full((MAXSEL, TILE), RB_DEV, jnp.int32)
        for n in range(MAXSEL):
            listed = jnp.where((sub == n) & (sub < count), list_ref[n], listed)
        for r in range(RB_DEV):
            pick_ref[r] = jnp.where(listed == r, 1.0, 0.0)
        for copy in copies:
            copy.wait()

    return kernel


def fetch(step, tiles, pattern, selected, after):
    outs = [
        ((MAXSEL, CAP, TILE, TILE), BF16),
        ((PRODUCTS, ALL), BF16),
        ((RB_DEV, MAXSEL, TILE), F32),
        ((8, TILE), F32),
    ]
    scratch = SCALARS + (pltpu.SemaphoreType.DMA((MAXSEL,)),)
    return call(
        fetch_kernel(step), outs, "hhha", (tiles, pattern, selected, after), scratch, 8 * 2**20, True
    )


def forward(hot_ref, blocks, picked_ref):
    cells = jnp.dot(hot_ref[...], blocks, preferred_element_type=F32)
    sub = lax.broadcasted_iota(jnp.int32, (MAXSEL, TILE), 0)
    total = jnp.zeros((MAXSEL, TILE), F32)
    for n in range(MAXSEL):
        for s in range(0, CAP, 8):
            rows = [cells[n * CAP + t : n * CAP + t + 1] for t in range(s, s + 8)]
            lhs = jnp.concatenate([jnp.where(sub == n, row, 0.0) for row in rows], axis=1).astype(BF16)
            rhs = jnp.concatenate([picked_ref[n, t] for t in range(s, s + 8)], axis=1)
            total = total + lax.dot_general(
                lhs, rhs, (((1,), (1,)), ((), ())), preferred_element_type=F32
            )
    return total


def predict_kernel(gathered_ref, picked_ref, hot_ref, out_ref):
    blocks = jnp.concatenate([gathered_ref[at(p, GATHER), 0:OWN, :] for p in range(N_RAY)], axis=0)
    total = forward(hot_ref, blocks, picked_ref)
    for m in range(N_MP):
        out_ref[m] = total


def dual_update(predicted, rays_ref, times_ref, pick_ref, new_rays_ref):
    rays = jnp.zeros((MAXSEL, TILE), F32)
    times = jnp.zeros((MAXSEL, TILE), F32)
    taken = jnp.zeros((MAXSEL, TILE), F32)
    for r in range(RB_DEV):
        pick = pick_ref[r]
        rays = rays + pick * rays_ref[r : r + 1, :]
        times = times + pick * times_ref[r : r + 1, :]
        taken = taken + pick
    fresh = (rays + dual_step * (predicted - times)) / (1.0 + dual_step)
    change = taken * (fresh - rays)
    for r in range(RB_DEV):
        new_rays_ref[r : r + 1, :] = rays_ref[r : r + 1, :] + jnp.sum(
            pick_ref[r] * change, axis=0, keepdims=True
        )
    return change


def products(change, picked_ref, n):
    sub = lax.broadcasted_iota(jnp.int32, (CAP, TILE), 0)
    row = change[n : n + 1]
    total = jnp.zeros((CAP, TILE), F32)
    for s in range(0, CAP, 8):
        lhs = jnp.concatenate(
            [jnp.where(sub == t, row, 0.0) for t in range(s, s + 8)], axis=1
        ).astype(BF16)
        rhs = picked_ref[n, s : s + 8].reshape(8 * TILE, TILE)
        total = total + jnp.dot(lhs, rhs, preferred_element_type=F32)
    return total


def share_kernel(
    parts_ref, rays_ref, times_ref, pick_ref, picked_ref, rest_ref, extra_ref, numbers_ref,
    new_rays_ref, out_ref,
):
    predicted = parts_ref[0]
    for m in range(1, N_MP):
        predicted = predicted + parts_ref[m]
    change = dual_update(predicted, rays_ref, times_ref, pick_ref, new_rays_ref)
    for n in range(0, MAXSEL, 2):
        pair = jnp.concatenate(
            [products(change, picked_ref, n), products(change, picked_ref, n + 1)], axis=0
        ).astype(BF16)
        for p in range(N_RAY):
            out_ref[p, n * CAP : (n + 2) * CAP, :] = pair
    extra = extra_ref[...] + numbers_ref[...]
    rest = jnp.concatenate([rest_ref[...].reshape(OWN, TILE), extra], axis=0).astype(BF16)
    for p in range(N_RAY):
        out_ref[p, PRODUCTS:SHARED, :] = rest


def image_kernel(
    shared_ref, gathered_ref, picked_ref, hot_ref, first_ref, base_ref, image_ref, tv_ref,
    field_ref, new_image_ref, edge_ref, out_ref, table_ref,
):
    lane = lax.broadcasted_iota(jnp.int32, (1, TILE), 1)
    singles = []
    for p in range(N_RAY):
        rows = shared_ref[at(p, SHARE), PRODUCTS:SHARED, :].astype(F32)[OWN:]
        singles.append(rows[4:5] * OWN + rows[5:6])
    pairs = [jnp.where(lane < PRODUCTS, singles[p], singles[p + 1]) for p in range(0, N_RAY, 2)]
    group = 4
    chunk = group * OWN
    numbers = []
    terms = []
    for g in range(0, N_RAY, group):
        numbers.append(jnp.concatenate(pairs[g // 2 : g // 2 + 2], axis=1).astype(jnp.int32))
        terms.append(
            jnp.concatenate(
                [shared_ref[at(p, SHARE), 0:PRODUCTS, :] for p in range(g, g + group)], axis=0
            )
        )
    place = lax.broadcasted_iota(jnp.int32, (chunk, group * PRODUCTS), 0)
    sub = lax.broadcasted_iota(jnp.int32, (GY, TILE), 0)
    blocks = []
    for g in range(0, N_RAY, group):
        back = jnp.zeros((chunk, TILE), F32)
        for k in range(N_RAY // group):
            hot = jnp.where(place + g * OWN == numbers[k], 1.0, 0.0).astype(BF16)
            back = back + jnp.dot(hot, terms[k], preferred_element_type=F32)
        table_ref[g * OWN : g * OWN + chunk, :] = back
        for p in range(g, g + group):
            rows = slice(p * OWN, (p + 1) * OWN)
            rest = shared_ref[at(p, SHARE), PRODUCTS:EXTRA, :].astype(F32)
            field = gathered_ref[at(p, GATHER), 0:OWN, :].astype(F32) + (rest - gain * table_ref[rows, :])
            if p > 0:
                change = shared_ref[at(p - 1, SHARE), PRODUCTS:SHARED, :].astype(F32)[OWN:]
                field = field - (2.0 * primal_step) * jnp.concatenate(
                    [jnp.where(sub == 0, change[x : x + 1], 0.0) for x in range(GX)], axis=0
                )
            blocks.append(field)
    total = forward(
        hot_ref, jnp.concatenate([field.astype(BF16) for field in blocks], axis=0), picked_ref
    )
    me, mp = lax.axis_index("ray"), lax.axis_index("mp")
    back = table_ref[pl.ds(pl.multiple_of(me * OWN, OWN), OWN), :]
    for p in range(N_RAY):
        table_ref[p * OWN : (p + 1) * OWN, :] = blocks[p]
    before = jnp.maximum(me - 1, 0)
    for side, peer, row in ((0, before, GY - 1), (1, jnp.minimum(me + 1, N_RAY - 1), 0)):
        field = table_ref[pl.ds(pl.multiple_of(peer * OWN, OWN), OWN), :]
        for x in range(GX):
            edge_ref[side * GX + x : side * GX + x + 1, :] = field[x * GY + row : x * GY + row + 1]
    extra = shared_ref[at(before, SHARE), PRODUCTS:SHARED, :].astype(F32)[OWN:]
    first_y = (sub == 0) & (me > 0)
    edge_ref[2 * GX :] = jnp.zeros((2 * GX, TILE), F32)
    field = []
    for x in range(GX):
        own = back[x * GY : (x + 1) * GY]
        from_y = jnp.where(first_y, extra[x : x + 1], 0.0)
        field.append(base_ref[x] - (gain * own + (2.0 * primal_step) * from_y))
        field_ref[x] = field[x]
        edge_ref[2 * GX + x : 2 * GX + x + 1] = field[x][GY - 1 : GY]
        new_image_ref[x] = image_ref[x] + own + (tv_ref[x] + from_y)
    high = total.astype(BF16).astype(F32)
    ends = [
        jnp.concatenate([high, total - high, field[x] - first_ref[x]], axis=0) for x in (0, GX - 1)
    ]
    for j in range(N_MP):
        out_ref[j] = jnp.where((SUM_2 + j) % N_MP == mp + 1, ends[1], ends[0]).astype(BF16)


def back_kernel(
    parts_ref, rays_ref, times_ref, pick_ref, picked_ref, hot_ref, far_ref, near_ref, dual_ref, edge_ref,
    new_rays_ref, out_ref, planes_ref,
):
    mp = lax.axis_index("mp")
    before, behind = x_halos(far_ref, near_ref)
    step = parts_ref[(mp + (N_MP - 1 - SUM_2)) & (N_MP - 1)].astype(F32)
    before = before[0:GY] + step[2 * MAXSEL :]
    step = parts_ref[(mp + (N_MP + 1 - SUM_2)) & (N_MP - 1)].astype(F32)
    behind = behind[0:GY] + step[2 * MAXSEL :]
    planes_ref[0] = before
    planes_ref[1] = behind
    sub = lax.broadcasted_iota(jnp.int32, (2 * GX, TILE), 0)

    own = [edge_ref[2 * GX + x : 2 * GX + x + 1] for x in range(GX)]
    last_ray = lax.axis_index("ray") == N_RAY - 1
    _, change = tv_cells(
        jnp.concatenate(own * 2, axis=0),
        jnp.concatenate((own[1:] + [behind[GY - 1 : GY]]) * 2, axis=0),
        jnp.concatenate([edge_ref[GX : 2 * GX]] * 2, axis=0),
        [
            jnp.concatenate([dual_ref[c, x][GY - 1 : GY] for x in range(GX)] * 2, axis=0)
            for c in range(3)
        ],
        ((sub & (GX - 1)) == GX - 1) & (mp == N_MP - 1), (sub >= 0) & last_ray,
    )
    high = before[0:1].astype(BF16).astype(F32)
    tail = jnp.where(last_ray, 0.0, change[1])
    tail = jnp.where(sub == 0, high, jnp.where(sub == 1, before[0:1] - high, tail))
    halves = parts_ref[0].astype(F32)
    for m in range(1, N_MP):
        halves = halves + parts_ref[m].astype(F32)
    predicted = halves[0:MAXSEL] + halves[MAXSEL : 2 * MAXSEL]
    change = dual_update(predicted, rays_ref, times_ref, pick_ref, new_rays_ref)
    terms = jnp.concatenate([products(change, picked_ref, n) for n in range(MAXSEL)], axis=0)
    high = terms.astype(BF16)
    low = (terms - high.astype(F32)).astype(BF16)
    turned = (((0,), (0,)), ((), ()))
    image = lax.dot_general(hot_ref[...], high, turned, preferred_element_type=F32)
    image = image + lax.dot_general(hot_ref[...], low, turned, preferred_element_type=F32)
    for p in range(N_RAY):
        out_ref[at(p, LAST)] = jnp.concatenate(
            [image[p * OWN : (p + 1) * OWN], tail], axis=0
        ).astype(BF16)


def swap(block, first):
    route = [(m, m + 1) for m in range(first, N_MP - 1, 2)]
    return lax.ppermute(block, "mp", route + [(b, a) for a, b in route])


def swap_far(block):
    return swap(block, 1)


def swap_near(block):
    return swap(block, 0)


def next_rows(gathered_ref):
    peer = jnp.minimum(lax.axis_index("ray") + 1, N_RAY - 1)
    rows = gathered_ref[at(peer, GATHER)].astype(F32)
    return [
        rows[x * GY : x * GY + 1] + rows[OWN + x : OWN + x + 1] for x in range(GX)
    ]


def first_edges_kernel(field_ref, dual_ref, gathered_ref, after_any, far_ref, near_ref):
    odd = (lax.axis_index("mp") & 1) == 1
    first = field_ref[0]
    last = field_ref[GX - 1]
    far_ref[0:GY] = jnp.where(odd, last, first)
    near_ref[0:GY] = jnp.where(odd, first, last)
    corner = jnp.broadcast_to(next_rows(gathered_ref)[GX - 1], (GY, TILE))
    far_ref[GY : 2 * GY] = corner
    near_ref[GY : 2 * GY] = corner
    for c in range(3):
        rows = slice((c + 2) * GY, (c + 3) * GY)
        far_ref[rows] = dual_ref[c, GX - 1]
        near_ref[rows] = dual_ref[c, GX - 1]


def x_halos(far_ref, near_ref):
    odd = (lax.axis_index("mp") & 1) == 1
    far, near = far_ref[...], near_ref[...]
    return jnp.where(odd, near, far), jnp.where(odd, far, near)


def tv_cells(here, ahead_x, ahead_y, dual, no_x, no_y):
    lane = lax.broadcasted_iota(jnp.int32, here.shape, len(here.shape) - 1)
    ahead_z = pltpu.roll(here, TILE - 1, len(here.shape) - 1)
    steps = (
        jnp.where(no_x, 0.0, ahead_x - here),
        jnp.where(no_y, 0.0, ahead_y - here),
        jnp.where(lane == TILE - 1, 0.0, ahead_z - here),
    )
    moved = [d + tv_step * g for d, g in zip(dual, steps)]
    length = jnp.sqrt(moved[0] * moved[0] + moved[1] * moved[1] + moved[2] * moved[2])
    scale = jnp.maximum(1.0, length / tv_weight)
    fresh = [m / scale for m in moved]
    return fresh, [a - b for a, b in zip(fresh, dual)]


def up_one(plane, row):
    sub = lax.broadcasted_iota(jnp.int32, plane.shape, 0)
    return jnp.where(sub == GY - 1, row, pltpu.roll(plane, GY - 1, 0))


def plane_before(before, before_next, dual, first):
    sub = lax.broadcasted_iota(jnp.int32, (GY, TILE), 0)
    last_y = (sub == GY - 1) & (lax.axis_index("ray") == N_RAY - 1)
    fresh, change = tv_cells(before, first, up_one(before, before_next), dual, sub < 0, last_y)
    return fresh, jnp.where(lax.axis_index("mp") == 0, 0.0, change[0])


def tv_step_all(field, dual, behind, nexts, from_x):
    mp, ray = lax.axis_index("mp"), lax.axis_index("ray")
    sub = lax.broadcasted_iota(jnp.int32, (GY, TILE), 0)
    lane = lax.broadcasted_iota(jnp.int32, (GY, TILE), 1)
    end_x = (mp == N_MP - 1) & (sub >= 0)
    last_y = (sub == GY - 1) & (ray == N_RAY - 1)
    never = sub < 0
    fresh, backs, second = [], [], []
    for x in range(GX):
        ahead = field[x + 1] if x + 1 < GX else behind
        no_x = end_x if x + 1 == GX else never
        new, change = tv_cells(
            field[x], ahead, up_one(field[x], nexts[x]), [d[x] for d in dual], no_x, last_y
        )
        comp_x = jnp.where(no_x, 0.0, change[0])
        comp_y = jnp.where(last_y, 0.0, change[1])
        comp_z = jnp.where(lane == TILE - 1, 0.0, change[2])
        back = from_x - comp_x
        back = back + (jnp.where(sub == 0, 0.0, pltpu.roll(comp_y, 1, 0)) - comp_y)
        back = back + (jnp.where(lane == 0, 0.0, pltpu.roll(comp_z, 1, 1)) - comp_z)
        from_x = comp_x
        fresh.append(new)
        backs.append(back)
        second.append(comp_y)
    return fresh, backs, second


def first_tv_kernel(
    field_ref, dual_ref, far_ref, near_ref, gathered_ref, image_ref,
    new_dual_ref, plane_ref, back_ref, base_ref, rest_ref, extra_ref,
):
    before, behind = x_halos(far_ref, near_ref)
    field = [field_ref[x] for x in range(GX)]
    halo, from_x = plane_before(
        before[0:GY], before[GY : GY + 1],
        [before[(c + 2) * GY : (c + 3) * GY] for c in range(3)], field[0],
    )
    fresh, backs, second = tv_step_all(
        field,
        [[dual_ref[c, x] for x in range(GX)] for c in range(3)],
        behind[0:GY], next_rows(gathered_ref), from_x,
    )
    extra_ref[...] = jnp.zeros_like(extra_ref)
    for x in range(GX):
        base = field[x] - primal_step * (image_ref[x] + 2.0 * backs[x])
        back_ref[x] = backs[x]
        base_ref[x] = base
        rest_ref[x] = base - field[x].astype(BF16).astype(F32)
        extra_ref[x : x + 1] = second[x][GY - 1 : GY]
        for c in range(3):
            new_dual_ref[c, x] = fresh[x][c]
    for c in range(3):
        plane_ref[c] = halo[c]


def second_tv_kernel(field_ref, dual_ref, planes_ref, edge_ref, new_dual_ref, back_ref):
    edge = edge_ref[...]
    fresh, backs, _ = tv_step_all(
        [field_ref[x] for x in range(GX)],
        [[dual_ref[c, x] for x in range(GX)] for c in range(3)],
        planes_ref[1], [edge[GX + x : GX + x + 1] for x in range(GX)], 0.0,
    )
    for x in range(GX):
        back_ref[x] = backs[x]
        for c in range(3):
            new_dual_ref[c, x] = fresh[x][c]


def last_kernel(
    shared_ref, field_ref, planes_ref, dual_plane_ref, image_ref, tv_ref, out_ref, bar_ref
):
    ray = lax.axis_index("ray")
    above = shared_ref[at(jnp.minimum(ray + 1, N_RAY - 1), LAST)].astype(F32)[OWN:]
    below = shared_ref[at(jnp.maximum(ray - 1, 0), LAST)].astype(F32)[OWN:]
    _, from_x = plane_before(
        planes_ref[0], above[0:1] + above[1:2], [dual_plane_ref[c] for c in range(3)], field_ref[0]
    )
    sub = lax.broadcasted_iota(jnp.int32, (GY, TILE), 0)
    first_y = (sub == 0) & (ray > 0)
    back = shared_ref[0].astype(F32)
    for p in range(1, N_RAY):
        back = back + shared_ref[p].astype(F32)
    for x in range(GX):
        tv_back = tv_ref[x] + jnp.where(first_y, below[GX + x : GX + x + 1], 0.0)
        if x == 0:
            tv_back = tv_back + from_x
        own = back[x * GY : (x + 1) * GY]
        image = image_ref[x] + own + tv_back
        out_ref[x] = image
        bar_ref[x] = image + extrapolation * own + tv_back


def on_device(
    slowness, accumulated, extrapolated, tv_dual, ray_dual, traveltimes, tiles, pattern, selected
):
    pattern = pattern.T
    busy = 8 * 2**20
    grid = (GRID, F32)
    duals = ((3,) + GRID, F32)

    field, sent = call(
        start_kernel, [grid, ((N_RAY, SENT, TILE), BF16)], "hh", (slowness, extrapolated),
        (pltpu.VMEM(GRID, F32), pltpu.VMEM(GRID, F32), pltpu.SemaphoreType.DMA((2,))),
    )
    gathered = exchange(sent, "ray", GATHER)
    picked, hot, pick, numbers = fetch(0, tiles, pattern, selected, field)
    (partial_value,) = call(predict_kernel, [SUMS], "vvv", (gathered, picked, hot))
    parts = exchange(partial_value, "mp", SUM_1)

    far, near = call(
        first_edges_kernel, [((5 * GY, TILE), F32)] * 2, "vvva",
        (field, tv_dual, gathered, partial_value), busy=busy,
    )
    far, near = swap_far(far), swap_near(near)
    dual, dual_plane, tv_back, base, rest, extra = call(
        first_tv_kernel,
        [duals, ((3, GY, TILE), F32), grid, grid, grid, ((8, TILE), F32)],
        "vvvvvv", (field, tv_dual, far, near, gathered, accumulated), busy=busy,
    )
    picked_2, hot_2, pick_2, _ = fetch(1, tiles, pattern, selected, partial_value)

    rays, share = call(
        share_kernel, [RAYS, ((N_RAY, SHARED, TILE), BF16)], "vvvvvvvv",
        (parts, ray_dual, traveltimes, pick, picked, rest, extra, numbers),
    )
    shared = exchange(share, "ray", SHARE)
    field, image, edge, partial_value = call(
        image_kernel,
        [grid, grid, ((4 * GX, TILE), F32), ((N_MP, 2 * MAXSEL + GY, TILE), BF16)], "vvvvvvvv",
        (shared, gathered, picked_2, hot_2, field, base, accumulated, tv_back),
        (pltpu.VMEM((ALL, TILE), F32),),
    )
    parts = exchange(partial_value, "mp", SUM_2)
    rays, share, planes = call(
        back_kernel, [RAYS, ((N_RAY, OWN + 8, TILE), BF16), ((2, GY, TILE), F32)], "vvvvvvvvvv",
        (parts, rays, traveltimes, pick_2, picked_2, hot_2, far, near, dual, edge),
    )
    shared = exchange(share, "ray", LAST)
    dual, tv_back = call(
        second_tv_kernel, [duals, grid], "vvvv", (field, dual, planes, edge), busy=busy
    )
    image, image_bar = call(
        last_kernel, [grid, grid], "vvvvvv",
        (shared, field, planes, dual_plane, image, tv_back),
    )
    return (field, rays, dual, image, image_bar)


def solution(mesh):
    in_specs = (
        P("mp", "ray", None),
        P("mp", "ray", None),
        P("mp", "ray", None),
        P(None, "mp", "ray", None),
        P("ray", None),
        P("ray", None),
        P("ray", "mp", None, None),
        P("ray", "mp"),
        P(None, "ray"),
    )
    out_specs = (
        P("mp", "ray", None),
        P("ray", None),
        P(None, "mp", "ray", None),
        P("mp", "ray", None),
        P("mp", "ray", None),
    )
    return jax.shard_map(
        on_device, mesh=mesh, in_specs=in_specs, out_specs=out_specs, check_vma=False
    )
```

```python
import jax
import jax.numpy as jnp
from jax import lax
from jax.experimental import pallas as pl
from jax.experimental.pallas import tpu as pltpu
from jax.sharding import PartitionSpec as P

TILE = 128
GX = 4
GY = 8
RB_DEV = 16
CAP = 8
MAXSEL = 8
N_RAY = 16
N_MP = 32
OWN = GX * GY
ALL = N_RAY * OWN
PRODUCTS = MAXSEL * CAP
SENT = OWN + 8
EXTRA = PRODUCTS + OWN
SHARED = EXTRA + 8
GATHER, SUM_1, SHARE, SUM_2, LAST = 9, 19, 9, 19, 10

primal_step = 0.5
dual_step = 0.5
tv_step = 0.25
tv_weight = 0.3
extrapolation = 2.0 * RB_DEV / (MAXSEL + 1)
gain = primal_step * (1.0 + extrapolation)

F32 = jnp.float32
BF16 = jnp.bfloat16
GRID = (GX, GY, TILE)
SUMS = ((N_MP, MAXSEL, TILE), F32)
RAYS = ((RB_DEV, TILE), F32)


def exchange(copies, axis, first):
    size = N_RAY if axis == "ray" else N_MP
    groups = [[(first + i) % size for i in range(size)]]
    return lax.all_to_all(copies, axis, 0, 0, tiled=True, axis_index_groups=groups)


def at(peer, first):
    return (peer + (N_RAY - first)) & (N_RAY - 1)


def call(kernel, outs, places, args, scratch=(), busy=0, keep=False):
    spaces = {"v": pltpu.VMEM, "h": pltpu.HBM, "a": pl.ANY}
    cost = pl.CostEstimate(flops=0, bytes_accessed=busy, transcendentals=0) if busy else None
    args = [
        pltpu.with_memory_space_constraint(arg, pltpu.HBM) if place == "h" else arg
        for arg, place in zip(args, places)
    ]
    return pl.pallas_call(
        kernel,
        out_shape=[
            pltpu.VMEM(shape, dtype) if keep else jax.ShapeDtypeStruct(shape, dtype)
            for shape, dtype in outs
        ],
        in_specs=[pl.BlockSpec(memory_space=spaces[c]) for c in places],
        out_specs=[pl.BlockSpec(memory_space=pltpu.VMEM) for _ in outs],
        scratch_shapes=list(scratch),
        cost_estimate=cost,
        compiler_params=pltpu.CompilerParams(vmem_limit_bytes=20 * 1024 * 1024),
    )(*args)


SCALARS = (
    pltpu.SMEM((CAP, RB_DEV), jnp.int32),
    pltpu.SMEM((2, RB_DEV), jnp.int32),
    pltpu.SMEM((RB_DEV,), jnp.int32),
    pltpu.SemaphoreType.DMA((2,)),
)


def scalar_copies(pattern_hbm, selected_hbm, pattern_ref, selected_ref, sems):
    return [
        pltpu.make_async_copy(pattern_hbm, pattern_ref, sems.at[0]),
        pltpu.make_async_copy(selected_hbm, selected_ref, sems.at[1]),
    ]


def block_number(pattern):
    row = pattern & (GY * N_RAY - 1)
    plane = lax.shift_right_logical(pattern, 7)
    return lax.shift_right_logical(row, 3) * OWN + plane * GY + (row & (GY - 1))


def list_selected(selected_ref, step, list_ref):
    for n in range(MAXSEL):
        list_ref[n] = jnp.int32(0)
    count = jnp.int32(0)
    for r in range(RB_DEV):
        list_ref[count] = jnp.int32(r)
        count = count + selected_ref[step, r]
    return count


def start_kernel(slowness_hbm, bar_hbm, field_ref, sent_ref, slowness_ref, bar_ref, sems):
    copies = [
        pltpu.make_async_copy(slowness_hbm, slowness_ref, sems.at[0]),
        pltpu.make_async_copy(bar_hbm, bar_ref, sems.at[1]),
    ]
    for copy in copies:
        copy.start()
    for copy in copies:
        copy.wait()
    field = slowness_ref[...] - primal_step * bar_ref[...]
    field_ref[...] = field
    field = field.reshape(OWN, TILE)
    rounded = field.astype(BF16).astype(F32)
    low = field - rounded
    sub = lax.broadcasted_iota(jnp.int32, (8, TILE), 0)
    tail = jnp.zeros((8, TILE), F32)
    for x in range(GX):
        tail = jnp.where(sub == x, low[x * GY : x * GY + 1], tail)
    sent = jnp.concatenate([rounded, tail], axis=0).astype(BF16)
    for p in range(N_RAY):
        sent_ref[p] = sent


def fetch_kernel(step):
    def kernel(
        tiles_hbm, pattern_hbm, selected_hbm, after_ref, picked_ref, hot_ref, pick_ref, numbers_ref,
        pattern_ref, selected_ref, list_ref, scalar_sems, sems,
    ):
        scalars = scalar_copies(pattern_hbm, selected_hbm, pattern_ref, selected_ref, scalar_sems)
        for copy in scalars:
            copy.start()
        for copy in scalars:
            copy.wait()
        count = list_selected(selected_ref, step, list_ref)
        copies = [
            pltpu.make_async_copy(tiles_hbm.at[list_ref[n]], picked_ref.at[n], sems.at[n])
            for n in range(MAXSEL)
        ]
        for copy in copies:
            copy.start()
        sub = lax.broadcasted_iota(jnp.int32, (MAXSEL, TILE), 0)
        lane = lax.broadcasted_iota(jnp.int32, (2 * CAP, TILE), 1)
        slot = lax.broadcasted_iota(jnp.int32, (8, TILE), 1) & (PRODUCTS - 1)
        line = jnp.zeros((8, TILE), jnp.int32)
        for n in range(0, MAXSEL, 2):
            halves = []
            for m in (n, n + 1):
                r = list_ref[m]
                numbers = jnp.zeros((CAP, TILE), jnp.int32)
                for s in range(CAP):
                    number = block_number(pattern_ref[s, r])
                    numbers = jnp.where(sub == s, number, numbers)
                    line = jnp.where(slot == m * CAP + s, number, line)
                halves.append(numbers)
            numbers = jnp.concatenate(halves, axis=0)
            for c in range(ALL // TILE):
                hot = jnp.where(numbers == lane + c * TILE, 1.0, 0.0).astype(BF16)
                hot_ref[n * CAP : (n + 2) * CAP, c * TILE : (c + 1) * TILE] = hot
        line = jnp.where(sub == 4, lax.shift_right_logical(line, 5), line & (OWN - 1))
        numbers_ref[...] = jnp.where((sub == 4) | (sub == 5), line.astype(F32), 0.0)
        listed = jnp.full((MAXSEL, TILE), RB_DEV, jnp.int32)
        for n in range(MAXSEL):
            listed = jnp.where((sub == n) & (sub < count), list_ref[n], listed)
        for r in range(RB_DEV):
            pick_ref[r] = jnp.where(listed == r, 1.0, 0.0)
        for copy in copies:
            copy.wait()

    return kernel


def fetch(step, tiles, pattern, selected, after):
    outs = [
        ((MAXSEL, CAP, TILE, TILE), BF16),
        ((PRODUCTS, ALL), BF16),
        ((RB_DEV, MAXSEL, TILE), F32),
        ((8, TILE), F32),
    ]
    scratch = SCALARS + (pltpu.SemaphoreType.DMA((MAXSEL,)),)
    return call(
        fetch_kernel(step), outs, "hhha", (tiles, pattern, selected, after), scratch, 8 * 2**20, True
    )


def forward(hot_ref, blocks, picked_ref):
    cells = jnp.dot(hot_ref[...], blocks, preferred_element_type=F32)
    sub = lax.broadcasted_iota(jnp.int32, (MAXSEL, TILE), 0)
    total = jnp.zeros((MAXSEL, TILE), F32)
    for n in range(MAXSEL):
        for s in range(0, CAP, 8):
            rows = [cells[n * CAP + t : n * CAP + t + 1] for t in range(s, s + 8)]
            lhs = jnp.concatenate([jnp.where(sub == n, row, 0.0) for row in rows], axis=1).astype(BF16)
            rhs = jnp.concatenate([picked_ref[n, t] for t in range(s, s + 8)], axis=1)
            total = total + lax.dot_general(
                lhs, rhs, (((1,), (1,)), ((), ())), preferred_element_type=F32
            )
    return total


def predict_kernel(gathered_ref, picked_ref, hot_ref, out_ref):
    blocks = jnp.concatenate([gathered_ref[at(p, GATHER), 0:OWN, :] for p in range(N_RAY)], axis=0)
    total = forward(hot_ref, blocks, picked_ref)
    for m in range(N_MP):
        out_ref[m] = total


def added(terms):
    while len(terms) > 1:
        terms = [a + b for a, b in zip(terms[::2], terms[1::2])]
    return terms[0]


def dual_update(predicted, rays_ref, times_ref, pick_ref, new_rays_ref):
    rays = jnp.zeros((MAXSEL, TILE), F32)
    times = jnp.zeros((MAXSEL, TILE), F32)
    taken = jnp.zeros((MAXSEL, TILE), F32)
    for r in range(RB_DEV):
        pick = pick_ref[r]
        rays = rays + pick * rays_ref[r : r + 1, :]
        times = times + pick * times_ref[r : r + 1, :]
        taken = taken + pick
    fresh = (rays + dual_step * (predicted - times)) / (1.0 + dual_step)
    change = taken * (fresh - rays)
    for r in range(RB_DEV):
        new_rays_ref[r : r + 1, :] = rays_ref[r : r + 1, :] + jnp.sum(
            pick_ref[r] * change, axis=0, keepdims=True
        )
    return change


def products(change, picked_ref, n):
    sub = lax.broadcasted_iota(jnp.int32, (CAP, TILE), 0)
    row = change[n : n + 1]
    total = jnp.zeros((CAP, TILE), F32)
    for s in range(0, CAP, 8):
        lhs = jnp.concatenate(
            [jnp.where(sub == t, row, 0.0) for t in range(s, s + 8)], axis=1
        ).astype(BF16)
        rhs = picked_ref[n, s : s + 8].reshape(8 * TILE, TILE)
        total = total + jnp.dot(lhs, rhs, preferred_element_type=F32)
    return total


def share_kernel(
    parts_ref, rays_ref, times_ref, pick_ref, picked_ref, rest_ref, extra_ref, numbers_ref,
    new_rays_ref, out_ref,
):
    predicted = added([parts_ref[m] for m in range(N_MP)])
    change = dual_update(predicted, rays_ref, times_ref, pick_ref, new_rays_ref)
    for n in range(0, MAXSEL, 2):
        pair = jnp.concatenate(
            [products(change, picked_ref, n), products(change, picked_ref, n + 1)], axis=0
        ).astype(BF16)
        for p in range(N_RAY):
            out_ref[p, n * CAP : (n + 2) * CAP, :] = pair
    extra = extra_ref[...] + numbers_ref[...]
    rest = jnp.concatenate([rest_ref[...].reshape(OWN, TILE), extra], axis=0).astype(BF16)
    for p in range(N_RAY):
        out_ref[p, PRODUCTS:SHARED, :] = rest


def image_kernel(
    shared_ref, gathered_ref, picked_ref, hot_ref, first_ref, base_ref, image_ref, tv_ref,
    field_ref, new_image_ref, edge_ref, out_ref, table_ref,
):
    lane = lax.broadcasted_iota(jnp.int32, (1, TILE), 1)
    singles = []
    for p in range(N_RAY):
        rows = shared_ref[at(p, SHARE), PRODUCTS:SHARED, :].astype(F32)[OWN:]
        singles.append(rows[4:5] * OWN + rows[5:6])
    pairs = [jnp.where(lane < PRODUCTS, singles[p], singles[p + 1]) for p in range(0, N_RAY, 2)]
    group = 4
    chunk = group * OWN
    numbers = []
    terms = []
    for g in range(0, N_RAY, group):
        numbers.append(jnp.concatenate(pairs[g // 2 : g // 2 + 2], axis=1).astype(jnp.int32))
        terms.append(
            jnp.concatenate(
                [shared_ref[at(p, SHARE), 0:PRODUCTS, :] for p in range(g, g + group)], axis=0
            )
        )
    place = lax.broadcasted_iota(jnp.int32, (chunk, group * PRODUCTS), 0)
    sub = lax.broadcasted_iota(jnp.int32, (GY, TILE), 0)
    blocks = []
    for g in range(0, N_RAY, group):
        back = jnp.zeros((chunk, TILE), F32)
        for k in range(N_RAY // group):
            hot = jnp.where(place + g * OWN == numbers[k], 1.0, 0.0).astype(BF16)
            back = back + jnp.dot(hot, terms[k], preferred_element_type=F32)
        table_ref[g * OWN : g * OWN + chunk, :] = back
        for p in range(g, g + group):
            rows = slice(p * OWN, (p + 1) * OWN)
            rest = shared_ref[at(p, SHARE), PRODUCTS:EXTRA, :].astype(F32)
            field = gathered_ref[at(p, GATHER), 0:OWN, :].astype(F32) + (rest - gain * table_ref[rows, :])
            if p > 0:
                change = shared_ref[at(p - 1, SHARE), PRODUCTS:SHARED, :].astype(F32)[OWN:]
                field = field - (2.0 * primal_step) * jnp.concatenate(
                    [jnp.where(sub == 0, change[x : x + 1], 0.0) for x in range(GX)], axis=0
                )
            blocks.append(field)
    total = forward(
        hot_ref, jnp.concatenate([field.astype(BF16) for field in blocks], axis=0), picked_ref
    )
    me, mp = lax.axis_index("ray"), lax.axis_index("mp")
    back = table_ref[pl.ds(pl.multiple_of(me * OWN, OWN), OWN), :]
    for p in range(N_RAY):
        table_ref[p * OWN : (p + 1) * OWN, :] = blocks[p]
    before = jnp.maximum(me - 1, 0)
    for side, peer, row in ((0, before, GY - 1), (1, jnp.minimum(me + 1, N_RAY - 1), 0)):
        field = table_ref[pl.ds(pl.multiple_of(peer * OWN, OWN), OWN), :]
        for x in range(GX):
            edge_ref[side * GX + x : side * GX + x + 1, :] = field[x * GY + row : x * GY + row + 1]
    extra = shared_ref[at(before, SHARE), PRODUCTS:SHARED, :].astype(F32)[OWN:]
    first_y = (sub == 0) & (me > 0)
    edge_ref[2 * GX :] = jnp.zeros((2 * GX, TILE), F32)
    field = []
    for x in range(GX):
        own = back[x * GY : (x + 1) * GY]
        from_y = jnp.where(first_y, extra[x : x + 1], 0.0)
        field.append(base_ref[x] - (gain * own + (2.0 * primal_step) * from_y))
        field_ref[x] = field[x]
        edge_ref[2 * GX + x : 2 * GX + x + 1] = field[x][GY - 1 : GY]
        new_image_ref[x] = image_ref[x] + own + (tv_ref[x] + from_y)
    high = total.astype(BF16).astype(F32)
    ends = [
        jnp.concatenate([high, total - high, field[x] - first_ref[x]], axis=0) for x in (0, GX - 1)
    ]
    for j in range(N_MP):
        out_ref[j] = jnp.where((SUM_2 + j) % N_MP == mp + 1, ends[1], ends[0]).astype(BF16)


def back_kernel(
    parts_ref, rays_ref, times_ref, pick_ref, picked_ref, hot_ref, far_ref, near_ref, dual_ref, edge_ref,
    new_rays_ref, out_ref, planes_ref,
):
    mp = lax.axis_index("mp")
    before, behind = x_halos(far_ref, near_ref)
    step = parts_ref[(mp + (N_MP - 1 - SUM_2)) & (N_MP - 1)].astype(F32)
    before = before[0:GY] + step[2 * MAXSEL :]
    step = parts_ref[(mp + (N_MP + 1 - SUM_2)) & (N_MP - 1)].astype(F32)
    behind = behind[0:GY] + step[2 * MAXSEL :]
    planes_ref[0] = before
    planes_ref[1] = behind
    sub = lax.broadcasted_iota(jnp.int32, (2 * GX, TILE), 0)

    own = [edge_ref[2 * GX + x : 2 * GX + x + 1] for x in range(GX)]
    last_ray = lax.axis_index("ray") == N_RAY - 1
    _, change = tv_cells(
        jnp.concatenate(own * 2, axis=0),
        jnp.concatenate((own[1:] + [behind[GY - 1 : GY]]) * 2, axis=0),
        jnp.concatenate([edge_ref[GX : 2 * GX]] * 2, axis=0),
        [
            jnp.concatenate([dual_ref[c, x][GY - 1 : GY] for x in range(GX)] * 2, axis=0)
            for c in range(3)
        ],
        ((sub & (GX - 1)) == GX - 1) & (mp == N_MP - 1), (sub >= 0) & last_ray,
    )
    high = before[0:1].astype(BF16).astype(F32)
    tail = jnp.where(last_ray, 0.0, change[1])
    tail = jnp.where(sub == 0, high, jnp.where(sub == 1, before[0:1] - high, tail))
    halves = added([parts_ref[m].astype(F32) for m in range(N_MP)])
    predicted = halves[0:MAXSEL] + halves[MAXSEL : 2 * MAXSEL]
    change = dual_update(predicted, rays_ref, times_ref, pick_ref, new_rays_ref)
    terms = jnp.concatenate([products(change, picked_ref, n) for n in range(MAXSEL)], axis=0)
    high = terms.astype(BF16)
    low = (terms - high.astype(F32)).astype(BF16)
    turned = (((0,), (0,)), ((), ()))
    image = lax.dot_general(hot_ref[...], high, turned, preferred_element_type=F32)
    image = image + lax.dot_general(hot_ref[...], low, turned, preferred_element_type=F32)
    for p in range(N_RAY):
        out_ref[at(p, LAST)] = jnp.concatenate(
            [image[p * OWN : (p + 1) * OWN], tail], axis=0
        ).astype(BF16)


def swap(block, first):
    route = [(m, m + 1) for m in range(first, N_MP - 1, 2)]
    return lax.ppermute(block, "mp", route + [(b, a) for a, b in route])


def swap_far(block):
    return swap(block, 1)


def swap_near(block):
    return swap(block, 0)


def next_rows(gathered_ref):
    peer = jnp.minimum(lax.axis_index("ray") + 1, N_RAY - 1)
    rows = gathered_ref[at(peer, GATHER)].astype(F32)
    return [
        rows[x * GY : x * GY + 1] + rows[OWN + x : OWN + x + 1] for x in range(GX)
    ]


def first_edges_kernel(field_ref, dual_ref, gathered_ref, after_any, far_ref, near_ref):
    odd = (lax.axis_index("mp") & 1) == 1
    first = field_ref[0]
    last = field_ref[GX - 1]
    far_ref[0:GY] = jnp.where(odd, last, first)
    near_ref[0:GY] = jnp.where(odd, first, last)
    corner = jnp.broadcast_to(next_rows(gathered_ref)[GX - 1], (GY, TILE))
    far_ref[GY : 2 * GY] = corner
    near_ref[GY : 2 * GY] = corner
    for c in range(3):
        rows = slice((c + 2) * GY, (c + 3) * GY)
        far_ref[rows] = dual_ref[c, GX - 1]
        near_ref[rows] = dual_ref[c, GX - 1]


def x_halos(far_ref, near_ref):
    odd = (lax.axis_index("mp") & 1) == 1
    far, near = far_ref[...], near_ref[...]
    return jnp.where(odd, near, far), jnp.where(odd, far, near)


def tv_cells(here, ahead_x, ahead_y, dual, no_x, no_y):
    lane = lax.broadcasted_iota(jnp.int32, here.shape, len(here.shape) - 1)
    ahead_z = pltpu.roll(here, TILE - 1, len(here.shape) - 1)
    steps = (
        jnp.where(no_x, 0.0, ahead_x - here),
        jnp.where(no_y, 0.0, ahead_y - here),
        jnp.where(lane == TILE - 1, 0.0, ahead_z - here),
    )
    moved = [d + tv_step * g for d, g in zip(dual, steps)]
    length = jnp.sqrt(moved[0] * moved[0] + moved[1] * moved[1] + moved[2] * moved[2])
    scale = jnp.maximum(1.0, length / tv_weight)
    fresh = [m / scale for m in moved]
    return fresh, [a - b for a, b in zip(fresh, dual)]


def up_one(plane, row):
    sub = lax.broadcasted_iota(jnp.int32, plane.shape, 0)
    return jnp.where(sub == GY - 1, row, pltpu.roll(plane, GY - 1, 0))


def plane_before(before, before_next, dual, first):
    sub = lax.broadcasted_iota(jnp.int32, (GY, TILE), 0)
    last_y = (sub == GY - 1) & (lax.axis_index("ray") == N_RAY - 1)
    fresh, change = tv_cells(before, first, up_one(before, before_next), dual, sub < 0, last_y)
    return fresh, jnp.where(lax.axis_index("mp") == 0, 0.0, change[0])


def tv_step_all(field, dual, behind, nexts, from_x):
    mp, ray = lax.axis_index("mp"), lax.axis_index("ray")
    sub = lax.broadcasted_iota(jnp.int32, (GY, TILE), 0)
    lane = lax.broadcasted_iota(jnp.int32, (GY, TILE), 1)
    end_x = (mp == N_MP - 1) & (sub >= 0)
    last_y = (sub == GY - 1) & (ray == N_RAY - 1)
    never = sub < 0
    fresh, backs, second = [], [], []
    for x in range(GX):
        ahead = field[x + 1] if x + 1 < GX else behind
        no_x = end_x if x + 1 == GX else never
        new, change = tv_cells(
            field[x], ahead, up_one(field[x], nexts[x]), [d[x] for d in dual], no_x, last_y
        )
        comp_x = jnp.where(no_x, 0.0, change[0])
        comp_y = jnp.where(last_y, 0.0, change[1])
        comp_z = jnp.where(lane == TILE - 1, 0.0, change[2])
        back = from_x - comp_x
        back = back + (jnp.where(sub == 0, 0.0, pltpu.roll(comp_y, 1, 0)) - comp_y)
        back = back + (jnp.where(lane == 0, 0.0, pltpu.roll(comp_z, 1, 1)) - comp_z)
        from_x = comp_x
        fresh.append(new)
        backs.append(back)
        second.append(comp_y)
    return fresh, backs, second


def first_tv_kernel(
    field_ref, dual_ref, far_ref, near_ref, gathered_ref, image_ref,
    new_dual_ref, plane_ref, back_ref, base_ref, rest_ref, extra_ref,
):
    before, behind = x_halos(far_ref, near_ref)
    field = [field_ref[x] for x in range(GX)]
    halo, from_x = plane_before(
        before[0:GY], before[GY : GY + 1],
        [before[(c + 2) * GY : (c + 3) * GY] for c in range(3)], field[0],
    )
    fresh, backs, second = tv_step_all(
        field,
        [[dual_ref[c, x] for x in range(GX)] for c in range(3)],
        behind[0:GY], next_rows(gathered_ref), from_x,
    )
    extra_ref[...] = jnp.zeros_like(extra_ref)
    for x in range(GX):
        base = field[x] - primal_step * (image_ref[x] + 2.0 * backs[x])
        back_ref[x] = backs[x]
        base_ref[x] = base
        rest_ref[x] = base - field[x].astype(BF16).astype(F32)
        extra_ref[x : x + 1] = second[x][GY - 1 : GY]
        for c in range(3):
            new_dual_ref[c, x] = fresh[x][c]
    for c in range(3):
        plane_ref[c] = halo[c]


def second_tv_kernel(field_ref, dual_ref, planes_ref, edge_ref, new_dual_ref, back_ref):
    edge = edge_ref[...]
    fresh, backs, _ = tv_step_all(
        [field_ref[x] for x in range(GX)],
        [[dual_ref[c, x] for x in range(GX)] for c in range(3)],
        planes_ref[1], [edge[GX + x : GX + x + 1] for x in range(GX)], 0.0,
    )
    for x in range(GX):
        back_ref[x] = backs[x]
        for c in range(3):
            new_dual_ref[c, x] = fresh[x][c]


def last_kernel(
    shared_ref, field_ref, planes_ref, dual_plane_ref, image_ref, tv_ref, out_ref, bar_ref
):
    ray = lax.axis_index("ray")
    above = shared_ref[at(jnp.minimum(ray + 1, N_RAY - 1), LAST)].astype(F32)[OWN:]
    below = shared_ref[at(jnp.maximum(ray - 1, 0), LAST)].astype(F32)[OWN:]
    _, from_x = plane_before(
        planes_ref[0], above[0:1] + above[1:2], [dual_plane_ref[c] for c in range(3)], field_ref[0]
    )
    sub = lax.broadcasted_iota(jnp.int32, (GY, TILE), 0)
    first_y = (sub == 0) & (ray > 0)
    back = added([shared_ref[p].astype(F32) for p in range(N_RAY)])
    for x in range(GX):
        tv_back = tv_ref[x] + jnp.where(first_y, below[GX + x : GX + x + 1], 0.0)
        if x == 0:
            tv_back = tv_back + from_x
        own = back[x * GY : (x + 1) * GY]
        image = image_ref[x] + own + tv_back
        out_ref[x] = image
        bar_ref[x] = image + extrapolation * own + tv_back


def on_device(
    slowness, accumulated, extrapolated, tv_dual, ray_dual, traveltimes, tiles, pattern, selected
):
    pattern = pattern.T
    busy = 8 * 2**20
    grid = (GRID, F32)
    duals = ((3,) + GRID, F32)

    field, sent = call(
        start_kernel, [grid, ((N_RAY, SENT, TILE), BF16)], "hh", (slowness, extrapolated),
        (pltpu.VMEM(GRID, F32), pltpu.VMEM(GRID, F32), pltpu.SemaphoreType.DMA((2,))),
    )
    gathered = exchange(sent, "ray", GATHER)
    picked, hot, pick, numbers = fetch(0, tiles, pattern, selected, field)
    (partial_value,) = call(predict_kernel, [SUMS], "vvv", (gathered, picked, hot))
    parts = exchange(partial_value, "mp", SUM_1)

    far, near = call(
        first_edges_kernel, [((5 * GY, TILE), F32)] * 2, "vvva",
        (field, tv_dual, gathered, partial_value), busy=busy,
    )
    far, near = swap_far(far), swap_near(near)
    dual, dual_plane, tv_back, base, rest, extra = call(
        first_tv_kernel,
        [duals, ((3, GY, TILE), F32), grid, grid, grid, ((8, TILE), F32)],
        "vvvvvv", (field, tv_dual, far, near, gathered, accumulated), busy=busy,
    )
    picked_2, hot_2, pick_2, _ = fetch(1, tiles, pattern, selected, partial_value)

    rays, share = call(
        share_kernel, [RAYS, ((N_RAY, SHARED, TILE), BF16)], "vvvvvvvv",
        (parts, ray_dual, traveltimes, pick, picked, rest, extra, numbers),
    )
    shared = exchange(share, "ray", SHARE)
    field, image, edge, partial_value = call(
        image_kernel,
        [grid, grid, ((4 * GX, TILE), F32), ((N_MP, 2 * MAXSEL + GY, TILE), BF16)], "vvvvvvvv",
        (shared, gathered, picked_2, hot_2, field, base, accumulated, tv_back),
        (pltpu.VMEM((ALL, TILE), F32),),
    )
    parts = exchange(partial_value, "mp", SUM_2)
    rays, share, planes = call(
        back_kernel, [RAYS, ((N_RAY, OWN + 8, TILE), BF16), ((2, GY, TILE), F32)], "vvvvvvvvvv",
        (parts, rays, traveltimes, pick_2, picked_2, hot_2, far, near, dual, edge),
    )
    shared = exchange(share, "ray", LAST)
    dual, tv_back = call(
        second_tv_kernel, [duals, grid], "vvvv", (field, dual, planes, edge), busy=busy
    )
    image, image_bar = call(
        last_kernel, [grid, grid], "vvvvvv",
        (shared, field, planes, dual_plane, image, tv_back),
    )
    return (field, rays, dual, image, image_bar)


def solution(mesh):
    in_specs = (
        P("mp", "ray", None),
        P("mp", "ray", None),
        P("mp", "ray", None),
        P(None, "mp", "ray", None),
        P("ray", None),
        P("ray", None),
        P("ray", "mp", None, None),
        P("ray", "mp"),
        P(None, "ray"),
    )
    out_specs = (
        P("mp", "ray", None),
        P("ray", None),
        P(None, "mp", "ray", None),
        P("mp", "ray", None),
        P("mp", "ray", None),
    )
    return jax.shard_map(
        on_device, mesh=mesh, in_specs=in_specs, out_specs=out_specs, check_vma=False
    )
```
